32 devices in a mesh: groups: 2 (over y), expert: 8 (over z, x), tensor: 2 (over core).
Axes of the slice: x: 2, y: 2, z: 4, core: 2. Of those that a mesh axis runs over, the one named last changes fastest.
Arguments:
- tokens: bfloat16 [256, 6144], P(('groups', 'expert'), 'tensor'), parts along dimension 0, may hold values from -6 to 6
- grad_out: bfloat16 [256, 6144], P(('groups', 'expert'), 'tensor'), parts along dimension 0, may hold values from -6 to 6
- expert_ids: int32 [256, 4], P(('groups', 'expert')), parts along dimension 0, may hold values from 0 to 15, all different within a row; in each aligned block of 16 rows (0 to 15, 16 to 31, ...) at most 5 rows name the same one
- gate_probs: bfloat16 [256, 4], P(('groups', 'expert')), parts along dimension 0, may hold values from 0.099609375 to 1
- w_gate: bfloat16 [21504, 6144], P(('expert', 'tensor')), may hold values from -0.078125 to 0.078125
- w_up: bfloat16 [21504, 6144], P(('expert', 'tensor')), may hold values from -0.078125 to 0.078125
- w_down: bfloat16 [21504, 6144], P(('expert', 'tensor')), may hold values from -0.0625 to 0.0625
Outputs:
- grad_tokens: bfloat16 [256, 6144], P(('groups', 'expert'), 'tensor'), parts along dimension 0
- grad_gates: float32 [256, 4], P(('groups', 'expert')), parts along dimension 0
- grad_w_gate: bfloat16 [21504, 12288], P(('expert', 'tensor'), 'groups'), parts along dimension 1
- grad_w_up: bfloat16 [21504, 12288], P(('expert', 'tensor'), 'groups'), parts along dimension 1
- grad_w_down: bfloat16 [21504, 12288], P(('expert', 'tensor'), 'groups'), parts along dimension 1
The draws below stay inside these ranges and needn't reach their ends.
There are 2 independent parts, one for each index of `groups`. The reference program is written for one: setup_inputs(seed, part) draws one part's arguments, and reference() takes and returns one part's arrays. A program takes and returns all parts, laid end to end along the dimension named above; an argument that names none is the same for every part. Nothing has to cross between parts.
Inputs may be any that keep to these rules, and one draw needn't show every extreme that they name: `expert_ids`: in each aligned block of 16 rows (the rows of one index of expert) no expert is named by more than 5 rows, a bound that some block reaches.
All inputs are finite; a program needn't handle non-finite values.
Results may differ from the reference program's by a relative error of at most 0.0051.
Values may be sent and summed in bfloat16 or wider, within the bound.
No kernel may reach another device: no remote copies, remote signals or barrier semaphores. Data moves between devices by JAX's collectives and lax.ppermute only.
A program may use at most 192 MiB of HBM per device.

```python
import math
import jax
import jax.numpy as jnp
import numpy as np

D = 6144
FF = 10752
EXPERTS = 16
TOP = 4
EXPERTS_ON = 2
TOK_DEV = 16
CAP = 5
TOKENS = 128
N_EXPERT = 8


def steps_of(key, extent, split, low, largest):
    def one(axis_at, parts):
        heights = jax.random.uniform(jax.random.fold_in(jax.random.fold_in(key, 6), axis_at), (parts,), jnp.float32, low / len(split), largest / len(split))
        return jnp.repeat(jnp.exp(heights), extent[axis_at] // parts).reshape((-1,) + (1,) * (len(extent) - axis_at - 1))

    level = one(*split[0])
    for cut in split[1:]:
        level = level * one(*cut)
    return level


def shared_out(key, own, number, rows, count, top, reach, slope):
    ranking = jax.random.permutation(key, count)
    crowded, ordinary = shares(count, rows * top, reach, slope, True), shares(count, rows * top, reach, slope, False)
    places = jnp.arange(count)

    def named(tallies, offset_by):
        used = int((tallies > 0).sum())
        fixed = max(1, used // 4)
        passed = fixed + (places - fixed + offset_by * (used - fixed)) % max(1, count - fixed)
        return jnp.zeros((count,), jnp.int32).at[ranking[jnp.where(places < fixed, places, passed)]].set(jnp.asarray(tallies, jnp.int32))

    tallies = jnp.where(number % 4 == 0, named(crowded, number // 4), named(ordinary, number - number // 4 - 1))
    mixed = jax.random.permutation(jax.random.fold_in(own, 3), count)
    source_of, sink = mixed[0:count // 2 * 2:2], mixed[1:count // 2 * 2:2]
    room = jnp.minimum(tallies[source_of] - 1, reach - tallies[sink]) // 2
    room = jnp.where((source_of == ranking[0]) | (sink == ranking[0]) | (tallies[sink] == 0), 0, jnp.maximum(room, 0))
    passed = jax.random.randint(jax.random.fold_in(own, 4), (count // 2,), 0, 1 << 20) % (room + 1)
    tallies = tallies.at[source_of].add(-passed).at[sink].add(passed)
    items = jnp.searchsorted(jnp.cumsum(tallies), jnp.arange(rows * top), side="right").astype(jnp.int32)
    table = items.reshape(top, rows).T
    table = table[jax.random.permutation(jax.random.fold_in(own, 1), rows)]
    offset_by = jax.random.randint(jax.random.fold_in(own, 2), (rows, 1), 0, top)
    return jnp.take_along_axis(table, (jnp.arange(top)[None, :] + offset_by) % top, axis=1)


def shares(count, total, most, slope, full):
    loads = [(1 << 20) // math.isqrt(standing ** slope) + 1 for standing in range(1, count + 1)]
    largest = most if full else min(most, max(-(-total // count), total * loads[0] // sum(loads)))
    least = 1 if total - largest >= count - 1 else 0
    counts, surplus = [largest] + [least] * (count - 1), total - largest - least * (count - 1)
    while surplus > 0:
        movable = [i for i in range(1, count) if counts[i] < largest] or [i for i in range(1, count) if counts[i] < most]
        pool, left = sum([loads[i] for i in movable]), surplus
        for i in movable:
            addition = min(most - counts[i], max(1, left * loads[i] // pool), surplus)
            counts[i] = counts[i] + addition
            surplus = surplus - addition
    return np.array(counts)


def scatter_about(key, dims, spread, bound, pieces=(), dtype=jnp.bfloat16):
    drawn = jax.random.normal(key, dims, jnp.float32) * spread
    if len(pieces) > 0:
        drawn = steps_of(key, dims, pieces, -0.22, 0.18) * drawn
    return jnp.clip(drawn, min=-bound, max=bound).astype(dtype)


def setup_inputs(seed: int = 0, part: int = 0) -> dict:
    keys = jax.random.split(jax.random.key(seed), 8)
    own_keys = jax.random.split(jax.random.fold_in(keys[7], part), 8)
    tokens = scatter_about(own_keys[0], (TOKENS, D), 1.0, 6.0, ((0, 8), (1, 2)))
    grad_out = scatter_about(own_keys[1], (TOKENS, D), 1.0, 6.0, ((0, 8), (1, 2)))
    expert_ids_keys = jax.random.split(jax.random.fold_in(own_keys[2], 1), TOKENS // TOK_DEV)
    expert_ids_turns = jax.random.permutation(jax.random.fold_in(own_keys[2], 3), TOKENS // TOK_DEV)
    expert_ids = jax.vmap(lambda own, number: shared_out(jax.random.fold_in(own_keys[2], 2), own, number, TOK_DEV, EXPERTS, TOP, CAP, 2))(expert_ids_keys, expert_ids_turns).reshape((TOKENS, TOP))
    gate_probs = jnp.clip(jnp.exp(math.log(1.0) - 2.306499 * jax.random.uniform(own_keys[3], (TOKENS, TOP), jnp.float32) ** steps_of(own_keys[3], (TOKENS, TOP), ((0, 8),), -0.2, 0.2)), 0.099609375, 1.0).astype(jnp.bfloat16)
    w_gate = scatter_about(keys[4], (EXPERTS_ON * FF, D), D ** -0.5, 0.078125, ((0, 16),))
    w_up = scatter_about(keys[5], (EXPERTS_ON * FF, D), D ** -0.5, 0.078125, ((0, 16),))
    w_down = scatter_about(keys[6], (EXPERTS_ON * FF, D), FF ** -0.5, 0.0625, ((0, 16),))
    return {"tokens": tokens, "grad_out": grad_out, "expert_ids": expert_ids, "gate_probs": gate_probs, "w_gate": w_gate, "w_up": w_up, "w_down": w_down}


def reference(tokens, grad_out, expert_ids, gate_probs, w_gate, w_up, w_down):
    rows_total = N_EXPERT * CAP
    grad_tokens = jnp.zeros(tokens.shape, jnp.float32)
    grad_gates = jnp.zeros(gate_probs.shape, jnp.float32)
    gate_blocks = []
    up_blocks = []
    down_blocks = []
    for expert in range(EXPERTS_ON):
        chosen = expert_ids == expert
        routed = jnp.any(chosen, axis=1)
        weight_of = jnp.sum(jnp.where(chosen, gate_probs.astype(jnp.float32), jnp.float32(0.0)), axis=1)
        order = jnp.argsort(jnp.where(routed, 0, 1).astype(jnp.int32), stable=True)[:rows_total].astype(jnp.int32)
        valid = routed[order]
        inputs = tokens[order]
        grads = grad_out[order]
        factor = jnp.where(valid, weight_of[order], jnp.float32(0.0))[:, None]
        gate_w = w_gate[expert * FF:(expert + 1) * FF, :]
        up_w = w_up[expert * FF:(expert + 1) * FF, :]
        down_w = w_down[expert * FF:(expert + 1) * FF, :]
        hidden = jnp.dot(inputs, gate_w.T, preferred_element_type=jnp.float32)
        upper = jnp.dot(inputs, up_w.T, preferred_element_type=jnp.float32)
        dact = jnp.dot(grads, down_w.T, preferred_element_type=jnp.float32)
        sigma = jax.nn.sigmoid(hidden)
        silu = hidden * sigma
        act = silu * upper
        part = jnp.sum(act * dact, axis=1)
        weighted = (factor * act).astype(jnp.bfloat16)
        scaled = factor * dact
        grad_h = (scaled * upper * sigma * (1.0 + hidden * (1.0 - sigma))).astype(jnp.bfloat16)
        grad_u = (scaled * silu).astype(jnp.bfloat16)
        down_blocks.append(jnp.dot(weighted.T, grads, preferred_element_type=jnp.float32).astype(jnp.bfloat16))
        gate_blocks.append(jnp.dot(grad_h.T, inputs, preferred_element_type=jnp.float32).astype(jnp.bfloat16))
        up_blocks.append(jnp.dot(grad_u.T, inputs, preferred_element_type=jnp.float32).astype(jnp.bfloat16))
        rows_grad = jnp.dot(grad_h, gate_w, preferred_element_type=jnp.float32) + jnp.dot(grad_u, up_w, preferred_element_type=jnp.float32)
        rows_grad = jnp.where(valid[:, None], rows_grad, jnp.float32(0.0))
        grad_tokens = grad_tokens.at[order].add(rows_grad)
        part_full = jnp.zeros((tokens.shape[0],), jnp.float32).at[order].add(jnp.where(valid, part, jnp.float32(0.0)))
        grad_gates = grad_gates + jnp.where(chosen, part_full[:, None], jnp.float32(0.0))
    return (grad_tokens.astype(jnp.bfloat16), grad_gates, jnp.concatenate(gate_blocks, axis=0), jnp.concatenate(up_blocks, axis=0), jnp.concatenate(down_blocks, axis=0))
```

```python
import functools
import math

import jax
import jax.numpy as jnp
from jax import lax
from jax.experimental import pallas as pl
from jax.experimental.pallas import tpu as pltpu
from jax.sharding import PartitionSpec as P

EXPERTS_ON = 2
CAP = 5
HALF = 4
MAIN = EXPERTS_ON * HALF
LANES = 128
F32 = jnp.float32
BF16 = jnp.bfloat16
MIB = 1 << 20


def iota(shape, dim):
    return lax.broadcasted_iota(jnp.int32, shape, dim)


def selection(ids, expert, position):
    rows, toks = expert.shape
    hits = [ids[k : k + 1, :] == expert for k in range(ids.shape[0])]
    member = functools.reduce(jnp.logical_or, hits).astype(F32)
    before = (iota((toks, toks), 0) < iota((toks, toks), 1)).astype(F32)
    earlier = jnp.dot(member, before, preferred_element_type=F32)
    chosen = jnp.where(earlier == position.astype(F32), member, 0.0)
    return chosen, hits


def slots(first, toks):
    row = iota((MAIN, toks), 0)
    group = (row >= HALF).astype(jnp.int32)
    expert = jnp.where(group == 0, first, 1 - first)
    return expert, row - HALF * group, jnp.full((MAIN, toks), CAP - 1, jnp.int32)


def pick_body(first_ref, ids_ref, probs_ref, tok_ref, grad_ref, x_ref, g_ref):
    ids = ids_ref[...]
    probs = probs_ref[...].astype(F32)
    toks, width = tok_ref.shape
    quarter = width // HALF
    expert, place, last = slots(first_ref[0], toks)
    main, hits = selection(ids, expert, place)
    tail, _ = selection(ids, expert, last)
    weight = sum(jnp.where(hit, probs[k : k + 1, :], 0.0) for k, hit in enumerate(hits))
    row = iota((MAIN, toks), 0)
    part = jnp.where(row >= HALF, row - HALF, row)
    for src, dst in ((tok_ref, x_ref), (grad_ref, g_ref)):
        dst[:, :width] = jnp.dot(main.astype(BF16), src[...], preferred_element_type=F32).astype(BF16)
        ext = jnp.zeros((MAIN, quarter), F32)
        for s in range(HALF):
            one = jnp.where(part == s, tail, 0.0).astype(BF16)
            ext += jnp.dot(one, src[:, s * quarter : (s + 1) * quarter], preferred_element_type=F32)
        dst[:, width : width + quarter] = ext.astype(BF16)
    base = width + quarter
    for at, chosen in enumerate((main, tail)):
        gate = jnp.sum(chosen * weight, axis=1, keepdims=True)
        x_ref[:, base + at * LANES : base + (at + 1) * LANES] = jnp.broadcast_to(gate, (MAIN, LANES)).astype(BF16)


def pick(first, ids_t, probs_t, tokens, grad_out):
    width = tokens.shape[1]
    packed = width + width // HALF
    return pl.pallas_call(
        pick_body,
        out_shape=(
            jax.ShapeDtypeStruct((MAIN, packed + 2 * LANES), BF16),
            jax.ShapeDtypeStruct((MAIN, packed), BF16),
        ),
        in_specs=[pl.BlockSpec(memory_space=pltpu.SMEM)] + [pl.BlockSpec(memory_space=pltpu.VMEM)] * 4,
        out_specs=[pl.BlockSpec(memory_space=pltpu.VMEM)] * 2,
        name="pick_rows",
    )(first, ids_t, probs_t, tokens, grad_out)


def unpack_maps(e, rows, copies, tensors):
    n_expert = EXPERTS_ON * copies
    senders = n_expert * tensors * MAIN
    r = iota((rows, senders), 0)
    k = iota((rows, senders), 1)
    whole = copies * MAIN
    is_main = r < whole
    rest = r - whole
    c = jnp.where(is_main, r // MAIN, rest // EXPERTS_ON)
    q = jnp.where(is_main, r % MAIN, 0)
    own = jnp.where(is_main, q // HALF, rest % EXPERTS_ON)
    p = q % HALF
    owner = (e * copies + c + (1 - own) * copies) % n_expert
    base = owner * (tensors * MAIN) + e * HALF
    is_tail = jnp.logical_and(r >= whole, rest < copies * EXPERTS_ON)

    def main(t):
        return jnp.logical_and(is_main, k == base + t * MAIN + p).astype(BF16)

    def tail(t, s):
        return jnp.logical_and(is_tail, k == base + t * MAIN + s).astype(BF16)

    return main, tail


def forward_body(copies, tensors, e_ref, xr_ref, gr_ref, wg_ref, wu_ref, wd_ref,
                 x_ref, g_ref, wt_ref, dh_ref, du_ref, back_ref, factor, acc, gates):
    step = pl.program_id(0)
    rows, depth = x_ref.shape
    width = depth // tensors
    quarter = width // HALF
    base = width + quarter

    @pl.when(step == 0)
    def _():
        main, tail = unpack_maps(e_ref[0], rows, copies, tensors)
        for t in range(tensors):
            whole = main(t)
            for s in range(HALF):
                piece = tail(t, s)
                cols = pl.ds(s * quarter, quarter)
                to = pl.ds(t * width + s * quarter, quarter)
                for src, dst in ((xr_ref, x_ref), (gr_ref, g_ref)):
                    dst[:, to] = (
                        jnp.dot(whole, src[:, cols], preferred_element_type=F32)
                        + jnp.dot(piece, src[:, width:base], preferred_element_type=F32)
                    ).astype(BF16)
        factor[...] = jnp.dot(main(0), xr_ref[:, base : base + LANES], preferred_element_type=F32) + jnp.dot(
            tail(0, 0), xr_ref[:, base + LANES : base + 2 * LANES], preferred_element_type=F32
        )
        acc[...] = jnp.zeros_like(acc)
        gates[...] = jnp.zeros_like(gates)

    nt = (((1,), (1,)), ((), ()))
    x = x_ref[...]
    hidden = lax.dot_general(x, wg_ref[...], nt, preferred_element_type=F32)
    upper = lax.dot_general(x, wu_ref[...], nt, preferred_element_type=F32)
    dact = lax.dot_general(g_ref[...], wd_ref[...], nt, preferred_element_type=F32)
    weight = factor[:, :1]
    sigma = 1.0 / (1.0 + jnp.exp(-hidden))
    silu = hidden * sigma
    act = silu * upper
    gates[...] += jnp.sum(act * dact, axis=1, keepdims=True)
    scaled = weight * dact
    wt_ref[0] = (weight * act).astype(BF16)
    dh = (scaled * upper * sigma * (1.0 + hidden * (1.0 - sigma))).astype(BF16)
    du = (scaled * silu).astype(BF16)
    dh_ref[0] = dh
    du_ref[0] = du
    acc[...] += jnp.dot(dh, wg_ref[...], preferred_element_type=F32) + jnp.dot(
        du, wu_ref[...], preferred_element_type=F32
    )

    @pl.when(step == pl.num_programs(0) - 1)
    def _():
        whole = copies * MAIN
        for c in range(copies):
            for t in range(tensors):
                at = (c * tensors + t) * MAIN
                back_ref[at : at + MAIN, :width] = acc[c * MAIN : (c + 1) * MAIN, t * width : (t + 1) * width]
                back_ref[at : at + MAIN, base : base + LANES] = gates[c * MAIN : (c + 1) * MAIN, :]
                for a in range(EXPERTS_ON):
                    r = whole + c * EXPERTS_ON + a
                    back_ref[at + a * HALF : at + (a + 1) * HALF, base + LANES :] = jnp.broadcast_to(
                        gates[r : r + 1, :], (HALF, LANES)
                    )
                    for s in range(HALF):
                        back_ref[at + a * HALF + s : at + a * HALF + s + 1, width:base] = acc[
                            r : r + 1, t * width + s * quarter : t * width + (s + 1) * quarter
                        ]


def tile_of(hidden):
    sizes = [n for n in range(16, 257, 16) if hidden % n == 0]
    return max(sizes) if sizes else hidden


def forward(copies, tensors, e, xr, gr, w_gate, w_up, w_down):
    hidden, depth = w_gate.shape
    width = depth // tensors
    rows = -(-copies * EXPERTS_ON * CAP // 16) * 16
    tile = tile_of(hidden)
    steps = hidden // tile
    back = (copies * tensors * MAIN, width + width // HALF + 2 * LANES)
    held = jax.ShapeDtypeStruct((rows, depth), BF16)
    per_unit = jax.ShapeDtypeStruct((steps, rows, tile), BF16)
    full = lambda shape: pl.BlockSpec(shape, lambda i: (0, 0))
    weights = pl.BlockSpec((tile, depth), lambda i: (i, 0))
    unit = pl.BlockSpec((1, rows, tile), lambda i: (i, 0, 0))
    return pl.pallas_call(
        functools.partial(forward_body, copies, tensors),
        grid=(steps,),
        out_shape=(held, held, per_unit, per_unit, per_unit, jax.ShapeDtypeStruct(back, F32)),
        in_specs=[pl.BlockSpec(memory_space=pltpu.SMEM), full(xr.shape), full(gr.shape), weights, weights, weights],
        out_specs=[full((rows, depth)), full((rows, depth)), unit, unit, unit, full(back)],
        scratch_shapes=[
            pltpu.VMEM((rows, LANES), F32),
            pltpu.VMEM((rows, depth), F32),
            pltpu.VMEM((rows, LANES), F32),
        ],
        compiler_params=pltpu.CompilerParams(vmem_limit_bytes=48 * MIB),
        cost_estimate=pl.CostEstimate(
            flops=10 * rows * hidden * depth, bytes_accessed=6 * hidden * depth, transcendentals=rows * hidden
        ),
        name="hidden_and_inputs",
    )(e, xr, gr, w_gate, w_up, w_down)


def weights_body(x_ref, g_ref, wt_ref, dh_ref, du_ref, og_ref, ou_ref, od_ref):
    tn = (((0,), (0,)), ((), ()))
    for left, right, out in ((dh_ref, x_ref, og_ref), (du_ref, x_ref, ou_ref), (wt_ref, g_ref, od_ref)):
        out[...] = lax.dot_general(left[0], right[...], tn, preferred_element_type=F32).astype(BF16)


def weight_grads(x, g, wt, dh, du):
    rows, depth = x.shape
    steps, _, tile = wt.shape
    hidden = steps * tile
    full = pl.BlockSpec((rows, depth), lambda i: (0, 0))
    unit = pl.BlockSpec((1, rows, tile), lambda i: (i, 0, 0))
    out = pl.BlockSpec((tile, depth), lambda i: (i, 0))
    return pl.pallas_call(
        weights_body,
        grid=(steps,),
        out_shape=[jax.ShapeDtypeStruct((hidden, depth), BF16)] * 3,
        in_specs=[full, full, unit, unit, unit],
        out_specs=[out, out, out],
        compiler_params=pltpu.CompilerParams(vmem_limit_bytes=48 * MIB),
        cost_estimate=pl.CostEstimate(
            flops=6 * rows * hidden * depth, bytes_accessed=6 * hidden * depth, transcendentals=0
        ),
        name="weight_grads",
    )(x, g, wt, dh, du)


def finish_body(first_ref, ids_ref, mine_ref, got_ref, tok_ref, gate_ref):
    ids = ids_ref[...]
    toks, width = tok_ref.shape
    quarter = width // HALF
    base = width + quarter
    expert, place, last = slots(first_ref[0], toks)
    main, hits = selection(ids, expert, place)
    tail, _ = selection(ids, expert, last)
    row = iota((MAIN, toks), 0)
    part = jnp.where(row >= HALF, row - HALF, row)
    tn = (((0,), (0,)), ((), ()))
    exact = dict(precision=lax.Precision.HIGHEST, preferred_element_type=F32)
    data = jnp.concatenate([got_ref[...], mine_ref[HALF:, :]], axis=0)
    for s in range(HALF):
        cols = slice(s * quarter, (s + 1) * quarter)
        one = jnp.where(part == s, tail, 0.0)
        tok_ref[:, cols] = (
            lax.dot_general(main, data[:, cols], tn, **exact)
            + lax.dot_general(one, data[:, width:base], tn, **exact)
        ).astype(BF16)
    term = main * data[:, base : base + 1] + jnp.where(part == 0, tail, 0.0) * data[:, base + LANES : base + LANES + 1]
    for k, hit in enumerate(hits):
        gate_ref[k : k + 1, :] = jnp.sum(jnp.where(hit, term, 0.0), axis=0, keepdims=True)


def finish(first, ids_t, mine, got, width):
    top, toks = ids_t.shape
    return pl.pallas_call(
        finish_body,
        out_shape=(jax.ShapeDtypeStruct((toks, width), BF16), jax.ShapeDtypeStruct((top, toks), F32)),
        in_specs=[pl.BlockSpec(memory_space=pltpu.SMEM)] + [pl.BlockSpec(memory_space=pltpu.VMEM)] * 3,
        out_specs=[pl.BlockSpec(memory_space=pltpu.VMEM)] * 2,
        name="finish_tokens",
    )(first, ids_t, mine, got)


def on_device(tokens, grad_out, expert_ids, gate_probs, w_gate, w_up, w_down):
    n_expert = lax.axis_size("expert")
    tensors = lax.axis_size("tensor")
    copies = n_expert // EXPERTS_ON
    e = (lax.axis_index("expert") // copies).astype(jnp.int32).reshape(1)
    zero = jnp.zeros((1,), jnp.int32)
    ids_t = expert_ids.T
    x_rows, g_rows = pick(zero, ids_t, gate_probs.T, tokens, grad_out)
    axes = ("expert", "tensor")
    xr = lax.all_gather(x_rows, axes, axis=0, tiled=True)
    gr = lax.all_gather(g_rows, axes, axis=0, tiled=True)
    x, g, wt, dh, du, back = forward(copies, tensors, e, xr, gr, w_gate, w_up, w_down)
    size = copies * tensors
    groups = [list(range(n * size, (n + 1) * size)) for n in range(EXPERTS_ON)]
    mine = lax.psum_scatter(back, axes, scatter_dimension=0, axis_index_groups=groups, tiled=True)
    swap = [(i, (i + copies) % n_expert) for i in range(n_expert)]
    got = lax.ppermute(mine[:HALF], "expert", swap)
    grad_w_gate, grad_w_up, grad_w_down = weight_grads(x, g, wt, dh, du)
    token_grad, gate_t = finish(1 - e, ids_t, mine, got, tokens.shape[1])
    return token_grad, gate_t.T, grad_w_gate, grad_w_up, grad_w_down


def solution(mesh):
    return jax.shard_map(
        on_device,
        mesh=mesh,
        in_specs=(
            P(("groups", "expert"), "tensor"),
            P(("groups", "expert"), "tensor"),
            P(("groups", "expert"), None),
            P(("groups", "expert"), None),
            P(("expert", "tensor"), None),
            P(("expert", "tensor"), None),
            P(("expert", "tensor"), None),
        ),
        out_specs=(
            P(("groups", "expert"), "tensor"),
            P(("groups", "expert"), None),
            P(("expert", "tensor"), "groups"),
            P(("expert", "tensor"), "groups"),
            P(("expert", "tensor"), "groups"),
        ),
        check_vma=False,
    )
```

```python
import functools

import jax
import jax.numpy as jnp
from jax import lax
from jax.experimental import pallas as pl
from jax.experimental.pallas import tpu as pltpu
from jax.sharding import PartitionSpec as P

EXPERTS_ON = 2
CAP = 5
LANES = 128
SUBS = 8
WHOLE = 4
F32 = jnp.float32
BF16 = jnp.bfloat16
MIB = 1 << 20
CHUNK = 512
VMEM = pl.BlockSpec(memory_space=pltpu.VMEM)
SMEM = pl.BlockSpec(memory_space=pltpu.SMEM)


def iota(shape, dim):
    return lax.broadcasted_iota(jnp.int32, shape, dim)


def chosen_rows(ids, expert, position):
    rows, toks = position.shape
    hits = [ids[k : k + 1, :] == expert for k in range(ids.shape[0])]
    member = functools.reduce(jnp.logical_or, hits).astype(F32)
    before = (iota((toks, toks), 0) < iota((toks, toks), 1)).astype(F32)
    earlier = jnp.dot(member, before, preferred_element_type=F32)
    return jnp.where(earlier == position.astype(F32), member, 0.0), hits


def sub_row(rows, toks):
    return iota((rows, toks), 0) % SUBS


def pick_body(e_ref, ids_ref, probs_ref, tok_ref, grad_ref, x_own, x_oth, g_own, g_oth):
    ids = ids_ref[...]
    probs = probs_ref[...].astype(F32)
    toks, width = tok_ref.shape
    half, eighth = width // 2, width // SUBS
    both = 2 * SUBS
    row = iota((both, toks), 0)
    sub = sub_row(both, toks)
    expert = jnp.where(row < SUBS, e_ref[0], 1 - e_ref[0])
    main, hits = chosen_rows(ids, expert, sub % WHOLE)
    tail, _ = chosen_rows(ids, expert, jnp.full((both, toks), WHOLE, jnp.int32))
    plain = jnp.where(sub < WHOLE, main, jnp.where(sub == WHOLE, tail, 0.0))
    for src, own, oth in ((tok_ref, x_own, x_oth), (grad_ref, g_own, g_oth)):
        packed = sum(
            jnp.dot(
                jnp.where(sub // WHOLE == h, main, 0.0).astype(BF16),
                src[:, h * half : (h + 1) * half],
                preferred_element_type=F32,
            )
            for h in range(2)
        ).astype(BF16)
        last = sum(
            jnp.dot(
                jnp.where(sub == s, tail, 0.0).astype(BF16),
                src[:, s * eighth : (s + 1) * eighth],
                preferred_element_type=F32,
            )
            for s in range(SUBS)
        ).astype(BF16)
        for n, dst in enumerate((own, oth)):
            dst[:, :half] = packed[n * SUBS : (n + 1) * SUBS]
            dst[:, half : half + eighth] = last[n * SUBS : (n + 1) * SUBS]
    weight = sum(jnp.where(hit, probs[k : k + 1, :], 0.0) for k, hit in enumerate(hits))
    gate = jnp.broadcast_to(jnp.sum(plain * weight, axis=1, keepdims=True), (both, LANES)).astype(BF16)
    for n, dst in enumerate((x_own, x_oth)):
        dst[:, half + eighth :] = gate[n * SUBS : (n + 1) * SUBS]


def pick(e, ids_t, probs_t, tokens, grad_out):
    width = tokens.shape[1]
    size = width // 2 + width // SUBS
    with_gate = jax.ShapeDtypeStruct((SUBS, size + LANES), BF16)
    without = jax.ShapeDtypeStruct((SUBS, size), BF16)
    return pl.pallas_call(
        pick_body,
        out_shape=(with_gate, with_gate, without, without),
        in_specs=[SMEM] + [VMEM] * 4,
        out_specs=[VMEM] * 4,
        name="pick_rows",
    )(e, ids_t, probs_t, tokens, grad_out)


def assemble_body(count, width, *refs):
    pieces, outs, held = refs[:count], refs[count:-1], refs[-1]
    half, eighth = width // 2, width // SUBS
    held[...] = jnp.zeros_like(held)
    for n, ref in enumerate(pieces):
        piece = ref[...].astype(F32)
        at = n * SUBS
        for h in range(2):
            held[at : at + WHOLE, h * half : (h + 1) * half] = piece[h * WHOLE : (h + 1) * WHOLE, :half]
        for s in range(SUBS):
            held[at + WHOLE : at + WHOLE + 1, s * eighth : (s + 1) * eighth] = piece[s : s + 1, half : half + eighth]
        if len(outs) == 2:
            outs[1][at : at + SUBS, :] = piece[:, half + eighth :]
    outs[0][...] = held[...].astype(BF16)


def assemble(pieces, width, gated):
    count = len(pieces)
    rows = count * SUBS
    shapes = [jax.ShapeDtypeStruct((rows, width), BF16)]
    if gated:
        shapes.append(jax.ShapeDtypeStruct((rows, LANES), F32))
    return pl.pallas_call(
        functools.partial(assemble_body, count, width),
        out_shape=shapes,
        in_specs=[VMEM] * count,
        out_specs=[VMEM] * len(shapes),
        scratch_shapes=[pltpu.VMEM((rows, width), F32)],
        name="assemble_rows",
    )(*pieces)


def tile_of(hidden, most):
    sizes = [n for n in range(16, most + 1, 16) if hidden % n == 0]
    return max(sizes) if sizes else hidden


def column_map(chunks):
    return lambda i, t: jnp.where(i < chunks, t, 1 - t) * chunks + lax.rem(i, chunks)


NT = (((1,), (1,)), ((), ()))


def hidden_body(chunks, t_ref, xa_ref, xb_ref, wg_ref, wu_ref, h_ref, u_ref):
    step = pl.program_id(0)
    x = jnp.where(step < chunks, xa_ref[...], xb_ref[...])

    @pl.when(step == 0)
    def _():
        h_ref[...] = jnp.zeros_like(h_ref)
        u_ref[...] = jnp.zeros_like(u_ref)

    h_ref[...] += lax.dot_general(wg_ref[...], x, NT, preferred_element_type=F32)
    u_ref[...] += lax.dot_general(wu_ref[...], x, NT, preferred_element_type=F32)


def halves_specs(rows, chunk, chunks):
    own = pl.BlockSpec((rows, chunk), lambda i, t: (0, jnp.minimum(i, chunks - 1)))
    oth = pl.BlockSpec((rows, chunk), lambda i, t: (0, jnp.clip(i - chunks, 0, chunks - 1)))
    return [own, oth]


def hidden_units(t, xa, xb, w_gate, w_up):
    hidden, depth = w_gate.shape
    rows, width = xa.shape
    chunk = CHUNK
    chunks = width // chunk
    column = column_map(chunks)
    unit = jax.ShapeDtypeStruct((hidden, rows), F32)
    kept = pl.BlockSpec((hidden, rows), lambda i, t: (0, 0))
    weight = pl.BlockSpec((hidden, chunk), lambda i, t: (0, column(i, t[0])))
    return pl.pallas_call(
        functools.partial(hidden_body, chunks),
        out_shape=(unit, unit),
        grid_spec=pltpu.PrefetchScalarGridSpec(
            num_scalar_prefetch=1,
            grid=(2 * chunks,),
            in_specs=halves_specs(rows, chunk, chunks) + [weight, weight],
            out_specs=[kept, kept],
        ),
        compiler_params=pltpu.CompilerParams(vmem_limit_bytes=32 * MIB),
        cost_estimate=pl.CostEstimate(
            flops=4 * rows * hidden * depth, bytes_accessed=4 * hidden * depth, transcendentals=0
        ),
        name="hidden_units",
    )(t, xa, xb, w_gate, w_up)


def inputs_body(chunks, t_ref, ga_ref, gb_ref, factor_ref, h_ref, u_ref, wd_ref, wg_ref, wu_ref,
                wt_ref, dh_ref, du_ref, dhr_ref, dur_ref, gate_ref, give_ref, dact):
    step = pl.program_id(0)
    last = 2 * chunks - 1
    rows = ga_ref.shape[0]

    @pl.when(step == 0)
    def _():
        dact[...] = jnp.zeros_like(dact)

    @pl.when(step <= last)
    def _():
        g = jnp.where(step < chunks, ga_ref[...], gb_ref[...])
        dact[...] += lax.dot_general(wd_ref[...], g, NT, preferred_element_type=F32)

    @pl.when(step == last)
    def _():
        weight = factor_ref[...].T[:1, :]
        h = h_ref[...]
        u = u_ref[...]
        da = dact[...]
        sigma = 1.0 / (1.0 + jnp.exp(-h))
        silu = h * sigma
        act = silu * u
        scaled = weight * da
        wt_ref[...] = (weight * act).astype(BF16)
        dh = scaled * u * sigma * (1.0 + h * (1.0 - sigma))
        du = scaled * silu
        dh_ref[...] = dh.astype(BF16)
        du_ref[...] = du.astype(BF16)
        dhr_ref[...] = dh.T.astype(BF16)
        dur_ref[...] = du.T.astype(BF16)
        total = jnp.sum(act * da, axis=0, keepdims=True)
        gate_ref[...] = jnp.broadcast_to(total, (LANES, rows)).T

    @pl.when(step > last)
    def _():
        give_ref[...] = jnp.dot(dhr_ref[...], wg_ref[...], preferred_element_type=F32) + jnp.dot(
            dur_ref[...], wu_ref[...], preferred_element_type=F32
        )


def first_input_grads(t, ga, gb, factor, h, u, w_gate, w_up, w_down):
    hidden, depth = w_gate.shape
    rows, width = ga.shape
    chunk = CHUNK
    chunks = width // chunk
    column = column_map(chunks)
    last = 2 * chunks - 1
    full = lambda shape: pl.BlockSpec(shape, lambda i, t: (0, 0))
    down = pl.BlockSpec((hidden, chunk), lambda i, t: (0, column(jnp.minimum(i, last), t[0])))
    later = lambda i: jnp.maximum(i - last - 1, 0)
    other = pl.BlockSpec((hidden, chunk), lambda i, t: (0, column(chunks + later(i), t[0])))
    unit = jax.ShapeDtypeStruct((hidden, rows), BF16)
    turned = jax.ShapeDtypeStruct((rows, hidden), BF16)
    return pl.pallas_call(
        functools.partial(inputs_body, chunks),
        out_shape=(
            unit,
            unit,
            unit,
            turned,
            turned,
            jax.ShapeDtypeStruct((rows, LANES), F32),
            jax.ShapeDtypeStruct((rows, width), F32),
        ),
        grid_spec=pltpu.PrefetchScalarGridSpec(
            num_scalar_prefetch=1,
            grid=(3 * chunks,),
            in_specs=halves_specs(rows, chunk, chunks)
            + [full((rows, LANES)), full((hidden, rows)), full((hidden, rows)), down, other, other],
            out_specs=[full((hidden, rows))] * 3
            + [full((rows, hidden))] * 2
            + [full((rows, LANES)), pl.BlockSpec((rows, chunk), lambda i, t: (0, later(i)))],
            scratch_shapes=[pltpu.VMEM((hidden, rows), F32)],
        ),
        compiler_params=pltpu.CompilerParams(vmem_limit_bytes=40 * MIB),
        cost_estimate=pl.CostEstimate(
            flops=4 * rows * hidden * depth, bytes_accessed=4 * hidden * depth, transcendentals=rows * hidden
        ),
        name="give_half",
    )(t, ga, gb, factor, h, u, w_down, w_gate, w_up)


def keep_body(t_ref, dhr_ref, dur_ref, wg_ref, wu_ref, keep_ref):
    keep_ref[...] = jnp.dot(dhr_ref[...], wg_ref[...], preferred_element_type=F32) + jnp.dot(
        dur_ref[...], wu_ref[...], preferred_element_type=F32
    )


def second_input_grads(t, dhr, dur, w_gate, w_up, width):
    hidden, depth = w_gate.shape
    rows = dhr.shape[0]
    chunk = CHUNK
    chunks = width // chunk
    column = column_map(chunks)
    full = pl.BlockSpec((rows, hidden), lambda i, t: (0, 0))
    own = pl.BlockSpec((hidden, chunk), lambda i, t: (0, column(i, t[0])))
    return pl.pallas_call(
        keep_body,
        out_shape=jax.ShapeDtypeStruct((rows, width), F32),
        grid_spec=pltpu.PrefetchScalarGridSpec(
            num_scalar_prefetch=1,
            grid=(chunks,),
            in_specs=[full, full, own, own],
            out_specs=pl.BlockSpec((rows, chunk), lambda i, t: (0, i)),
        ),
        compiler_params=pltpu.CompilerParams(vmem_limit_bytes=32 * MIB),
        cost_estimate=pl.CostEstimate(
            flops=4 * rows * hidden * width, bytes_accessed=4 * hidden * width, transcendentals=0
        ),
        name="keep_half",
    )(t, dhr, dur, w_gate, w_up)


def weights_body(t_ref, left_ref, own_ref, oth_ref, out_ref):
    width = own_ref.shape[1]
    t = t_ref[0]
    for at, ref in ((t, own_ref), (1 - t, oth_ref)):
        cols = pl.ds(pl.multiple_of(at * width, width), width)
        out_ref[:, cols] = jnp.dot(left_ref[...], ref[...], preferred_element_type=F32).astype(BF16)


def weight_grad(t, left, own, oth, name):
    hidden, rows = left.shape
    width = own.shape[1]
    depth = 2 * width
    tile = tile_of(hidden, 192)
    half = pl.BlockSpec((rows, width), lambda i, t: (0, 0))
    return pl.pallas_call(
        weights_body,
        out_shape=jax.ShapeDtypeStruct((hidden, depth), BF16),
        grid_spec=pltpu.PrefetchScalarGridSpec(
            num_scalar_prefetch=1,
            grid=(hidden // tile,),
            in_specs=[pl.BlockSpec((tile, rows), lambda i, t: (i, 0)), half, half],
            out_specs=pl.BlockSpec((tile, depth), lambda i, t: (i, 0)),
        ),
        compiler_params=pltpu.CompilerParams(vmem_limit_bytes=24 * MIB),
        cost_estimate=pl.CostEstimate(
            flops=2 * rows * hidden * depth, bytes_accessed=2 * hidden * depth, transcendentals=0
        ),
        name=name,
    )(t, left, own, oth)


def fold_body(copies, keep_ref, got_ref, gate_mine, gate_got, *outs):
    width = keep_ref.shape[1]
    half, eighth = width // 2, width // SUBS
    both = 2 * SUBS
    for d in range(copies):
        out = outs[d]
        for a in range(2):
            r = d * both + a * SUBS
            to = a * SUBS
            block = keep_ref[r : r + SUBS, :] + got_ref[r : r + SUBS, :]
            for h in range(2):
                out[to + h * WHOLE : to + (h + 1) * WHOLE, :half] = block[:WHOLE, h * half : (h + 1) * half]
            for s in range(SUBS):
                out[to + s : to + s + 1, half : half + eighth] = block[
                    WHOLE : WHOLE + 1, s * eighth : (s + 1) * eighth
                ]
            out[to : to + SUBS, half + eighth :] = gate_mine[r : r + SUBS, :] + gate_got[r : r + SUBS, :]


def fold(copies, keep, got, gate_mine, gate_got):
    width = keep.shape[1]
    size = width // 2 + width // SUBS + LANES
    return pl.pallas_call(
        functools.partial(fold_body, copies),
        out_shape=[jax.ShapeDtypeStruct((2 * SUBS, size), F32)] * copies,
        in_specs=[VMEM] * 4,
        out_specs=[VMEM] * copies,
        name="fold_cores",
    )(keep, got, gate_mine, gate_got)


def finish_body(e_ref, ids_ref, mine_ref, got_ref, tok_ref, gate_ref):
    ids = ids_ref[...]
    toks, width = tok_ref.shape
    half, eighth = width // 2, width // SUBS
    both = 2 * SUBS
    row = iota((both, toks), 0)
    sub = sub_row(both, toks)
    expert = jnp.where(row < SUBS, e_ref[0], 1 - e_ref[0])
    main, hits = chosen_rows(ids, expert, sub % WHOLE)
    tail, _ = chosen_rows(ids, expert, jnp.full((both, toks), WHOLE, jnp.int32))
    plain = jnp.where(sub < WHOLE, main, jnp.where(sub == WHOLE, tail, 0.0))
    data = jnp.concatenate([mine_ref[...], got_ref[...]], axis=0)
    tn = (((0,), (0,)), ((), ()))
    exact = dict(precision=lax.Precision.HIGHEST, preferred_element_type=F32)
    halves = [
        lax.dot_general(jnp.where(sub // WHOLE == h, main, 0.0), data[:, :half], tn, **exact) for h in range(2)
    ]
    for s in range(SUBS):
        last = lax.dot_general(jnp.where(sub == s, tail, 0.0), data[:, half : half + eighth], tn, **exact)
        h, at = divmod(s * eighth, half)
        tok_ref[:, s * eighth : (s + 1) * eighth] = (halves[h][:, at : at + eighth] + last).astype(BF16)
    term = plain * data[:, half + eighth : half + eighth + 1]
    for k, hit in enumerate(hits):
        gate_ref[k : k + 1, :] = jnp.sum(jnp.where(hit, term, 0.0), axis=0, keepdims=True)


def finish(e, ids_t, mine, got, width):
    top, toks = ids_t.shape
    return pl.pallas_call(
        finish_body,
        out_shape=(jax.ShapeDtypeStruct((toks, width), BF16), jax.ShapeDtypeStruct((top, toks), F32)),
        in_specs=[SMEM] + [VMEM] * 3,
        out_specs=[VMEM] * 2,
        name="finish_tokens",
    )(e, ids_t, mine, got)


def on_device(tokens, grad_out, expert_ids, gate_probs, w_gate, w_up, w_down):
    n_expert = lax.axis_size("expert")
    copies = n_expert // EXPERTS_ON
    place = lax.axis_index("expert")
    e = (place >= copies).astype(jnp.int32).reshape(1)
    t = lax.axis_index("tensor").astype(jnp.int32).reshape(1)
    width = tokens.shape[1]

    def partner(v):
        return lax.ppermute(v, "expert", [(i, (i + copies) % n_expert) for i in range(n_expert)])

    def across(v, d):
        return lax.ppermute(v, "expert", [(i, i ^ d) for i in range(n_expert)])

    def other_core(v):
        return lax.ppermute(v, "tensor", [(0, 1), (1, 0)])

    def spread(own, oth):
        got = partner(oth)
        first = [own if d == 0 else across(own, d) for d in range(copies)]
        second = [got if d == 0 else across(got, d) for d in range(copies)]
        return [piece for pair in zip(first, second) for piece in pair]

    w_gate, w_up, w_down = (pltpu.with_memory_space_constraint(w, pltpu.HBM) for w in (w_gate, w_up, w_down))
    ids_t = expert_ids.T
    x_own, x_oth, g_own, g_oth = pick(e, ids_t, gate_probs.T, tokens, grad_out)
    xa, factor = assemble(spread(x_own, x_oth), width, True)
    xb = other_core(xa)
    (ga,) = assemble(spread(g_own, g_oth), width, False)
    gb = other_core(ga)
    h, u = hidden_units(t, xa, xb, w_gate, w_up)
    wt, dh, du, dhr, dur, gate, give = first_input_grads(t, ga, gb, factor, h, u, w_gate, w_up, w_down)
    got, gate_got = other_core(give), other_core(gate)
    keep = second_input_grads(t, dhr, dur, w_gate, w_up, width)
    keep, got, gate_got = lax.optimization_barrier((keep, got, gate_got))
    blocks = fold(copies, keep, got, gate, gate_got)
    arrived = [across(blocks[d], d) for d in range(1, copies)]
    dh, mine = lax.optimization_barrier((dh, blocks[0]))
    grad_w_gate = weight_grad(t, dh, xa, xb, "grad_w_gate")
    grad_w_gate, du, arrived = lax.optimization_barrier((grad_w_gate, du, arrived))
    summed = functools.reduce(jnp.add, arrived, mine)
    theirs = partner(summed[SUBS:])
    du, summed = lax.optimization_barrier((du, summed))
    grad_w_up = weight_grad(t, du, xa, xb, "grad_w_up")
    grad_w_down = weight_grad(t, wt, ga, gb, "grad_w_down")
    grad_w_up, grad_w_down, theirs = lax.optimization_barrier((grad_w_up, grad_w_down, theirs))
    token_grad, gate_t = finish(e, ids_t, summed[:SUBS], theirs, width)
    return token_grad, gate_t.T, grad_w_gate, grad_w_up, grad_w_down


def solution(mesh):
    return jax.shard_map(
        on_device,
        mesh=mesh,
        in_specs=(
            P(("groups", "expert"), "tensor"),
            P(("groups", "expert"), "tensor"),
            P(("groups", "expert"), None),
            P(("groups", "expert"), None),
            P(("expert", "tensor"), None),
            P(("expert", "tensor"), None),
            P(("expert", "tensor"), None),
        ),
        out_specs=(
            P(("groups", "expert"), "tensor"),
            P(("groups", "expert"), None),
            P(("expert", "tensor"), "groups"),
            P(("expert", "tensor"), "groups"),
            P(("expert", "tensor"), "groups"),
        ),
        check_vma=False,
    )
```

```python
import functools

import jax
import jax.numpy as jnp
from jax import lax
from jax.experimental import pallas as pl
from jax.experimental.pallas import tpu as pltpu
from jax.sharding import PartitionSpec as P

EXPERTS_ON = 2
CAP = 5
LANES = 128
SUBS = 8
WHOLE = 4
F32 = jnp.float32
BF16 = jnp.bfloat16
MIB = 1 << 20
VMEM = pl.BlockSpec(memory_space=pltpu.VMEM)
SMEM = pl.BlockSpec(memory_space=pltpu.SMEM)
HBM = pl.BlockSpec(memory_space=pltpu.HBM)


def iota(shape, dim):
    return lax.broadcasted_iota(jnp.int32, shape, dim)


def chosen_rows(ids, expert, position):
    rows, toks = position.shape
    hits = [ids[k : k + 1, :] == expert for k in range(ids.shape[0])]
    member = functools.reduce(jnp.logical_or, hits).astype(F32)
    before = (iota((toks, toks), 0) < iota((toks, toks), 1)).astype(F32)
    earlier = jnp.dot(member, before, preferred_element_type=F32)
    return jnp.where(earlier == position.astype(F32), member, 0.0), hits


def sub_row(rows, toks):
    return iota((rows, toks), 0) % SUBS


def tile_of(hidden, most):
    sizes = [n for n in range(16, most + 1, 16) if hidden % n == 0]
    return max(sizes) if sizes else hidden


def pick_body(e_ref, ids_ref, probs_ref, tok_ref, grad_ref, own_ref, oth_ref):
    ids = ids_ref[...]
    probs = probs_ref[...].astype(F32)
    toks, width = tok_ref.shape
    half, eighth = width // 2, width // SUBS
    size = half + eighth
    both = 2 * SUBS
    row = iota((both, toks), 0)
    sub = sub_row(both, toks)
    expert = jnp.where(row < SUBS, e_ref[0], 1 - e_ref[0])
    main, hits = chosen_rows(ids, expert, sub % WHOLE)
    tail, _ = chosen_rows(ids, expert, jnp.full((both, toks), WHOLE, jnp.int32))
    plain = jnp.where(sub < WHOLE, main, jnp.where(sub == WHOLE, tail, 0.0))
    halves = [jnp.where(sub // WHOLE == h, main, 0.0).astype(BF16) for h in range(2)]
    eighths = [jnp.where(sub == s, tail, 0.0).astype(BF16) for s in range(SUBS)]
    for at, src in enumerate((tok_ref, grad_ref)):
        packed = sum(
            jnp.dot(one, src[:, h * half : (h + 1) * half], preferred_element_type=F32)
            for h, one in enumerate(halves)
        ).astype(BF16)
        last = sum(
            jnp.dot(one, src[:, s * eighth : (s + 1) * eighth], preferred_element_type=F32)
            for s, one in enumerate(eighths)
        ).astype(BF16)
        for n, dst in enumerate((own_ref, oth_ref)):
            dst[:, at * size : at * size + half] = packed[n * SUBS : (n + 1) * SUBS]
            dst[:, at * size + half : (at + 1) * size] = last[n * SUBS : (n + 1) * SUBS]
    weight = sum(jnp.where(hit, probs[k : k + 1, :], 0.0) for k, hit in enumerate(hits))
    gate = jnp.broadcast_to(jnp.sum(plain * weight, axis=1, keepdims=True), (both, LANES)).astype(BF16)
    for n, dst in enumerate((own_ref, oth_ref)):
        dst[:, 2 * size :] = gate[n * SUBS : (n + 1) * SUBS]


def pick(e, ids_t, probs_t, tokens, grad_out):
    width = tokens.shape[1]
    size = width // 2 + width // SUBS
    piece = jax.ShapeDtypeStruct((SUBS, 2 * size + LANES), BF16)
    return pl.pallas_call(
        pick_body,
        out_shape=(piece, piece),
        in_specs=[SMEM] + [VMEM] * 4,
        out_specs=[VMEM] * 2,
        name="pick_rows",
    )(e, ids_t, probs_t, tokens, grad_out)


def assemble_body(count, *refs):
    pieces, (x_ref, g_ref, factor_ref, held) = refs[:count], refs[count:]
    width = x_ref.shape[1]
    half, eighth = width // 2, width // SUBS
    size = half + eighth
    held[...] = jnp.zeros_like(held)
    for side, out in enumerate((x_ref, g_ref)):
        base = side * size
        for n, ref in enumerate(pieces):
            at = n * SUBS
            piece = ref[:, base : base + size].astype(F32)
            for h in range(2):
                held[at : at + WHOLE, h * half : (h + 1) * half] = piece[h * WHOLE : (h + 1) * WHOLE, :half]
            for s in range(SUBS):
                held[at + WHOLE : at + WHOLE + 1, s * eighth : (s + 1) * eighth] = piece[s : s + 1, half:]
        out[...] = held[...].astype(BF16)
    for n, ref in enumerate(pieces):
        factor_ref[n * SUBS : (n + 1) * SUBS, :] = ref[:, 2 * size :].astype(F32)


def assemble(pieces, width):
    count = len(pieces)
    rows = count * SUBS
    held = jax.ShapeDtypeStruct((rows, width), BF16)
    return pl.pallas_call(
        functools.partial(assemble_body, count),
        out_shape=(held, held, jax.ShapeDtypeStruct((rows, LANES), F32)),
        in_specs=[VMEM] * count,
        out_specs=[VMEM] * 3,
        scratch_shapes=[pltpu.VMEM((rows, width), F32)],
        name="assemble_rows",
    )(*pieces)


NT = (((1,), (1,)), ((), ()))


def chunk_of(width, most):
    return max(n for n in range(LANES, most + 1, LANES) if width % n == 0)


def place_of(step, chunks, chunk, t):
    side = jnp.where(step < chunks, t, 1 - t)
    return pl.multiple_of((side * chunks + lax.rem(step, chunks)) * chunk, chunk)


def half_grad(part, wg_ref, wu_ref, dhr_ref, dur_ref, base, chunk):
    def step(c, carry):
        at = pl.multiple_of(c * chunk, chunk)
        cols = pl.ds(base + at, chunk)
        part[:, pl.ds(at, chunk)] = jnp.dot(dhr_ref[...], wg_ref[:, cols], preferred_element_type=F32) + jnp.dot(
            dur_ref[...], wu_ref[:, cols], preferred_element_type=F32
        )
        return carry

    lax.fori_loop(0, part.shape[1] // chunk, step, 0)


def pack_rows(part, gates, out):
    rows, width = part.shape
    half, eighth = width // 2, width // SUBS
    for at in range(0, rows, SUBS):
        for h in range(2):
            out[at + h * WHOLE : at + (h + 1) * WHOLE, :half] = part[at : at + WHOLE, h * half : (h + 1) * half]
        for s in range(SUBS):
            out[at + s : at + s + 1, half : half + eighth] = part[
                at + WHOLE : at + WHOLE + 1, s * eighth : (s + 1) * eighth
            ]
    out[:, half + eighth :] = gates


def experts_body(chunk, t_ref, xa_ref, xb_ref, ga_ref, gb_ref, factor_ref, wg_hbm, wu_hbm, wd_hbm,
                 wt_ref, dh_ref, du_ref, give_ref, keep_ref,
                 wg_ref, wu_ref, ring, h_ref, u_ref, da_ref, dhr_ref, dur_ref, part, landed, ring_landed):
    rows, width = xa_ref.shape
    chunks = width // chunk
    depth = ring.shape[0]
    steps = 2 * chunks
    t = t_ref[0]

    def load(i, n):
        cols = pl.ds(place_of(i, chunks, chunk, t), chunk)
        src, dst = ((wg_hbm, wg_ref), (wu_hbm, wu_ref))[n]
        return pltpu.make_async_copy(src.at[:, cols], dst.at[:, cols], landed.at[i, n])

    def load_down(i):
        cols = pl.ds(place_of(i, chunks, chunk, t), chunk)
        slot = lax.rem(i, depth)
        return pltpu.make_async_copy(wd_hbm.at[:, cols], ring.at[slot], ring_landed.at[slot])

    for i in range(steps):
        for n in range(2):
            load(i, n).start()
    for i in range(min(steps, depth)):
        load_down(i).start()

    def add_to(out, i, w, x):
        more = lax.dot_general(w, x, NT, preferred_element_type=F32)
        out[...] = jnp.where(i == 0, more, out[...] + more)

    for side, x_ref in enumerate((xa_ref, xb_ref)):

        def up_step(c, carry):
            i = side * chunks + c
            x = x_ref[:, pl.ds(pl.multiple_of(c * chunk, chunk), chunk)]
            cols = pl.ds(place_of(i, chunks, chunk, t), chunk)
            for n, (w, out) in enumerate(((wg_ref, h_ref), (wu_ref, u_ref))):
                load(i, n).wait()
                add_to(out, i, w[:, cols], x)
            return carry

        lax.fori_loop(0, chunks, up_step, 0)

    for side, g_ref in enumerate((ga_ref, gb_ref)):

        def down_step(c, carry):
            i = side * chunks + c
            g = g_ref[:, pl.ds(pl.multiple_of(c * chunk, chunk), chunk)]
            load_down(i).wait()
            add_to(da_ref, i, ring[lax.rem(i, depth)], g)

            @pl.when(i + depth < steps)
            def _():
                load_down(i + depth).start()

            return carry

        lax.fori_loop(0, chunks, down_step, 0)

    weight = factor_ref[...].T[:1, :]
    h = h_ref[...]
    u = u_ref[...]
    da = da_ref[...]
    sigma = 1.0 / (1.0 + jnp.exp(-h))
    silu = h * sigma
    act = silu * u
    scaled = weight * da
    wt_ref[...] = (weight * act).astype(BF16)
    dh = scaled * u * sigma * (1.0 + h * (1.0 - sigma))
    du = scaled * silu
    dh_ref[...] = dh.astype(BF16)
    du_ref[...] = du.astype(BF16)
    dhr_ref[...] = dh.T.astype(BF16)
    dur_ref[...] = du.T.astype(BF16)
    total = jnp.sum(act * da, axis=0, keepdims=True)
    gates = jnp.broadcast_to(total, (LANES, rows)).T
    for at, out in ((1 - t, give_ref), (t, keep_ref)):
        base = pl.multiple_of(at * width, width)
        half_grad(part, wg_ref, wu_ref, dhr_ref, dur_ref, base, chunk_of(width, 512))
        pack_rows(part, gates, out)


def expert_units(t, xa, xb, ga, gb, factor, w_gate, w_up, w_down):
    hidden, depth = w_gate.shape
    rows, width = xa.shape
    chunk = chunk_of(width, 1024)
    steps = depth // chunk
    ring = min(3, steps)
    unit = jax.ShapeDtypeStruct((hidden, rows), BF16)
    packed = jax.ShapeDtypeStruct((rows, width // 2 + width // SUBS + LANES), F32)
    return pl.pallas_call(
        functools.partial(experts_body, chunk),
        out_shape=(unit, unit, unit, packed, packed),
        in_specs=[SMEM] + [VMEM] * 5 + [HBM] * 3,
        out_specs=[VMEM] * 5,
        scratch_shapes=[
            pltpu.VMEM((hidden, depth), BF16),
            pltpu.VMEM((hidden, depth), BF16),
            pltpu.VMEM((ring, hidden, chunk), BF16),
            pltpu.VMEM((hidden, rows), F32),
            pltpu.VMEM((hidden, rows), F32),
            pltpu.VMEM((hidden, rows), F32),
            pltpu.VMEM((rows, hidden), BF16),
            pltpu.VMEM((rows, hidden), BF16),
            pltpu.VMEM((rows, width), F32),
            pltpu.SemaphoreType.DMA((steps, 2)),
            pltpu.SemaphoreType.DMA((ring,)),
        ],
        compiler_params=pltpu.CompilerParams(vmem_limit_bytes=48 * MIB),
        cost_estimate=pl.CostEstimate(
            flops=10 * rows * hidden * depth, bytes_accessed=6 * hidden * depth, transcendentals=rows * hidden
        ),
        name="expert_units",
    )(t, xa, xb, ga, gb, factor, w_gate, w_up, w_down)


def weights_body(chunk, t_ref, left_ref, own_ref, oth_ref, out_ref, ring, sent):
    width = own_ref.shape[1]
    chunks = width // chunk
    depth = ring.shape[0]
    hidden = left_ref.shape[0]
    tile = tile_of(hidden, 448)
    t = t_ref[0]

    def store(i):
        cols = pl.ds(place_of(i, chunks, chunk, t), chunk)
        slot = lax.rem(i, depth)
        return pltpu.make_async_copy(ring.at[slot], out_ref.at[:, cols], sent.at[slot])

    for side, x_ref in enumerate((own_ref, oth_ref)):

        def step(c, carry):
            i = side * chunks + c
            slot = lax.rem(i, depth)

            @pl.when(i >= depth)
            def _():
                store(i - depth).wait()

            x = x_ref[:, pl.ds(pl.multiple_of(c * chunk, chunk), chunk)]
            for at in range(0, hidden, tile):
                ring[slot, at : at + tile, :] = jnp.dot(
                    left_ref[at : at + tile, :], x, preferred_element_type=F32
                ).astype(BF16)
            store(i).start()
            return carry

        lax.fori_loop(0, chunks, step, 0)
    for i in range(max(0, 2 * chunks - depth), 2 * chunks):
        store(i).wait()


def weight_grad(t, left, own, oth, name):
    hidden, rows = left.shape
    width = own.shape[1]
    depth = 2 * width
    chunk = chunk_of(width, 512)
    ring = min(4, depth // chunk)
    return pl.pallas_call(
        functools.partial(weights_body, chunk),
        out_shape=jax.ShapeDtypeStruct((hidden, depth), BF16),
        in_specs=[SMEM] + [VMEM] * 3,
        out_specs=HBM,
        scratch_shapes=[pltpu.VMEM((ring, hidden, chunk), BF16), pltpu.SemaphoreType.DMA((ring,))],
        compiler_params=pltpu.CompilerParams(vmem_limit_bytes=24 * MIB),
        cost_estimate=pl.CostEstimate(
            flops=2 * rows * hidden * depth, bytes_accessed=2 * hidden * depth, transcendentals=0
        ),
        name=name,
    )(t, left, own, oth)


def finish_body(e_ref, ids_ref, mine_ref, got_ref, tok_ref, gate_ref):
    ids = ids_ref[...]
    toks, width = tok_ref.shape
    half, eighth = width // 2, width // SUBS
    both = 2 * SUBS
    row = iota((both, toks), 0)
    sub = sub_row(both, toks)
    expert = jnp.where(row < SUBS, e_ref[0], 1 - e_ref[0])
    main, hits = chosen_rows(ids, expert, sub % WHOLE)
    tail, _ = chosen_rows(ids, expert, jnp.full((both, toks), WHOLE, jnp.int32))
    plain = jnp.where(sub < WHOLE, main, jnp.where(sub == WHOLE, tail, 0.0))
    data = jnp.concatenate([mine_ref[...], got_ref[...]], axis=0)
    tn = (((0,), (0,)), ((), ()))
    exact = dict(precision=lax.Precision.HIGHEST, preferred_element_type=F32)
    halves = [
        lax.dot_general(jnp.where(sub // WHOLE == h, main, 0.0), data[:, :half], tn, **exact) for h in range(2)
    ]
    for s in range(SUBS):
        last = lax.dot_general(jnp.where(sub == s, tail, 0.0), data[:, half : half + eighth], tn, **exact)
        h, at = divmod(s * eighth, half)
        tok_ref[:, s * eighth : (s + 1) * eighth] = (halves[h][:, at : at + eighth] + last).astype(BF16)
    term = plain * data[:, half + eighth : half + eighth + 1]
    for k, hit in enumerate(hits):
        gate_ref[k : k + 1, :] = jnp.sum(jnp.where(hit, term, 0.0), axis=0, keepdims=True)


def finish(e, ids_t, mine, got, width):
    top, toks = ids_t.shape
    return pl.pallas_call(
        finish_body,
        out_shape=(jax.ShapeDtypeStruct((toks, width), BF16), jax.ShapeDtypeStruct((top, toks), F32)),
        in_specs=[SMEM] + [VMEM] * 3,
        out_specs=[VMEM] * 2,
        name="finish_tokens",
    )(e, ids_t, mine, got)


def on_device(tokens, grad_out, expert_ids, gate_probs, w_gate, w_up, w_down):
    n_expert = lax.axis_size("expert")
    copies = n_expert // EXPERTS_ON
    place = lax.axis_index("expert")
    e = (place >= copies).astype(jnp.int32).reshape(1)
    t = lax.axis_index("tensor").astype(jnp.int32).reshape(1)
    width = tokens.shape[1]

    def partner(v):
        return lax.ppermute(v, "expert", [(i, (i + copies) % n_expert) for i in range(n_expert)])

    def across(v, d):
        return lax.ppermute(v, "expert", [(i, i ^ d) for i in range(n_expert)])

    def other_core(v):
        return lax.ppermute(v, "tensor", [(0, 1), (1, 0)])

    ids_t = expert_ids.T
    own, oth = pick(e, ids_t, gate_probs.T, tokens, grad_out)
    first, second = [own], [partner(oth)]
    d = 1
    while d < copies:
        first += [across(piece, d) for piece in first]
        second += [across(piece, d) for piece in second]
        d *= 2
    xa, ga, factor = assemble([piece for pair in zip(first, second) for piece in pair], width)
    xb = other_core(xa)
    gb = other_core(ga)
    wt, dh, du, give, keep = expert_units(t, xa, xb, ga, gb, factor, w_gate, w_up, w_down)
    total = keep + other_core(give)
    grads = []
    jobs = [(dh, xa, xb, "grad_w_gate"), (du, xa, xb, "grad_w_up"), (wt, ga, gb, "grad_w_down")]
    d = copies // 2
    while d:
        rows = d * 2 * SUBS
        coming = across(total[rows:], d)
        if len(jobs) > 1:
            left, a, b, name = jobs.pop(0)
            left, total = lax.optimization_barrier((left, total))
            grads.append(weight_grad(t, left, a, b, name))
            grads[-1], coming = lax.optimization_barrier((grads[-1], coming))
        total = total[:rows] + coming
        d //= 2
    theirs = partner(total[SUBS:])
    for left, a, b, name in jobs:
        left, total = lax.optimization_barrier((left, total))
        grads.append(weight_grad(t, left, a, b, name))
    grads, theirs = lax.optimization_barrier((grads, theirs))
    token_grad, gate_t = finish(e, ids_t, total[:SUBS], theirs, width)
    return token_grad, gate_t.T, *grads


def solution(mesh):
    return jax.shard_map(
        on_device,
        mesh=mesh,
        in_specs=(
            P(("groups", "expert"), "tensor"),
            P(("groups", "expert"), "tensor"),
            P(("groups", "expert"), None),
            P(("groups", "expert"), None),
            P(("expert", "tensor"), None),
            P(("expert", "tensor"), None),
            P(("expert", "tensor"), None),
        ),
        out_specs=(
            P(("groups", "expert"), "tensor"),
            P(("groups", "expert"), None),
            P(("expert", "tensor"), "groups"),
            P(("expert", "tensor"), "groups"),
            P(("expert", "tensor"), "groups"),
        ),
        check_vma=False,
    )
```

```python
import functools

import jax
import jax.numpy as jnp
from jax import lax
from jax.experimental import pallas as pl
from jax.experimental.pallas import tpu as pltpu
from jax.sharding import PartitionSpec as P

EXPERTS_ON = 2
CAP = 5
LANES = 128
SUBS = 8
WHOLE = 4
F32 = jnp.float32
BF16 = jnp.bfloat16
MIB = 1 << 20
VMEM = pl.BlockSpec(memory_space=pltpu.VMEM)
SMEM = pl.BlockSpec(memory_space=pltpu.SMEM)
HBM = pl.BlockSpec(memory_space=pltpu.HBM)


def iota(shape, dim):
    return lax.broadcasted_iota(jnp.int32, shape, dim)


def chosen_rows(ids, expert, position):
    rows, toks = position.shape
    hits = [ids[k : k + 1, :] == expert for k in range(ids.shape[0])]
    member = functools.reduce(jnp.logical_or, hits).astype(F32)
    before = (iota((toks, toks), 0) < iota((toks, toks), 1)).astype(F32)
    earlier = jnp.dot(member, before, preferred_element_type=F32)
    return jnp.where(earlier == position.astype(F32), member, 0.0), hits


def sub_row(rows, toks):
    return iota((rows, toks), 0) % SUBS


def tile_of(hidden, most):
    sizes = [n for n in range(16, most + 1, 16) if hidden % n == 0]
    return max(sizes) if sizes else hidden


def pick_body(e_ref, ids_ref, probs_ref, tok_ref, grad_ref, own_ref, oth_ref):
    ids = ids_ref[...]
    probs = probs_ref[...].astype(F32)
    toks, width = tok_ref.shape
    half, eighth = width // 2, width // SUBS
    size = half + eighth
    both = 2 * SUBS
    row = iota((both, toks), 0)
    sub = sub_row(both, toks)
    expert = jnp.where(row < SUBS, e_ref[0], 1 - e_ref[0])
    main, hits = chosen_rows(ids, expert, sub % WHOLE)
    tail, _ = chosen_rows(ids, expert, jnp.full((both, toks), WHOLE, jnp.int32))
    plain = jnp.where(sub < WHOLE, main, jnp.where(sub == WHOLE, tail, 0.0))
    halves = [jnp.where(sub // WHOLE == h, main, 0.0).astype(BF16) for h in range(2)]
    eighths = [jnp.where(sub == s, tail, 0.0).astype(BF16) for s in range(SUBS)]
    for at, src in enumerate((tok_ref, grad_ref)):
        packed = sum(
            jnp.dot(one, src[:, h * half : (h + 1) * half], preferred_element_type=F32)
            for h, one in enumerate(halves)
        ).astype(BF16)
        last = sum(
            jnp.dot(one, src[:, s * eighth : (s + 1) * eighth], preferred_element_type=F32)
            for s, one in enumerate(eighths)
        ).astype(BF16)
        for n, dst in enumerate((own_ref, oth_ref)):
            dst[:, at * size : at * size + half] = packed[n * SUBS : (n + 1) * SUBS]
            dst[:, at * size + half : (at + 1) * size] = last[n * SUBS : (n + 1) * SUBS]
    weight = sum(jnp.where(hit, probs[k : k + 1, :], 0.0) for k, hit in enumerate(hits))
    gate = jnp.broadcast_to(jnp.sum(plain * weight, axis=1, keepdims=True), (both, LANES)).astype(BF16)
    for n, dst in enumerate((own_ref, oth_ref)):
        dst[:, 2 * size :] = gate[n * SUBS : (n + 1) * SUBS]


def pick(e, ids_t, probs_t, tokens, grad_out):
    width = tokens.shape[1]
    size = width // 2 + width // SUBS
    piece = jax.ShapeDtypeStruct((SUBS, 2 * size + LANES), BF16)
    return pl.pallas_call(
        pick_body,
        out_shape=(piece, piece),
        in_specs=[SMEM] + [VMEM] * 4,
        out_specs=[VMEM] * 2,
        name="pick_rows",
    )(e, ids_t, probs_t, tokens, grad_out)


def assemble_body(count, *refs):
    pieces, (x_ref, g_ref, factor_ref, held) = refs[:count], refs[count:]
    width = x_ref.shape[1]
    half, eighth = width // 2, width // SUBS
    size = half + eighth
    held[...] = jnp.zeros_like(held)
    for side, out in enumerate((x_ref, g_ref)):
        base = side * size
        for n, ref in enumerate(pieces):
            at = n * SUBS
            piece = ref[:, base : base + size].astype(F32)
            for h in range(2):
                held[at : at + WHOLE, h * half : (h + 1) * half] = piece[h * WHOLE : (h + 1) * WHOLE, :half]
            for s in range(SUBS):
                held[at + WHOLE : at + WHOLE + 1, s * eighth : (s + 1) * eighth] = piece[s : s + 1, half:]
        out[...] = held[...].astype(BF16)
    for n, ref in enumerate(pieces):
        factor_ref[n * SUBS : (n + 1) * SUBS, :] = ref[:, 2 * size :].astype(F32)


def assemble(pieces, width):
    count = len(pieces)
    rows = count * SUBS
    held = jax.ShapeDtypeStruct((rows, width), BF16)
    return pl.pallas_call(
        functools.partial(assemble_body, count),
        out_shape=(held, held, jax.ShapeDtypeStruct((rows, LANES), F32)),
        in_specs=[VMEM] * count,
        out_specs=[VMEM] * 3,
        scratch_shapes=[pltpu.VMEM((rows, width), F32)],
        name="assemble_rows",
    )(*pieces)


NT = (((1,), (1,)), ((), ()))


def chunk_of(width, most):
    return max(n for n in range(LANES, most + 1, LANES) if width % n == 0)


def place_of(step, chunks, chunk, t):
    side = jnp.where(step < chunks, t, 1 - t)
    return pl.multiple_of((side * chunks + lax.rem(step, chunks)) * chunk, chunk)


def pack_rows(part, gates, out):
    rows, width = part.shape
    half, eighth = width // 2, width // SUBS
    for at in range(0, rows, SUBS):
        for h in range(2):
            out[at + h * WHOLE : at + (h + 1) * WHOLE, :half] = part[at : at + WHOLE, h * half : (h + 1) * half]
        for s in range(SUBS):
            out[at + s : at + s + 1, half : half + eighth] = part[
                at + WHOLE : at + WHOLE + 1, s * eighth : (s + 1) * eighth
            ]
    out[:, half + eighth :] = gates


def stream_body(chunk, t_ref, xa_ref, xb_ref, w_hbm, out_ref, held, landed):
    chunks = xa_ref.shape[1] // chunk
    t = t_ref[0]

    def load(i):
        cols = pl.ds(place_of(i, chunks, chunk, t), chunk)
        return pltpu.make_async_copy(w_hbm.at[:, cols], held.at[i], landed.at[i])

    for i in range(2 * chunks):
        load(i).start()
    for side, x_ref in enumerate((xa_ref, xb_ref)):

        def step(c, carry):
            i = side * chunks + c
            x = x_ref[:, pl.ds(pl.multiple_of(c * chunk, chunk), chunk)]
            load(i).wait()
            more = lax.dot_general(held[i], x, NT, preferred_element_type=F32)
            out_ref[...] = jnp.where(i == 0, more, out_ref[...] + more)
            return carry

        lax.fori_loop(0, chunks, step, 0)


def stream_units(t, xa, xb, w, name):
    hidden, depth = w.shape
    rows, width = xa.shape
    chunk = chunk_of(width, 1024)
    steps = depth // chunk
    return pl.pallas_call(
        functools.partial(stream_body, chunk),
        out_shape=jax.ShapeDtypeStruct((hidden, rows), F32),
        in_specs=[SMEM, VMEM, VMEM, HBM],
        out_specs=VMEM,
        scratch_shapes=[pltpu.VMEM((steps, hidden, chunk), BF16), pltpu.SemaphoreType.DMA((steps,))],
        compiler_params=pltpu.CompilerParams(vmem_limit_bytes=32 * MIB),
        cost_estimate=pl.CostEstimate(
            flops=2 * rows * hidden * depth, bytes_accessed=2 * hidden * depth, transcendentals=0
        ),
        name=name,
    )(t, xa, xb, w)


def rows_body(tile, t_ref, xa_ref, xb_ref, w_hbm, out_ref, held, x, landed):
    width = xa_ref.shape[1]
    steps = w_hbm.shape[0] // tile
    t = t_ref[0]

    def load(i):
        rows = pl.ds(pl.multiple_of(i * tile, tile), tile)
        return pltpu.make_async_copy(w_hbm.at[rows, :], held.at[i], landed.at[i])

    for i in range(steps):
        load(i).start()
    for at, ref in ((t, xa_ref), (1 - t, xb_ref)):
        x[:, pl.ds(pl.multiple_of(at * width, width), width)] = ref[...]

    def step(i, carry):
        rows = pl.ds(pl.multiple_of(i * tile, tile), tile)
        load(i).wait()
        out_ref[rows, :] = lax.dot_general(x[...], held[i], NT, preferred_element_type=F32).T
        return carry

    lax.fori_loop(0, steps, step, 0)


def row_units(t, xa, xb, w, name):
    hidden, depth = w.shape
    rows, width = xa.shape
    tile = tile_of(hidden, 256)
    steps = hidden // tile
    return pl.pallas_call(
        functools.partial(rows_body, tile),
        out_shape=jax.ShapeDtypeStruct((hidden, rows), F32),
        in_specs=[SMEM, VMEM, VMEM, HBM],
        out_specs=VMEM,
        scratch_shapes=[
            pltpu.VMEM((steps, tile, depth), BF16),
            pltpu.VMEM((rows, depth), BF16),
            pltpu.SemaphoreType.DMA((steps,)),
        ],
        compiler_params=pltpu.CompilerParams(vmem_limit_bytes=32 * MIB),
        cost_estimate=pl.CostEstimate(
            flops=2 * rows * hidden * depth, bytes_accessed=2 * hidden * depth, transcendentals=0
        ),
        name=name,
    )(t, xa, xb, w)


def half_loads(t, chunk, width, wg_hbm, wu_hbm, held, landed, own):
    base = pl.multiple_of((t if own else 1 - t) * width, width)

    def load(c, n):
        cols = pl.ds(base + pl.multiple_of(c * chunk, chunk), chunk)
        return pltpu.make_async_copy((wg_hbm, wu_hbm)[n].at[:, cols], held.at[c, n], landed.at[c, n])

    return load


def half_grad(part, load, held, dhr_ref, dur_ref, chunk):
    def step(c, carry):
        for n in range(2):
            load(c, n).wait()
        part[:, pl.ds(pl.multiple_of(c * chunk, chunk), chunk)] = jnp.dot(
            dhr_ref[...], held[c, 0], preferred_element_type=F32
        ) + jnp.dot(dur_ref[...], held[c, 1], preferred_element_type=F32)
        return carry

    lax.fori_loop(0, part.shape[1] // chunk, step, 0)


def give_body(chunk, small, t_ref, ga_ref, gb_ref, factor_ref, h_ref, u_ref, wg_hbm, wu_hbm, wd_hbm,
              wt_ref, dh_ref, du_ref, dhr_ref, dur_ref, gate_ref, give_ref,
              ring, held, da_ref, part, ring_landed, landed):
    rows, width = ga_ref.shape
    chunks = width // chunk
    depth = ring.shape[0]
    steps = 2 * chunks
    t = t_ref[0]

    def load_down(i):
        cols = pl.ds(place_of(i, chunks, chunk, t), chunk)
        slot = lax.rem(i, depth)
        return pltpu.make_async_copy(wd_hbm.at[:, cols], ring.at[slot], ring_landed.at[slot])

    load = half_loads(t, small, width, wg_hbm, wu_hbm, held, landed, False)
    for i in range(min(steps, depth)):
        load_down(i).start()
    for c in range(width // small):
        for n in range(2):
            load(c, n).start()

    for side, g_ref in enumerate((ga_ref, gb_ref)):

        def down_step(c, carry):
            i = side * chunks + c
            g = g_ref[:, pl.ds(pl.multiple_of(c * chunk, chunk), chunk)]
            load_down(i).wait()
            more = lax.dot_general(ring[lax.rem(i, depth)], g, NT, preferred_element_type=F32)
            da_ref[...] = jnp.where(i == 0, more, da_ref[...] + more)

            @pl.when(i + depth < steps)
            def _():
                load_down(i + depth).start()

            return carry

        lax.fori_loop(0, chunks, down_step, 0)

    weight = factor_ref[...].T[:1, :]
    h = h_ref[...]
    u = u_ref[...]
    da = da_ref[...]
    sigma = 1.0 / (1.0 + jnp.exp(-h))
    silu = h * sigma
    act = silu * u
    scaled = weight * da
    wt_ref[...] = (weight * act).astype(BF16)
    dh = scaled * u * sigma * (1.0 + h * (1.0 - sigma))
    du = scaled * silu
    dh_ref[...] = dh.astype(BF16)
    du_ref[...] = du.astype(BF16)
    dhr_ref[...] = dh.T.astype(BF16)
    dur_ref[...] = du.T.astype(BF16)
    total = jnp.sum(act * da, axis=0, keepdims=True)
    gate_ref[...] = jnp.broadcast_to(total, (LANES, rows)).T
    half_grad(part, load, held, dhr_ref, dur_ref, small)
    pack_rows(part, gate_ref[...], give_ref)


def give_half(t, ga, gb, factor, h, u, w_gate, w_up, w_down):
    hidden, depth = w_gate.shape
    rows, width = ga.shape
    chunk = chunk_of(width, 1024)
    small = chunk_of(width, 512)
    ring = min(4, depth // chunk)
    unit = jax.ShapeDtypeStruct((hidden, rows), BF16)
    turned = jax.ShapeDtypeStruct((rows, hidden), BF16)
    packed = jax.ShapeDtypeStruct((rows, width // 2 + width // SUBS + LANES), F32)
    return pl.pallas_call(
        functools.partial(give_body, chunk, small),
        out_shape=(unit, unit, unit, turned, turned, jax.ShapeDtypeStruct((rows, LANES), F32), packed),
        in_specs=[SMEM] + [VMEM] * 5 + [HBM] * 3,
        out_specs=[VMEM] * 7,
        scratch_shapes=[
            pltpu.VMEM((ring, hidden, chunk), BF16),
            pltpu.VMEM((width // small, 2, hidden, small), BF16),
            pltpu.VMEM((hidden, rows), F32),
            pltpu.VMEM((rows, width), F32),
            pltpu.SemaphoreType.DMA((ring,)),
            pltpu.SemaphoreType.DMA((width // small, 2)),
        ],
        compiler_params=pltpu.CompilerParams(vmem_limit_bytes=44 * MIB),
        cost_estimate=pl.CostEstimate(
            flops=4 * rows * hidden * depth, bytes_accessed=4 * hidden * depth, transcendentals=rows * hidden
        ),
        name="give_half",
    )(t, ga, gb, factor, h, u, w_gate, w_up, w_down)


def keep_body(small, t_ref, gate_ref, dhr_ref, dur_ref, wg_hbm, wu_hbm, keep_ref, held, part, landed):
    width = part.shape[1]
    load = half_loads(t_ref[0], small, width, wg_hbm, wu_hbm, held, landed, True)
    for c in range(width // small):
        for n in range(2):
            load(c, n).start()
    half_grad(part, load, held, dhr_ref, dur_ref, small)
    pack_rows(part, gate_ref[...], keep_ref)


def keep_half(t, gate, dhr, dur, w_gate, w_up, width):
    rows, hidden = dhr.shape
    small = chunk_of(width, 512)
    return pl.pallas_call(
        functools.partial(keep_body, small),
        out_shape=jax.ShapeDtypeStruct((rows, width // 2 + width // SUBS + LANES), F32),
        in_specs=[SMEM] + [VMEM] * 3 + [HBM] * 2,
        out_specs=VMEM,
        scratch_shapes=[
            pltpu.VMEM((width // small, 2, hidden, small), BF16),
            pltpu.VMEM((rows, width), F32),
            pltpu.SemaphoreType.DMA((width // small, 2)),
        ],
        compiler_params=pltpu.CompilerParams(vmem_limit_bytes=32 * MIB),
        cost_estimate=pl.CostEstimate(
            flops=4 * rows * hidden * width, bytes_accessed=4 * hidden * width, transcendentals=0
        ),
        name="keep_half",
    )(t, gate, dhr, dur, w_gate, w_up)


def column_body(chunk, tile, t_ref, left_ref, own_ref, oth_ref, out_ref, ring, sent):
    width = own_ref.shape[1]
    chunks = width // chunk
    depth = ring.shape[0]
    hidden = left_ref.shape[0]
    t = t_ref[0]

    def store(i):
        cols = pl.ds(place_of(i, chunks, chunk, t), chunk)
        slot = lax.rem(i, depth)
        return pltpu.make_async_copy(ring.at[slot], out_ref.at[:, cols], sent.at[slot])

    for side, x_ref in enumerate((own_ref, oth_ref)):

        def step(c, carry):
            i = side * chunks + c
            slot = lax.rem(i, depth)

            @pl.when(i >= depth)
            def _():
                store(i - depth).wait()

            x = x_ref[:, pl.ds(pl.multiple_of(c * chunk, chunk), chunk)]
            for at in range(0, hidden, tile):
                ring[slot, at : at + tile, :] = jnp.dot(
                    left_ref[at : at + tile, :], x, preferred_element_type=F32
                ).astype(BF16)
            store(i).start()
            return carry

        lax.fori_loop(0, chunks, step, 0)
    for i in range(max(0, 2 * chunks - depth), 2 * chunks):
        store(i).wait()


def weight_grad_columns(t, left, own, oth, name, most, tile):
    hidden, rows = left.shape
    width = own.shape[1]
    depth = 2 * width
    chunk = chunk_of(width, most)
    tile = tile_of(hidden, tile)
    ring = min(4, depth // chunk)
    return pl.pallas_call(
        functools.partial(column_body, chunk, tile),
        out_shape=jax.ShapeDtypeStruct((hidden, depth), BF16),
        in_specs=[SMEM] + [VMEM] * 3,
        out_specs=HBM,
        scratch_shapes=[pltpu.VMEM((ring, hidden, chunk), BF16), pltpu.SemaphoreType.DMA((ring,))],
        compiler_params=pltpu.CompilerParams(vmem_limit_bytes=24 * MIB),
        cost_estimate=pl.CostEstimate(
            flops=2 * rows * hidden * depth, bytes_accessed=2 * hidden * depth, transcendentals=0
        ),
        name=name,
    )(t, left, own, oth)


def tile_body(t_ref, left_ref, own_ref, oth_ref, out_ref, ring, sent):
    width = own_ref.shape[1]
    depth, tile, _ = ring.shape
    steps = left_ref.shape[0] // tile
    t = t_ref[0]

    def store(i):
        slot = lax.rem(i, depth)
        rows = pl.ds(pl.multiple_of(i * tile, tile), tile)
        return pltpu.make_async_copy(ring.at[slot], out_ref.at[rows, :], sent.at[slot])

    def step(i, carry):
        slot = lax.rem(i, depth)

        @pl.when(i >= depth)
        def _():
            store(i - depth).wait()

        left = left_ref[pl.ds(pl.multiple_of(i * tile, tile), tile), :]
        for at, ref in ((t, own_ref), (1 - t, oth_ref)):
            cols = pl.ds(pl.multiple_of(at * width, width), width)
            ring[slot, :, cols] = jnp.dot(left, ref[...], preferred_element_type=F32).astype(BF16)
        store(i).start()
        return carry

    lax.fori_loop(0, steps, step, 0)
    for i in range(max(0, steps - depth), steps):
        store(i).wait()


def weight_grad_tiles(t, left, own, oth, name):
    hidden, rows = left.shape
    width = own.shape[1]
    depth = 2 * width
    tile = tile_of(hidden, 256)
    ring = min(4, hidden // tile)
    return pl.pallas_call(
        tile_body,
        out_shape=jax.ShapeDtypeStruct((hidden, depth), BF16),
        in_specs=[SMEM] + [VMEM] * 3,
        out_specs=HBM,
        scratch_shapes=[pltpu.VMEM((ring, tile, depth), BF16), pltpu.SemaphoreType.DMA((ring,))],
        compiler_params=pltpu.CompilerParams(vmem_limit_bytes=24 * MIB),
        cost_estimate=pl.CostEstimate(
            flops=2 * rows * hidden * depth, bytes_accessed=2 * hidden * depth, transcendentals=0
        ),
        name=name,
    )(t, left, own, oth)


def finish_body(e_ref, ids_ref, mine_ref, got_ref, tok_ref, gate_ref):
    ids = ids_ref[...]
    toks, width = tok_ref.shape
    half, eighth = width // 2, width // SUBS
    both = 2 * SUBS
    row = iota((both, toks), 0)
    sub = sub_row(both, toks)
    expert = jnp.where(row < SUBS, e_ref[0], 1 - e_ref[0])
    main, hits = chosen_rows(ids, expert, sub % WHOLE)
    tail, _ = chosen_rows(ids, expert, jnp.full((both, toks), WHOLE, jnp.int32))
    plain = jnp.where(sub < WHOLE, main, jnp.where(sub == WHOLE, tail, 0.0))
    data = jnp.concatenate([mine_ref[...], got_ref[...]], axis=0)
    tn = (((0,), (0,)), ((), ()))
    exact = dict(precision=lax.Precision.HIGHEST, preferred_element_type=F32)
    halves = [
        lax.dot_general(jnp.where(sub // WHOLE == h, main, 0.0), data[:, :half], tn, **exact) for h in range(2)
    ]
    for s in range(SUBS):
        last = lax.dot_general(jnp.where(sub == s, tail, 0.0), data[:, half : half + eighth], tn, **exact)
        h, at = divmod(s * eighth, half)
        tok_ref[:, s * eighth : (s + 1) * eighth] = (halves[h][:, at : at + eighth] + last).astype(BF16)
    term = plain * data[:, half + eighth : half + eighth + 1]
    for k, hit in enumerate(hits):
        gate_ref[k : k + 1, :] = jnp.sum(jnp.where(hit, term, 0.0), axis=0, keepdims=True)


def finish(e, ids_t, mine, got, width):
    top, toks = ids_t.shape
    return pl.pallas_call(
        finish_body,
        out_shape=(jax.ShapeDtypeStruct((toks, width), BF16), jax.ShapeDtypeStruct((top, toks), F32)),
        in_specs=[SMEM] + [VMEM] * 3,
        out_specs=[VMEM] * 2,
        name="finish_tokens",
    )(e, ids_t, mine, got)


def on_device(tokens, grad_out, expert_ids, gate_probs, w_gate, w_up, w_down):
    n_expert = lax.axis_size("expert")
    copies = n_expert // EXPERTS_ON
    place = lax.axis_index("expert")
    e = (place >= copies).astype(jnp.int32).reshape(1)
    t = lax.axis_index("tensor").astype(jnp.int32).reshape(1)
    width = tokens.shape[1]

    def partner(v):
        return lax.ppermute(v, "expert", [(i, (i + copies) % n_expert) for i in range(n_expert)])

    def across(v, d):
        return lax.ppermute(v, "expert", [(i, i ^ d) for i in range(n_expert)])

    def other_core(v):
        return lax.ppermute(v, "tensor", [(0, 1), (1, 0)])

    w_gate, w_up, w_down = (pltpu.with_memory_space_constraint(w, pltpu.HBM) for w in (w_gate, w_up, w_down))
    ids_t = expert_ids.T
    own, oth = pick(e, ids_t, gate_probs.T, tokens, grad_out)
    first, second = [own], [partner(oth)]
    d = 1
    while d < copies:
        first += [across(piece, d) for piece in first]
        second += [across(piece, d) for piece in second]
        d *= 2
    xa, ga, factor = assemble([piece for pair in zip(first, second) for piece in pair], width)
    xb = other_core(xa)
    gb = other_core(ga)
    h = stream_units(t, xa, xb, w_gate, "gate_units")
    u = row_units(t, xa, xb, w_up, "up_units")
    wt, dh, du, dhr, dur, gate, give = give_half(t, ga, gb, factor, h, u, w_gate, w_up, w_down)
    got = other_core(give)
    keep = keep_half(t, gate, dhr, dur, w_gate, w_up, width)
    keep, got = lax.optimization_barrier((keep, got))
    total = keep + got
    grads = []
    forms = (
        functools.partial(weight_grad_tiles, name="grad_w_gate"),
        functools.partial(weight_grad_columns, name="grad_w_up", most=512, tile=1344),
        functools.partial(weight_grad_columns, name="grad_w_down", most=1024, tile=448),
    )
    jobs = [(dh, xa, xb, forms[0]), (du, xa, xb, forms[1]), (wt, ga, gb, forms[2])]
    d = copies // 2
    while d:
        rows = d * 2 * SUBS
        coming = across(total[rows:], d)
        if len(jobs) > 1:
            left, a, b, job = jobs.pop(0)
            left, total = lax.optimization_barrier((left, total))
            grads.append(job(t, left, a, b))
            grads[-1], coming = lax.optimization_barrier((grads[-1], coming))
        total = total[:rows] + coming
        d //= 2
    theirs = partner(total[SUBS:])
    for left, a, b, job in jobs:
        left, total = lax.optimization_barrier((left, total))
        grads.append(job(t, left, a, b))
    grads, theirs = lax.optimization_barrier((grads, theirs))
    token_grad, gate_t = finish(e, ids_t, total[:SUBS], theirs, width)
    return token_grad, gate_t.T, *grads


def solution(mesh):
    return jax.shard_map(
        on_device,
        mesh=mesh,
        in_specs=(
            P(("groups", "expert"), "tensor"),
            P(("groups", "expert"), "tensor"),
            P(("groups", "expert"), None),
            P(("groups", "expert"), None),
            P(("expert", "tensor"), None),
            P(("expert", "tensor"), None),
            P(("expert", "tensor"), None),
        ),
        out_specs=(
            P(("groups", "expert"), "tensor"),
            P(("groups", "expert"), None),
            P(("expert", "tensor"), "groups"),
            P(("expert", "tensor"), "groups"),
            P(("expert", "tensor"), "groups"),
        ),
        check_vma=False,
    )
```

```python
import functools

import jax
import jax.numpy as jnp
from jax import lax
from jax.experimental import pallas as pl
from jax.experimental.pallas import tpu as pltpu
from jax.sharding import PartitionSpec as P

EXPERTS_ON = 2
CAP = 5
LANES = 128
SUBS = 8
WHOLE = 4
F32 = jnp.float32
BF16 = jnp.bfloat16
MIB = 1 << 20
VMEM = pl.BlockSpec(memory_space=pltpu.VMEM)
SMEM = pl.BlockSpec(memory_space=pltpu.SMEM)
HBM = pl.BlockSpec(memory_space=pltpu.HBM)


def iota(shape, dim):
    return lax.broadcasted_iota(jnp.int32, shape, dim)


def chosen_rows(ids, expert, position):
    rows, toks = position.shape
    hits = [ids[k : k + 1, :] == expert for k in range(ids.shape[0])]
    member = functools.reduce(jnp.logical_or, hits).astype(F32)
    before = (iota((toks, toks), 0) < iota((toks, toks), 1)).astype(F32)
    earlier = jnp.dot(member, before, preferred_element_type=F32)
    return jnp.where(earlier == position.astype(F32), member, 0.0), hits


def sub_row(rows, toks):
    return iota((rows, toks), 0) % SUBS


def tile_of(hidden, most):
    sizes = [n for n in range(16, most + 1, 16) if hidden % n == 0]
    return max(sizes) if sizes else hidden


def pick_body(e_ref, ids_ref, probs_ref, tok_ref, grad_ref, own_ref, oth_ref):
    ids = ids_ref[...]
    probs = probs_ref[...].astype(F32)
    toks, width = tok_ref.shape
    half, eighth = width // 2, width // SUBS
    size = half + eighth
    both = 2 * SUBS
    row = iota((both, toks), 0)
    sub = sub_row(both, toks)
    expert = jnp.where(row < SUBS, e_ref[0], 1 - e_ref[0])
    main, hits = chosen_rows(ids, expert, sub % WHOLE)
    tail, _ = chosen_rows(ids, expert, jnp.full((both, toks), WHOLE, jnp.int32))
    plain = jnp.where(sub < WHOLE, main, jnp.where(sub == WHOLE, tail, 0.0))
    halves = [jnp.where(sub // WHOLE == h, main, 0.0).astype(BF16) for h in range(2)]
    eighths = [jnp.where(sub == s, tail, 0.0).astype(BF16) for s in range(SUBS)]
    for at, src in enumerate((tok_ref, grad_ref)):
        packed = sum(
            jnp.dot(one, src[:, h * half : (h + 1) * half], preferred_element_type=F32)
            for h, one in enumerate(halves)
        ).astype(BF16)
        last = sum(
            jnp.dot(one, src[:, s * eighth : (s + 1) * eighth], preferred_element_type=F32)
            for s, one in enumerate(eighths)
        ).astype(BF16)
        for n, dst in enumerate((own_ref, oth_ref)):
            dst[:, at * size : at * size + half] = packed[n * SUBS : (n + 1) * SUBS]
            dst[:, at * size + half : (at + 1) * size] = last[n * SUBS : (n + 1) * SUBS]
    weight = sum(jnp.where(hit, probs[k : k + 1, :], 0.0) for k, hit in enumerate(hits))
    gate = jnp.broadcast_to(jnp.sum(plain * weight, axis=1, keepdims=True), (both, LANES)).astype(BF16)
    for n, dst in enumerate((own_ref, oth_ref)):
        dst[:, 2 * size :] = gate[n * SUBS : (n + 1) * SUBS]


def pick(e, ids_t, probs_t, tokens, grad_out):
    width = tokens.shape[1]
    size = width // 2 + width // SUBS
    piece = jax.ShapeDtypeStruct((SUBS, 2 * size + LANES), BF16)
    return pl.pallas_call(
        pick_body,
        out_shape=(piece, piece),
        in_specs=[SMEM] + [VMEM] * 4,
        out_specs=[VMEM] * 2,
        name="pick_rows",
    )(e, ids_t, probs_t, tokens, grad_out)


def assemble_body(count, *refs):
    pieces, (x_ref, g_ref, factor_ref, held) = refs[:count], refs[count:]
    width = x_ref.shape[1]
    half, eighth = width // 2, width // SUBS
    size = half + eighth
    held[...] = jnp.zeros_like(held)
    for side, out in enumerate((x_ref, g_ref)):
        base = side * size
        for n, ref in enumerate(pieces):
            at = n * SUBS
            piece = ref[:, base : base + size].astype(F32)
            for h in range(2):
                held[at : at + WHOLE, h * half : (h + 1) * half] = piece[h * WHOLE : (h + 1) * WHOLE, :half]
            for s in range(SUBS):
                held[at + WHOLE : at + WHOLE + 1, s * eighth : (s + 1) * eighth] = piece[s : s + 1, half:]
        out[...] = held[...].astype(BF16)
    for n, ref in enumerate(pieces):
        factor_ref[n * SUBS : (n + 1) * SUBS, :] = ref[:, 2 * size :].astype(F32)


def assemble(pieces, width):
    count = len(pieces)
    rows = count * SUBS
    held = jax.ShapeDtypeStruct((rows, width), BF16)
    return pl.pallas_call(
        functools.partial(assemble_body, count),
        out_shape=(held, held, jax.ShapeDtypeStruct((rows, LANES), F32)),
        in_specs=[VMEM] * count,
        out_specs=[VMEM] * 3,
        scratch_shapes=[pltpu.VMEM((rows, width), F32)],
        compiler_params=pltpu.CompilerParams(vmem_limit_bytes=6 * MIB),
        name="assemble_rows",
    )(*pieces)


NT = (((1,), (1,)), ((), ()))


def chunk_of(width, most):
    return max(n for n in range(LANES, most + 1, LANES) if width % n == 0)


def place_of(step, chunks, chunk, t):
    side = jnp.where(step < chunks, t, 1 - t)
    return pl.multiple_of((side * chunks + lax.rem(step, chunks)) * chunk, chunk)


def half_grad(part, wg_ref, wu_ref, dhr_ref, dur_ref, base, chunk):
    def step(c, carry):
        at = pl.multiple_of(c * chunk, chunk)
        cols = pl.ds(base + at, chunk)
        part[:, pl.ds(at, chunk)] = jnp.dot(dhr_ref[...], wg_ref[:, cols], preferred_element_type=F32) + jnp.dot(
            dur_ref[...], wu_ref[:, cols], preferred_element_type=F32
        )
        return carry

    lax.fori_loop(0, part.shape[1] // chunk, step, 0)


def pack_rows(part, gates, out):
    rows, width = part.shape
    half, eighth = width // 2, width // SUBS
    for at in range(0, rows, SUBS):
        for h in range(2):
            out[at + h * WHOLE : at + (h + 1) * WHOLE, :half] = part[at : at + WHOLE, h * half : (h + 1) * half]
        for s in range(SUBS):
            out[at + s : at + s + 1, half : half + eighth] = part[
                at + WHOLE : at + WHOLE + 1, s * eighth : (s + 1) * eighth
            ]
    out[:, half + eighth :] = gates


def experts_body(chunk, t_ref, xa_ref, xb_ref, ga_ref, gb_ref, factor_ref, wg_hbm, wu_hbm, wd_hbm,
                 wt_ref, dh_ref, du_ref, give_ref, keep_ref,
                 wg_ref, wu_ref, ring, h_ref, u_ref, da_ref, dhr_ref, dur_ref, part, landed, ring_landed):
    rows, width = xa_ref.shape
    chunks = width // chunk
    depth = ring.shape[0]
    steps = 2 * chunks
    t = t_ref[0]

    def load(i, n):
        cols = pl.ds(place_of(i, chunks, chunk, t), chunk)
        src, dst = ((wg_hbm, wg_ref), (wu_hbm, wu_ref))[n]
        return pltpu.make_async_copy(src.at[:, cols], dst.at[:, cols], landed.at[i, n])

    def load_down(i):
        cols = pl.ds(place_of(i, chunks, chunk, t), chunk)
        slot = lax.rem(i, depth)
        return pltpu.make_async_copy(wd_hbm.at[:, cols], ring.at[slot], ring_landed.at[slot])

    for i in range(steps):
        for n in range(2):
            load(i, n).start()
    for i in range(min(steps, depth)):
        load_down(i).start()

    def add_to(out, i, w, x):
        more = lax.dot_general(w, x, NT, preferred_element_type=F32)
        out[...] = jnp.where(i == 0, more, out[...] + more)

    for side, x_ref in enumerate((xa_ref, xb_ref)):

        def up_step(c, carry):
            i = side * chunks + c
            x = x_ref[:, pl.ds(pl.multiple_of(c * chunk, chunk), chunk)]
            cols = pl.ds(place_of(i, chunks, chunk, t), chunk)
            for n, (w, out) in enumerate(((wg_ref, h_ref), (wu_ref, u_ref))):
                load(i, n).wait()
                add_to(out, i, w[:, cols], x)
            return carry

        lax.fori_loop(0, chunks, up_step, 0)

    for side, g_ref in enumerate((ga_ref, gb_ref)):

        def down_step(c, carry):
            i = side * chunks + c
            g = g_ref[:, pl.ds(pl.multiple_of(c * chunk, chunk), chunk)]
            load_down(i).wait()
            add_to(da_ref, i, ring[lax.rem(i, depth)], g)

            @pl.when(i + depth < steps)
            def _():
                load_down(i + depth).start()

            return carry

        lax.fori_loop(0, chunks, down_step, 0)

    weight = factor_ref[...].T[:1, :]

    def units(start, size, total):
        at = pl.ds(start, size)
        h = h_ref[at, :]
        u = u_ref[at, :]
        da = da_ref[at, :]
        sigma = 1.0 / (1.0 + jnp.exp(-h))
        silu = h * sigma
        act = silu * u
        scaled = weight * da
        wt_ref[at, :] = (weight * act).astype(BF16)
        dh = scaled * u * sigma * (1.0 + h * (1.0 - sigma))
        du = scaled * silu
        dh_ref[at, :] = dh.astype(BF16)
        du_ref[at, :] = du.astype(BF16)
        dhr_ref[:, at] = dh.T.astype(BF16)
        dur_ref[:, at] = du.T.astype(BF16)
        return total + jnp.sum(act * da, axis=0, keepdims=True)

    hidden = h_ref.shape[0]
    whole = hidden // LANES
    total = lax.fori_loop(
        0, whole, lambda i, v: units(pl.multiple_of(i * LANES, LANES), LANES, v), jnp.zeros((1, rows), F32)
    )
    if hidden % LANES:
        total = units(whole * LANES, hidden % LANES, total)
    gates = jnp.broadcast_to(total, (LANES, rows)).T
    for at, out in ((1 - t, give_ref), (t, keep_ref)):
        base = pl.multiple_of(at * width, width)
        half_grad(part, wg_ref, wu_ref, dhr_ref, dur_ref, base, chunk_of(width, 512))
        pack_rows(part, gates, out)


def expert_units(t, xa, xb, ga, gb, factor, w_gate, w_up, w_down):
    hidden, depth = w_gate.shape
    rows, width = xa.shape
    chunk = chunk_of(width, 1024)
    steps = depth // chunk
    ring = min(3, steps)
    unit = jax.ShapeDtypeStruct((hidden, rows), BF16)
    packed = jax.ShapeDtypeStruct((rows, width // 2 + width // SUBS + LANES), F32)
    return pl.pallas_call(
        functools.partial(experts_body, chunk),
        out_shape=(unit, unit, unit, packed, packed),
        in_specs=[SMEM] + [VMEM] * 5 + [HBM] * 3,
        out_specs=[VMEM] * 5,
        scratch_shapes=[
            pltpu.VMEM((hidden, depth), BF16),
            pltpu.VMEM((hidden, depth), BF16),
            pltpu.VMEM((ring, hidden, chunk), BF16),
            pltpu.VMEM((hidden, rows), F32),
            pltpu.VMEM((hidden, rows), F32),
            pltpu.VMEM((hidden, rows), F32),
            pltpu.VMEM((rows, hidden), BF16),
            pltpu.VMEM((rows, hidden), BF16),
            pltpu.VMEM((rows, width), F32),
            pltpu.SemaphoreType.DMA((steps, 2)),
            pltpu.SemaphoreType.DMA((ring,)),
        ],
        compiler_params=pltpu.CompilerParams(vmem_limit_bytes=48 * MIB),
        cost_estimate=pl.CostEstimate(
            flops=10 * rows * hidden * depth, bytes_accessed=6 * hidden * depth, transcendentals=rows * hidden
        ),
        name="expert_units",
    )(t, xa, xb, ga, gb, factor, w_gate, w_up, w_down)


def weights_body(count, chunk, t_ref, *refs):
    lefts, (own_ref, oth_ref), outs = refs[:count], refs[count : count + 2], refs[count + 2 : 2 * count + 2]
    ring, sent = refs[2 * count + 2 :]
    width = own_ref.shape[1]
    chunks = width // chunk
    depth = ring.shape[1]
    hidden = lefts[0].shape[0]
    tile = tile_of(hidden, 448)
    t = t_ref[0]

    def store(i, n):
        cols = pl.ds(place_of(i, chunks, chunk, t), chunk)
        slot = lax.rem(i, depth)
        return pltpu.make_async_copy(ring.at[n, slot], outs[n].at[:, cols], sent.at[n, slot])

    for side, x_ref in enumerate((own_ref, oth_ref)):

        def step(c, carry):
            i = side * chunks + c
            slot = lax.rem(i, depth)
            x = x_ref[:, pl.ds(pl.multiple_of(c * chunk, chunk), chunk)]
            for n in range(count):

                @pl.when(i >= depth)
                def _():
                    store(i - depth, n).wait()

                for at in range(0, hidden, tile):
                    ring[n, slot, at : at + tile, :] = jnp.dot(
                        lefts[n][at : at + tile, :], x, preferred_element_type=F32
                    ).astype(BF16)
                store(i, n).start()
            return carry

        lax.fori_loop(0, chunks, step, 0)
    for i in range(max(0, 2 * chunks - depth), 2 * chunks):
        for n in range(count):
            store(i, n).wait()


def weight_grads(t, lefts, own, oth, name):
    count = len(lefts)
    hidden, rows = lefts[0].shape
    width = own.shape[1]
    depth = 2 * width
    chunk = chunk_of(width, 512)
    ring = min(4, depth // chunk)
    return pl.pallas_call(
        functools.partial(weights_body, count, chunk),
        out_shape=[jax.ShapeDtypeStruct((hidden, depth), BF16)] * count,
        in_specs=[SMEM] + [VMEM] * (count + 2),
        out_specs=[HBM] * count,
        scratch_shapes=[pltpu.VMEM((count, ring, hidden, chunk), BF16), pltpu.SemaphoreType.DMA((count, ring))],
        compiler_params=pltpu.CompilerParams(vmem_limit_bytes=24 * MIB),
        cost_estimate=pl.CostEstimate(
            flops=2 * count * rows * hidden * depth, bytes_accessed=2 * count * hidden * depth, transcendentals=0
        ),
        name=name,
    )(t, *lefts, own, oth)


def fold_body(copies, keep_ref, got_ref, *outs):
    for d, out in enumerate(outs):
        rows = slice(d * 2 * SUBS, (d + 1) * 2 * SUBS)
        out[...] = keep_ref[rows, :] + got_ref[rows, :]


def fold(copies, keep, got):
    return pl.pallas_call(
        functools.partial(fold_body, copies),
        out_shape=[jax.ShapeDtypeStruct((2 * SUBS, keep.shape[1]), F32)] * copies,
        in_specs=[VMEM] * 2,
        out_specs=[VMEM] * copies,
        compiler_params=pltpu.CompilerParams(vmem_limit_bytes=6 * MIB),
        name="fold_cores",
    )(keep, got)


def merge_body(*refs):
    blocks, (mine_ref, other_ref) = refs[:-2], refs[-2:]
    for at, out in ((0, mine_ref), (SUBS, other_ref)):
        total = blocks[0][at : at + SUBS, :]
        for block in blocks[1:]:
            total += block[at : at + SUBS, :]
        out[...] = total


def merge(blocks):
    part = jax.ShapeDtypeStruct((SUBS, blocks[0].shape[1]), F32)
    return pl.pallas_call(
        merge_body,
        out_shape=(part, part),
        in_specs=[VMEM] * len(blocks),
        out_specs=[VMEM] * 2,
        compiler_params=pltpu.CompilerParams(vmem_limit_bytes=6 * MIB),
        name="merge_chips",
    )(*blocks)


def finish_body(e_ref, ids_ref, mine_ref, got_ref, tok_ref, gate_ref):
    ids = ids_ref[...]
    toks, width = tok_ref.shape
    half, eighth = width // 2, width // SUBS
    both = 2 * SUBS
    row = iota((both, toks), 0)
    sub = sub_row(both, toks)
    expert = jnp.where(row < SUBS, e_ref[0], 1 - e_ref[0])
    main, hits = chosen_rows(ids, expert, sub % WHOLE)
    tail, _ = chosen_rows(ids, expert, jnp.full((both, toks), WHOLE, jnp.int32))
    plain = jnp.where(sub < WHOLE, main, jnp.where(sub == WHOLE, tail, 0.0))
    data = jnp.concatenate([mine_ref[...], got_ref[...]], axis=0)
    tn = (((0,), (0,)), ((), ()))
    exact = dict(precision=lax.Precision.HIGHEST, preferred_element_type=F32)
    halves = [
        lax.dot_general(jnp.where(sub // WHOLE == h, main, 0.0), data[:, :half], tn, **exact) for h in range(2)
    ]
    for s in range(SUBS):
        last = lax.dot_general(jnp.where(sub == s, tail, 0.0), data[:, half : half + eighth], tn, **exact)
        h, at = divmod(s * eighth, half)
        tok_ref[:, s * eighth : (s + 1) * eighth] = (halves[h][:, at : at + eighth] + last).astype(BF16)
    term = plain * data[:, half + eighth : half + eighth + 1]
    for k, hit in enumerate(hits):
        gate_ref[k : k + 1, :] = jnp.sum(jnp.where(hit, term, 0.0), axis=0, keepdims=True)


def finish(e, ids_t, mine, got, width):
    top, toks = ids_t.shape
    return pl.pallas_call(
        finish_body,
        out_shape=(jax.ShapeDtypeStruct((toks, width), BF16), jax.ShapeDtypeStruct((top, toks), F32)),
        in_specs=[SMEM] + [VMEM] * 3,
        out_specs=[VMEM] * 2,
        compiler_params=pltpu.CompilerParams(vmem_limit_bytes=6 * MIB),
        name="finish_tokens",
    )(e, ids_t, mine, got)


def on_device(tokens, grad_out, expert_ids, gate_probs, w_gate, w_up, w_down):
    n_expert = lax.axis_size("expert")
    copies = n_expert // EXPERTS_ON
    place = lax.axis_index("expert")
    e = (place >= copies).astype(jnp.int32).reshape(1)
    t = lax.axis_index("tensor").astype(jnp.int32).reshape(1)
    width = tokens.shape[1]

    def partner(v):
        return lax.ppermute(v, "expert", [(i, (i + copies) % n_expert) for i in range(n_expert)])

    def across(v, d):
        return lax.ppermute(v, "expert", [(i, i ^ d) for i in range(n_expert)])

    def other_core(v):
        return lax.ppermute(v, "tensor", [(0, 1), (1, 0)])

    w_gate, w_up, w_down = (pltpu.with_memory_space_constraint(w, pltpu.HBM) for w in (w_gate, w_up, w_down))
    ids_t = expert_ids.T
    own, oth = pick(e, ids_t, gate_probs.T, tokens, grad_out)
    far_first = sorted(range(1, copies), key=lambda d: (-d.bit_count(), d))
    got = partner(oth)
    first = {0: own} | {d: across(own, d) for d in far_first}
    second = {0: got} | {d: across(got, d) for d in far_first}
    xa, ga, factor = assemble([piece for d in range(copies) for piece in (first[d], second[d])], width)
    xb = other_core(xa)
    gb = other_core(ga)
    wt, dh, du, give, keep = expert_units(t, xa, xb, ga, gb, factor, w_gate, w_up, w_down)
    blocks = list(fold(copies, keep, other_core(give)))
    arrived = {d: across(blocks[d], d) for d in far_first}
    dh, mine = lax.optimization_barrier((dh, blocks[0]))
    grads = weight_grads(t, (dh, du), xa, xb, "grads_gate_up")
    grads, arrived = lax.optimization_barrier((grads, arrived))
    mine, others = merge([mine] + [arrived[d] for d in range(1, copies)])
    theirs = partner(others)
    wt, mine = lax.optimization_barrier((wt, mine))
    grads = [*grads, *weight_grads(t, (wt,), ga, gb, "grad_down")]
    grads, theirs = lax.optimization_barrier((grads, theirs))
    token_grad, gate_t = finish(e, ids_t, mine, theirs, width)
    return token_grad, gate_t.T, *grads


def solution(mesh):
    return jax.shard_map(
        on_device,
        mesh=mesh,
        in_specs=(
            P(("groups", "expert"), "tensor"),
            P(("groups", "expert"), "tensor"),
            P(("groups", "expert"), None),
            P(("groups", "expert"), None),
            P(("expert", "tensor"), None),
            P(("expert", "tensor"), None),
            P(("expert", "tensor"), None),
        ),
        out_specs=(
            P(("groups", "expert"), "tensor"),
            P(("groups", "expert"), None),
            P(("expert", "tensor"), "groups"),
            P(("expert", "tensor"), "groups"),
            P(("expert", "tensor"), "groups"),
        ),
        check_vma=False,
    )
```

```python
import functools

import jax
import jax.numpy as jnp
from jax import lax
from jax.experimental import pallas as pl
from jax.experimental.pallas import tpu as pltpu
from jax.sharding import PartitionSpec as P

EXPERTS_ON = 2
CAP = 5
LANES = 128
SUBS = 8
WHOLE = 4
F32 = jnp.float32
BF16 = jnp.bfloat16
MIB = 1 << 20
VMEM = pl.BlockSpec(memory_space=pltpu.VMEM)
SMEM = pl.BlockSpec(memory_space=pltpu.SMEM)
HBM = pl.BlockSpec(memory_space=pltpu.HBM)


def iota(shape, dim):
    return lax.broadcasted_iota(jnp.int32, shape, dim)


def chosen_rows(ids, expert, position):
    rows, toks = position.shape
    hits = [ids[k : k + 1, :] == expert for k in range(ids.shape[0])]
    member = functools.reduce(jnp.logical_or, hits).astype(F32)
    before = (iota((toks, toks), 0) < iota((toks, toks), 1)).astype(F32)
    earlier = jnp.dot(member, before, preferred_element_type=F32)
    return jnp.where(earlier == position.astype(F32), member, 0.0), hits


def sub_row(rows, toks):
    return iota((rows, toks), 0) % SUBS


def tile_of(hidden, most):
    sizes = [n for n in range(16, most + 1, 16) if hidden % n == 0]
    return max(sizes) if sizes else hidden


def pick_body(e_ref, ids_any, probs_any, tok_any, grad_any, own_ref, oth_ref, ids_ref, probs_ref, tok_ref, grad_ref, landed):
    copies = [
        pltpu.make_async_copy(src, dst, landed.at[n])
        for n, (src, dst) in enumerate(
            ((ids_any, ids_ref), (probs_any, probs_ref), (tok_any, tok_ref), (grad_any, grad_ref))
        )
    ]
    for copy in copies:
        copy.start()
    for copy in copies[:2]:
        copy.wait()
    ids = ids_ref[...]
    probs = probs_ref[...].astype(F32)
    toks, width = tok_ref.shape
    half, eighth = width // 2, width // SUBS
    size = half + eighth
    both = 2 * SUBS
    row = iota((both, toks), 0)
    sub = sub_row(both, toks)
    expert = jnp.where(row < SUBS, e_ref[0], 1 - e_ref[0])
    main, hits = chosen_rows(ids, expert, sub % WHOLE)
    tail, _ = chosen_rows(ids, expert, jnp.full((both, toks), WHOLE, jnp.int32))
    plain = jnp.where(sub < WHOLE, main, jnp.where(sub == WHOLE, tail, 0.0))
    halves = [jnp.where(sub // WHOLE == h, main, 0.0).astype(BF16) for h in range(2)]
    eighths = [jnp.where(sub == s, tail, 0.0).astype(BF16) for s in range(SUBS)]
    for at, src in enumerate((tok_ref, grad_ref)):
        copies[2 + at].wait()
        packed = sum(
            jnp.dot(one, src[:, h * half : (h + 1) * half], preferred_element_type=F32)
            for h, one in enumerate(halves)
        ).astype(BF16)
        last = sum(
            jnp.dot(one, src[:, s * eighth : (s + 1) * eighth], preferred_element_type=F32)
            for s, one in enumerate(eighths)
        ).astype(BF16)
        for n, dst in enumerate((own_ref, oth_ref)):
            dst[:, at * size : at * size + half] = packed[n * SUBS : (n + 1) * SUBS]
            dst[:, at * size + half : (at + 1) * size] = last[n * SUBS : (n + 1) * SUBS]
    weight = sum(jnp.where(hit, probs[k : k + 1, :], 0.0) for k, hit in enumerate(hits))
    gate = jnp.broadcast_to(jnp.sum(plain * weight, axis=1, keepdims=True), (both, LANES)).astype(BF16)
    for n, dst in enumerate((own_ref, oth_ref)):
        dst[:, 2 * size :] = gate[n * SUBS : (n + 1) * SUBS]


def pick(e, ids_t, probs_t, tokens, grad_out):
    width = tokens.shape[1]
    size = width // 2 + width // SUBS
    piece = jax.ShapeDtypeStruct((SUBS, 2 * size + LANES), BF16)
    return pl.pallas_call(
        pick_body,
        out_shape=(piece, piece),
        in_specs=[SMEM] + [HBM] * 4,
        out_specs=[VMEM] * 2,
        scratch_shapes=[pltpu.VMEM(v.shape, v.dtype) for v in (ids_t, probs_t, tokens, grad_out)]
        + [pltpu.SemaphoreType.DMA((4,))],
        compiler_params=pltpu.CompilerParams(vmem_limit_bytes=6 * MIB),
        name="pick_rows",
    )(e, ids_t, probs_t, tokens, grad_out)


NT = (((1,), (1,)), ((), ()))


def chunk_of(width, most):
    return max(n for n in range(LANES, most + 1, LANES) if width % n == 0)


def assemble(pieces, held, out, base, side):
    width = held.shape[1]
    half, eighth = width // 2, width // SUBS
    size = half + eighth
    for n, ref in enumerate(pieces):
        at = n * CAP
        piece = ref[:, side * size : (side + 1) * size].astype(F32)
        for h in range(2):
            held[at : at + WHOLE, h * half : (h + 1) * half] = piece[h * WHOLE : (h + 1) * WHOLE, :half]
        for s in range(SUBS):
            held[at + WHOLE : at + CAP, s * eighth : (s + 1) * eighth] = piece[s : s + 1, half:]
    out[:, pl.ds(base, width)] = held[...].astype(BF16)


def pack(part, gates, out, pieces):
    width = part.shape[1]
    half, eighth = width // 2, width // SUBS
    size = half + eighth
    for n in range(pieces):
        at, to = n * CAP, n * SUBS
        for h in range(2):
            out[to + h * WHOLE : to + (h + 1) * WHOLE, :half] = part[at : at + WHOLE, h * half : (h + 1) * half]
        for s in range(SUBS):
            out[to + s : to + s + 1, half:size] = part[at + WHOLE : at + CAP, s * eighth : (s + 1) * eighth]
        out[to : to + CAP, size:] = gates[at : at + CAP, :]
        out[to + CAP : to + SUBS, size:] = jnp.zeros((SUBS - CAP, LANES), F32)


def experts_body(pieces, t_ref, *refs):
    mine, theirs = refs[:pieces], refs[pieces : 2 * pieces]
    (wg_hbm, wu_hbm, wd_hbm, x_ref, g_ref, wt_ref, dh_ref, du_ref, give_ref, keep_ref,
     ring, held, acc, factor, gates, landed) = refs[2 * pieces :]
    rows, depth = x_ref.shape
    width = depth // 2
    slots, _, tile, _ = ring.shape
    steps = wg_hbm.shape[0] // tile
    t = t_ref[0]

    def load(i, n):
        at = pl.ds(pl.multiple_of(i * tile, tile), tile)
        slot = lax.rem(i, slots)
        return pltpu.make_async_copy((wg_hbm, wu_hbm, wd_hbm)[n].at[at, :], ring.at[slot, n], landed.at[slot, n])

    for i in range(min(steps, slots)):
        for n in range(3):
            load(i, n).start()

    held[...] = jnp.zeros_like(held)
    factor[...] = jnp.zeros_like(factor)
    for n, ref in enumerate(mine):
        factor[n * CAP : (n + 1) * CAP, :] = ref[:CAP, ref.shape[1] - LANES :].astype(F32)
    for group, at in ((mine, t), (theirs, 1 - t)):
        base = pl.multiple_of(at * width, width)
        for side, out in enumerate((x_ref, g_ref)):
            assemble(group, held, out, base, side)
    acc[...] = jnp.zeros_like(acc)
    gates[...] = jnp.zeros_like(gates)

    def step(i, carry):
        slot = lax.rem(i, slots)
        at = pl.ds(pl.multiple_of(i * tile, tile), tile)
        load(i, 0).wait()
        hidden = lax.dot_general(x_ref[...], ring[slot, 0], NT, preferred_element_type=F32)
        load(i, 1).wait()
        upper = lax.dot_general(x_ref[...], ring[slot, 1], NT, preferred_element_type=F32)
        load(i, 2).wait()
        dact = lax.dot_general(g_ref[...], ring[slot, 2], NT, preferred_element_type=F32)
        weight = factor[:, :1]
        sigma = 1.0 / (1.0 + jnp.exp(-hidden))
        silu = hidden * sigma
        act = silu * upper
        gates[...] += jnp.sum(act * dact, axis=1, keepdims=True)
        scaled = weight * dact
        dh = scaled * upper * sigma * (1.0 + hidden * (1.0 - sigma))
        du = scaled * silu
        wt_ref[at, :] = (weight * act).T.astype(BF16)
        dh_ref[at, :] = dh.T.astype(BF16)
        du_ref[at, :] = du.T.astype(BF16)
        acc[...] += jnp.dot(dh.astype(BF16), ring[slot, 0], preferred_element_type=F32) + jnp.dot(
            du.astype(BF16), ring[slot, 1], preferred_element_type=F32
        )

        @pl.when(i + slots < steps)
        def _():
            for n in range(3):
                load(i + slots, n).start()

        return carry

    lax.fori_loop(0, steps, step, 0)
    for at, out in ((1 - t, give_ref), (t, keep_ref)):
        held[...] = acc[:, pl.ds(pl.multiple_of(at * width, width), width)]
        pack(held, gates, out, pieces)


def expert_units(t, mine, theirs, w_gate, w_up, w_down, width):
    hidden, depth = w_gate.shape
    pieces = len(mine)
    rows = -(-pieces * CAP // 16) * 16
    tile = tile_of(hidden, 256)
    slots = min(3, hidden // tile)
    held = jax.ShapeDtypeStruct((rows, depth), BF16)
    unit = jax.ShapeDtypeStruct((hidden, rows), BF16)
    packed = jax.ShapeDtypeStruct((pieces * SUBS, width // 2 + width // SUBS + LANES), F32)
    return pl.pallas_call(
        functools.partial(experts_body, pieces),
        out_shape=(held, held, unit, unit, unit, packed, packed),
        in_specs=[SMEM] + [VMEM] * (2 * pieces) + [HBM] * 3,
        out_specs=[VMEM] * 7,
        scratch_shapes=[
            pltpu.VMEM((slots, 3, tile, depth), BF16),
            pltpu.VMEM((rows, width), F32),
            pltpu.VMEM((rows, depth), F32),
            pltpu.VMEM((rows, LANES), F32),
            pltpu.VMEM((rows, LANES), F32),
            pltpu.SemaphoreType.DMA((slots, 3)),
        ],
        compiler_params=pltpu.CompilerParams(vmem_limit_bytes=36 * MIB),
        cost_estimate=pl.CostEstimate(
            flops=10 * rows * hidden * depth, bytes_accessed=6 * hidden * depth, transcendentals=rows * hidden
        ),
        name="expert_units",
    )(t, *mine, *theirs, w_gate, w_up, w_down)


def weights_body(count, chunk, *refs):
    lefts, x_ref, outs, (ring, sent) = refs[:count], refs[count], refs[count + 1 : 2 * count + 1], refs[2 * count + 1 :]
    slots = ring.shape[1]
    hidden = lefts[0].shape[0]
    steps = x_ref.shape[1] // chunk
    tile = tile_of(hidden, 448)

    def store(i, n):
        cols = pl.ds(pl.multiple_of(i * chunk, chunk), chunk)
        slot = lax.rem(i, slots)
        return pltpu.make_async_copy(ring.at[n, slot], outs[n].at[:, cols], sent.at[n, slot])

    def step(i, carry):
        slot = lax.rem(i, slots)
        x = x_ref[:, pl.ds(pl.multiple_of(i * chunk, chunk), chunk)]
        for n in range(count):

            @pl.when(i >= slots)
            def _():
                store(i - slots, n).wait()

            for at in range(0, hidden, tile):
                ring[n, slot, at : at + tile, :] = jnp.dot(
                    lefts[n][at : at + tile, :], x, preferred_element_type=F32
                ).astype(BF16)
            store(i, n).start()
        return carry

    lax.fori_loop(0, steps, step, 0)
    for i in range(max(0, steps - slots), steps):
        for n in range(count):
            store(i, n).wait()


def weight_grads(lefts, right, name):
    count = len(lefts)
    hidden, rows = lefts[0].shape
    depth = right.shape[1]
    chunk = chunk_of(depth, 512)
    slots = min(4, depth // chunk)
    return pl.pallas_call(
        functools.partial(weights_body, count, chunk),
        out_shape=[jax.ShapeDtypeStruct((hidden, depth), BF16)] * count,
        in_specs=[VMEM] * (count + 1),
        out_specs=[HBM] * count,
        scratch_shapes=[pltpu.VMEM((count, slots, hidden, chunk), BF16), pltpu.SemaphoreType.DMA((count, slots))],
        compiler_params=pltpu.CompilerParams(vmem_limit_bytes=24 * MIB),
        cost_estimate=pl.CostEstimate(
            flops=2 * count * rows * hidden * depth, bytes_accessed=2 * count * hidden * depth, transcendentals=0
        ),
        name=name,
    )(*lefts, right)


def fold_body(copies, keep_ref, got_ref, *outs):
    for d, out in enumerate(outs):
        rows = slice(d * 2 * SUBS, (d + 1) * 2 * SUBS)
        out[...] = keep_ref[rows, :] + got_ref[rows, :]


def fold(copies, keep, got):
    return pl.pallas_call(
        functools.partial(fold_body, copies),
        out_shape=[jax.ShapeDtypeStruct((2 * SUBS, keep.shape[1]), F32)] * copies,
        in_specs=[VMEM] * 2,
        out_specs=[VMEM] * copies,
        compiler_params=pltpu.CompilerParams(vmem_limit_bytes=6 * MIB),
        name="fold_cores",
    )(keep, got)


def merge_body(*refs):
    blocks, (mine_ref, other_ref) = refs[:-2], refs[-2:]
    for at, out in ((0, mine_ref), (SUBS, other_ref)):
        total = blocks[0][at : at + SUBS, :]
        for block in blocks[1:]:
            total += block[at : at + SUBS, :]
        out[...] = total


def merge(blocks):
    part = jax.ShapeDtypeStruct((SUBS, blocks[0].shape[1]), F32)
    return pl.pallas_call(
        merge_body,
        out_shape=(part, part),
        in_specs=[VMEM] * len(blocks),
        out_specs=[VMEM] * 2,
        compiler_params=pltpu.CompilerParams(vmem_limit_bytes=6 * MIB),
        name="merge_chips",
    )(*blocks)


def finish_body(e_ref, ids_ref, mine_ref, got_ref, tok_ref, gate_ref):
    ids = ids_ref[...]
    toks, width = tok_ref.shape
    half, eighth = width // 2, width // SUBS
    both = 2 * SUBS
    row = iota((both, toks), 0)
    sub = sub_row(both, toks)
    expert = jnp.where(row < SUBS, e_ref[0], 1 - e_ref[0])
    main, hits = chosen_rows(ids, expert, sub % WHOLE)
    tail, _ = chosen_rows(ids, expert, jnp.full((both, toks), WHOLE, jnp.int32))
    plain = jnp.where(sub < WHOLE, main, jnp.where(sub == WHOLE, tail, 0.0))
    data = jnp.concatenate([mine_ref[...], got_ref[...]], axis=0)
    tn = (((0,), (0,)), ((), ()))
    exact = dict(precision=lax.Precision.HIGHEST, preferred_element_type=F32)
    halves = [
        lax.dot_general(jnp.where(sub // WHOLE == h, main, 0.0), data[:, :half], tn, **exact) for h in range(2)
    ]
    for s in range(SUBS):
        last = lax.dot_general(jnp.where(sub == s, tail, 0.0), data[:, half : half + eighth], tn, **exact)
        h, at = divmod(s * eighth, half)
        tok_ref[:, s * eighth : (s + 1) * eighth] = (halves[h][:, at : at + eighth] + last).astype(BF16)
    term = plain * data[:, half + eighth : half + eighth + 1]
    for k, hit in enumerate(hits):
        gate_ref[k : k + 1, :] = jnp.sum(jnp.where(hit, term, 0.0), axis=0, keepdims=True)


def finish(e, ids_t, mine, got, width):
    top, toks = ids_t.shape
    return pl.pallas_call(
        finish_body,
        out_shape=(jax.ShapeDtypeStruct((toks, width), BF16), jax.ShapeDtypeStruct((top, toks), F32)),
        in_specs=[SMEM] + [VMEM] * 3,
        out_specs=[VMEM] * 2,
        compiler_params=pltpu.CompilerParams(vmem_limit_bytes=6 * MIB),
        name="finish_tokens",
    )(e, ids_t, mine, got)


def on_device(tokens, grad_out, expert_ids, gate_probs, w_gate, w_up, w_down):
    n_expert = lax.axis_size("expert")
    copies = n_expert // EXPERTS_ON
    place = lax.axis_index("expert")
    e = (place >= copies).astype(jnp.int32).reshape(1)
    t = lax.axis_index("tensor").astype(jnp.int32).reshape(1)
    width = tokens.shape[1]

    def partner(v):
        return lax.ppermute(v, "expert", [(i, (i + copies) % n_expert) for i in range(n_expert)])

    def across(v, d):
        return lax.ppermute(v, "expert", [(i, i ^ d) for i in range(n_expert)])

    def other_core(v):
        return lax.ppermute(v, "tensor", [(0, 1), (1, 0)])

    w_gate, w_up, w_down = (pltpu.with_memory_space_constraint(w, pltpu.HBM) for w in (w_gate, w_up, w_down))
    ids_t = expert_ids.T
    here = (pltpu.with_memory_space_constraint(v, pltpu.HBM) for v in (ids_t, gate_probs.T, tokens, grad_out))
    own, oth = pick(e, *here)
    far_first = sorted(range(1, copies), key=lambda d: (-d.bit_count(), d))
    got = partner(oth)
    first = {0: own} | {d: across(own, d) for d in far_first}
    second = {0: got} | {d: across(got, d) for d in far_first}
    mine = [piece for d in range(copies) for piece in (first[d], second[d])]
    theirs = [other_core(piece) for piece in mine]
    x, g, wt, dh, du, give, keep = expert_units(t, mine, theirs, w_gate, w_up, w_down, width)
    blocks = list(fold(copies, keep, other_core(give)))
    arrived = {d: across(blocks[d], d) for d in far_first}
    dh, mine = lax.optimization_barrier((dh, blocks[0]))
    grads = weight_grads((dh, du), x, "grads_gate_up")
    grads, arrived = lax.optimization_barrier((grads, arrived))
    mine, others = merge([mine] + [arrived[d] for d in range(1, copies)])
    theirs = partner(others)
    wt, mine = lax.optimization_barrier((wt, mine))
    grads = [*grads, *weight_grads((wt,), g, "grad_down")]
    grads, theirs = lax.optimization_barrier((grads, theirs))
    token_grad, gate_t = finish(e, ids_t, mine, theirs, width)
    return token_grad, gate_t.T, *grads


def solution(mesh):
    return jax.shard_map(
        on_device,
        mesh=mesh,
        in_specs=(
            P(("groups", "expert"), "tensor"),
            P(("groups", "expert"), "tensor"),
            P(("groups", "expert"), None),
            P(("groups", "expert"), None),
            P(("expert", "tensor"), None),
            P(("expert", "tensor"), None),
            P(("expert", "tensor"), None),
        ),
        out_specs=(
            P(("groups", "expert"), "tensor"),
            P(("groups", "expert"), None),
            P(("expert", "tensor"), "groups"),
            P(("expert", "tensor"), "groups"),
            P(("expert", "tensor"), "groups"),
        ),
        check_vma=False,
    )
```

```python
import functools

import jax
import jax.numpy as jnp
from jax import lax
from jax.experimental import pallas as pl
from jax.experimental.pallas import tpu as pltpu
from jax.sharding import PartitionSpec as P

EXPERTS_ON = 2
CAP = 5
LANES = 128
SUBS = 8
WHOLE = 4
F32 = jnp.float32
BF16 = jnp.bfloat16
MIB = 1 << 20
VMEM = pl.BlockSpec(memory_space=pltpu.VMEM)
SMEM = pl.BlockSpec(memory_space=pltpu.SMEM)
HBM = pl.BlockSpec(memory_space=pltpu.HBM)


def iota(shape, dim):
    return lax.broadcasted_iota(jnp.int32, shape, dim)


def chosen_rows(ids, expert, position):
    rows, toks = position.shape
    hits = [ids[k : k + 1, :] == expert for k in range(ids.shape[0])]
    member = functools.reduce(jnp.logical_or, hits).astype(F32)
    before = (iota((toks, toks), 0) < iota((toks, toks), 1)).astype(F32)
    earlier = jnp.dot(member, before, preferred_element_type=F32)
    return jnp.where(earlier == position.astype(F32), member, 0.0), hits


def sub_row(rows, toks):
    return iota((rows, toks), 0) % SUBS


def tile_of(hidden, most):
    sizes = [n for n in range(16, most + 1, 16) if hidden % n == 0]
    return max(sizes) if sizes else hidden


def pick_body(e_ref, ids_any, probs_any, tok_any, grad_any, own_ref, oth_ref, ids_ref, probs_ref, tok_ref, grad_ref, landed):
    copies = [
        pltpu.make_async_copy(src, dst, landed.at[n])
        for n, (src, dst) in enumerate(
            ((ids_any, ids_ref), (probs_any, probs_ref), (tok_any, tok_ref), (grad_any, grad_ref))
        )
    ]
    for copy in copies:
        copy.start()
    for copy in copies[:2]:
        copy.wait()
    ids = ids_ref[...]
    probs = probs_ref[...].astype(F32)
    toks, width = tok_ref.shape
    half, eighth = width // 2, width // SUBS
    size = half + eighth
    both = 2 * SUBS
    row = iota((both, toks), 0)
    sub = sub_row(both, toks)
    expert = jnp.where(row < SUBS, e_ref[0], 1 - e_ref[0])
    main, hits = chosen_rows(ids, expert, sub % WHOLE)
    tail, _ = chosen_rows(ids, expert, jnp.full((both, toks), WHOLE, jnp.int32))
    plain = jnp.where(sub < WHOLE, main, jnp.where(sub == WHOLE, tail, 0.0))
    halves = [jnp.where(sub // WHOLE == h, main, 0.0).astype(BF16) for h in range(2)]
    eighths = [jnp.where(sub == s, tail, 0.0).astype(BF16) for s in range(SUBS)]
    for at, src in enumerate((tok_ref, grad_ref)):
        copies[2 + at].wait()
        packed = sum(
            jnp.dot(one, src[:, h * half : (h + 1) * half], preferred_element_type=F32)
            for h, one in enumerate(halves)
        ).astype(BF16)
        last = sum(
            jnp.dot(one, src[:, s * eighth : (s + 1) * eighth], preferred_element_type=F32)
            for s, one in enumerate(eighths)
        ).astype(BF16)
        for n, dst in enumerate((own_ref, oth_ref)):
            dst[:, at * size : at * size + half] = packed[n * SUBS : (n + 1) * SUBS]
            dst[:, at * size + half : (at + 1) * size] = last[n * SUBS : (n + 1) * SUBS]
    weight = sum(jnp.where(hit, probs[k : k + 1, :], 0.0) for k, hit in enumerate(hits))
    gate = jnp.broadcast_to(jnp.sum(plain * weight, axis=1, keepdims=True), (both, LANES)).astype(BF16)
    for n, dst in enumerate((own_ref, oth_ref)):
        dst[:, 2 * size :] = gate[n * SUBS : (n + 1) * SUBS]


def pick(e, ids_t, probs_t, tokens, grad_out):
    width = tokens.shape[1]
    size = width // 2 + width // SUBS
    piece = jax.ShapeDtypeStruct((SUBS, 2 * size + LANES), BF16)
    return pl.pallas_call(
        pick_body,
        out_shape=(piece, piece),
        in_specs=[SMEM] + [HBM] * 4,
        out_specs=[VMEM] * 2,
        scratch_shapes=[pltpu.VMEM(v.shape, v.dtype) for v in (ids_t, probs_t, tokens, grad_out)]
        + [pltpu.SemaphoreType.DMA((4,))],
        compiler_params=pltpu.CompilerParams(vmem_limit_bytes=6 * MIB),
        name="pick_rows",
    )(e, ids_t, probs_t, tokens, grad_out)


NT = (((1,), (1,)), ((), ()))


def chunk_of(width, most):
    return max(n for n in range(LANES, most + 1, LANES) if width % n == 0)


def assemble(pieces, held, out, base, side):
    width = held.shape[1]
    half, eighth = width // 2, width // SUBS
    size = half + eighth
    for n, ref in enumerate(pieces):
        at = n * CAP
        piece = ref[:, side * size : (side + 1) * size].astype(F32)
        for h in range(2):
            held[at : at + WHOLE, h * half : (h + 1) * half] = piece[h * WHOLE : (h + 1) * WHOLE, :half]
        for s in range(SUBS):
            held[at + WHOLE : at + CAP, s * eighth : (s + 1) * eighth] = piece[s : s + 1, half:]
    out[:, pl.ds(base, width)] = held[...].astype(BF16)


def pack(part, gates, out, pieces):
    width = part.shape[1]
    half, eighth = width // 2, width // SUBS
    size = half + eighth
    for n in range(pieces):
        at, to = n * CAP, n * SUBS
        for h in range(2):
            out[to + h * WHOLE : to + (h + 1) * WHOLE, :half] = part[at : at + WHOLE, h * half : (h + 1) * half]
        for s in range(SUBS):
            out[to + s : to + s + 1, half:size] = part[at + WHOLE : at + CAP, s * eighth : (s + 1) * eighth]
        out[to : to + CAP, size:] = gates[at : at + CAP, :]
        out[to + CAP : to + SUBS, size:] = jnp.zeros((SUBS - CAP, LANES), F32)


def experts_body(pieces, chunk, ahead, t_ref, *refs):
    mine, theirs = refs[:pieces], refs[pieces : 2 * pieces]
    (wg_hbm, wu_hbm, wd_hbm, x_ref, dh_ref, du_ref, give_ref, keep_ref, down_ref,
     wg_ref, wu_ref, ring, g_ref, wt_ref, h_ref, u_ref, da_ref, dhr_ref, dur_ref, acc,
     held, factor, landed, ring_landed, sent) = refs[2 * pieces :]
    rows, depth = x_ref.shape
    hidden = wg_ref.shape[0]
    width = depth // 2
    slots = ring.shape[0]
    steps = depth // chunk
    t = t_ref[0]

    def columns(i):
        return pl.ds(pl.multiple_of(i * chunk, chunk), chunk)

    def load(i, n):
        src, dst = ((wg_hbm, wg_ref), (wu_hbm, wu_ref))[n]
        return pltpu.make_async_copy(src.at[:, columns(i)], dst.at[:, columns(i)], landed.at[i, n])

    def load_down(i):
        slot = lax.rem(i, slots)
        return pltpu.make_async_copy(wd_hbm.at[:, columns(i)], ring.at[slot], ring_landed.at[slot])

    def store_down(i):
        slot = lax.rem(i, slots)
        return pltpu.make_async_copy(ring.at[slot], down_ref.at[:, columns(i)], sent.at[slot])

    for n in range(2):
        load(0, n).start()
    held[...] = jnp.zeros_like(held)
    factor[...] = jnp.zeros_like(factor)
    for n, ref in enumerate(mine):
        factor[n * CAP : (n + 1) * CAP, :] = ref[:CAP, ref.shape[1] - LANES :].astype(F32)
    for side, out in enumerate((x_ref, g_ref)):
        for group, at in ((mine, t), (theirs, 1 - t)):
            assemble(group, held, out, pl.multiple_of(at * width, width), side)
        if side == 0:
            for i in range(1, min(ahead, steps)):
                for n in range(2):
                    load(i, n).start()

    def add_to(out, i, w, x):
        more = lax.dot_general(w, x, NT, preferred_element_type=F32)
        out[...] = jnp.where(i == 0, more, out[...] + more)

    def up_step(i, carry):
        x = x_ref[:, columns(i)]
        load(i, 0).wait()
        add_to(h_ref, i, wg_ref[:, columns(i)], x)
        load(i, 1).wait()

        @pl.when(i + ahead < steps)
        def _():
            for n in range(2):
                load(i + ahead, n).start()

        @pl.when(i + ahead >= steps)
        def _():
            load_down(i + ahead - steps).start()

        add_to(u_ref, i, wu_ref[:, columns(i)], x)
        return carry

    lax.fori_loop(0, steps, up_step, 0)

    def down_step(i, carry):
        g = g_ref[:, columns(i)]
        load_down(i).wait()

        @pl.when(i + ahead < steps)
        def _():
            load_down(i + ahead).start()

        add_to(da_ref, i, ring[lax.rem(i, slots)], g)
        return carry

    lax.fori_loop(0, steps, down_step, 0)

    weight = factor[...].T[:1, :]

    def units(start, size, total):
        at = pl.ds(start, size)
        h = h_ref[at, :]
        u = u_ref[at, :]
        da = da_ref[at, :]
        sigma = 1.0 / (1.0 + jnp.exp(-h))
        silu = h * sigma
        act = silu * u
        scaled = weight * da
        wt_ref[at, :] = (weight * act).astype(BF16)
        dh = scaled * u * sigma * (1.0 + h * (1.0 - sigma))
        du = scaled * silu
        dh_ref[at, :] = dh.astype(BF16)
        du_ref[at, :] = du.astype(BF16)
        dhr_ref[:, at] = dh.T.astype(BF16)
        dur_ref[:, at] = du.T.astype(BF16)
        return total + jnp.sum(act * da, axis=0, keepdims=True)

    whole = hidden // LANES
    total = lax.fori_loop(
        0, whole, lambda i, v: units(pl.multiple_of(i * LANES, LANES), LANES, v), jnp.zeros((1, rows), F32)
    )
    if hidden % LANES:
        total = units(whole * LANES, hidden % LANES, total)
    gates = jnp.broadcast_to(total, (LANES, rows)).T
    tile = tile_of(hidden, 448)

    def grad_step(i, carry):
        slot = lax.rem(i, slots)
        cols = columns(i)

        @pl.when(i >= slots)
        def _():
            store_down(i - slots).wait()

        g = g_ref[:, cols]
        for at in range(0, hidden, tile):
            ring[slot, at : at + tile, :] = jnp.dot(
                wt_ref[at : at + tile, :], g, preferred_element_type=F32
            ).astype(BF16)
        store_down(i).start()
        acc[:, cols] = jnp.dot(dhr_ref[...], wg_ref[:, cols], preferred_element_type=F32) + jnp.dot(
            dur_ref[...], wu_ref[:, cols], preferred_element_type=F32
        )
        return carry

    lax.fori_loop(0, steps, grad_step, 0)
    for at, out in ((1 - t, give_ref), (t, keep_ref)):
        held[...] = acc[:, pl.ds(pl.multiple_of(at * width, width), width)]
        pack(held, gates, out, pieces)
    for i in range(max(0, steps - slots), steps):
        store_down(i).wait()


def expert_units(t, mine, theirs, w_gate, w_up, w_down, width):
    hidden, depth = w_gate.shape
    pieces = len(mine)
    rows = -(-pieces * CAP // 16) * 16
    chunk = chunk_of(width, 768)
    steps = depth // chunk
    ahead = 2
    slots = 4
    unit = jax.ShapeDtypeStruct((hidden, rows), BF16)
    packed = jax.ShapeDtypeStruct((pieces * SUBS, width // 2 + width // SUBS + LANES), F32)
    return pl.pallas_call(
        functools.partial(experts_body, pieces, chunk, ahead),
        out_shape=(
            jax.ShapeDtypeStruct((rows, depth), BF16),
            unit,
            unit,
            packed,
            packed,
            jax.ShapeDtypeStruct((hidden, depth), BF16),
        ),
        in_specs=[SMEM] + [VMEM] * (2 * pieces) + [HBM] * 3,
        out_specs=[VMEM] * 5 + [HBM],
        scratch_shapes=[
            pltpu.VMEM((hidden, depth), BF16),
            pltpu.VMEM((hidden, depth), BF16),
            pltpu.VMEM((slots, hidden, chunk), BF16),
            pltpu.VMEM((rows, depth), BF16),
            pltpu.VMEM((hidden, rows), BF16),
            pltpu.VMEM((hidden, rows), F32),
            pltpu.VMEM((hidden, rows), F32),
            pltpu.VMEM((hidden, rows), F32),
            pltpu.VMEM((rows, hidden), BF16),
            pltpu.VMEM((rows, hidden), BF16),
            pltpu.VMEM((rows, depth), F32),
            pltpu.VMEM((rows, width), F32),
            pltpu.VMEM((rows, LANES), F32),
            pltpu.SemaphoreType.DMA((steps, 2)),
            pltpu.SemaphoreType.DMA((slots,)),
            pltpu.SemaphoreType.DMA((slots,)),
        ],
        compiler_params=pltpu.CompilerParams(vmem_limit_bytes=50 * MIB),
        cost_estimate=pl.CostEstimate(
            flops=12 * rows * hidden * depth, bytes_accessed=8 * hidden * depth, transcendentals=rows * hidden
        ),
        name="expert_units",
    )(t, *mine, *theirs, w_gate, w_up, w_down)


def weights_body(count, chunk, *refs):
    lefts, x_ref, outs, (ring, sent) = refs[:count], refs[count], refs[count + 1 : 2 * count + 1], refs[2 * count + 1 :]
    slots = ring.shape[1]
    hidden = lefts[0].shape[0]
    steps = x_ref.shape[1] // chunk
    tile = tile_of(hidden, 448)

    def store(i, n):
        cols = pl.ds(pl.multiple_of(i * chunk, chunk), chunk)
        slot = lax.rem(i, slots)
        return pltpu.make_async_copy(ring.at[n, slot], outs[n].at[:, cols], sent.at[n, slot])

    def step(i, carry):
        slot = lax.rem(i, slots)
        x = x_ref[:, pl.ds(pl.multiple_of(i * chunk, chunk), chunk)]
        for n in range(count):

            @pl.when(i >= slots)
            def _():
                store(i - slots, n).wait()

            for at in range(0, hidden, tile):
                ring[n, slot, at : at + tile, :] = jnp.dot(
                    lefts[n][at : at + tile, :], x, preferred_element_type=F32
                ).astype(BF16)
            store(i, n).start()
        return carry

    lax.fori_loop(0, steps, step, 0)
    for i in range(max(0, steps - slots), steps):
        for n in range(count):
            store(i, n).wait()


def weight_grads(lefts, right, name):
    count = len(lefts)
    hidden, rows = lefts[0].shape
    depth = right.shape[1]
    chunk = chunk_of(depth, 512)
    slots = min(4, depth // chunk)
    return pl.pallas_call(
        functools.partial(weights_body, count, chunk),
        out_shape=[jax.ShapeDtypeStruct((hidden, depth), BF16)] * count,
        in_specs=[VMEM] * (count + 1),
        out_specs=[HBM] * count,
        scratch_shapes=[pltpu.VMEM((count, slots, hidden, chunk), BF16), pltpu.SemaphoreType.DMA((count, slots))],
        compiler_params=pltpu.CompilerParams(vmem_limit_bytes=24 * MIB),
        cost_estimate=pl.CostEstimate(
            flops=2 * count * rows * hidden * depth, bytes_accessed=2 * count * hidden * depth, transcendentals=0
        ),
        name=name,
    )(*lefts, right)


def fold_body(copies, keep_ref, got_ref, *outs):
    for d, out in enumerate(outs):
        rows = slice(d * 2 * SUBS, (d + 1) * 2 * SUBS)
        out[...] = keep_ref[rows, :] + got_ref[rows, :]


def fold(copies, keep, got):
    return pl.pallas_call(
        functools.partial(fold_body, copies),
        out_shape=[jax.ShapeDtypeStruct((2 * SUBS, keep.shape[1]), F32)] * copies,
        in_specs=[VMEM] * 2,
        out_specs=[VMEM] * copies,
        compiler_params=pltpu.CompilerParams(vmem_limit_bytes=6 * MIB),
        name="fold_cores",
    )(keep, got)


def merge_body(*refs):
    blocks, (mine_ref, other_ref) = refs[:-2], refs[-2:]
    for at, out in ((0, mine_ref), (SUBS, other_ref)):
        total = blocks[0][at : at + SUBS, :]
        for block in blocks[1:]:
            total += block[at : at + SUBS, :]
        out[...] = total


def merge(blocks):
    part = jax.ShapeDtypeStruct((SUBS, blocks[0].shape[1]), F32)
    return pl.pallas_call(
        merge_body,
        out_shape=(part, part),
        in_specs=[VMEM] * len(blocks),
        out_specs=[VMEM] * 2,
        compiler_params=pltpu.CompilerParams(vmem_limit_bytes=6 * MIB),
        name="merge_chips",
    )(*blocks)


def finish_body(e_ref, ids_ref, mine_ref, got_ref, tok_ref, gate_ref):
    ids = ids_ref[...]
    toks, width = tok_ref.shape
    half, eighth = width // 2, width // SUBS
    both = 2 * SUBS
    row = iota((both, toks), 0)
    sub = sub_row(both, toks)
    expert = jnp.where(row < SUBS, e_ref[0], 1 - e_ref[0])
    main, hits = chosen_rows(ids, expert, sub % WHOLE)
    tail, _ = chosen_rows(ids, expert, jnp.full((both, toks), WHOLE, jnp.int32))
    plain = jnp.where(sub < WHOLE, main, jnp.where(sub == WHOLE, tail, 0.0))
    data = jnp.concatenate([mine_ref[...], got_ref[...]], axis=0)
    tn = (((0,), (0,)), ((), ()))
    exact = dict(precision=lax.Precision.HIGHEST, preferred_element_type=F32)
    halves = [
        lax.dot_general(jnp.where(sub // WHOLE == h, main, 0.0), data[:, :half], tn, **exact) for h in range(2)
    ]
    for s in range(SUBS):
        last = lax.dot_general(jnp.where(sub == s, tail, 0.0), data[:, half : half + eighth], tn, **exact)
        h, at = divmod(s * eighth, half)
        tok_ref[:, s * eighth : (s + 1) * eighth] = (halves[h][:, at : at + eighth] + last).astype(BF16)
    term = plain * data[:, half + eighth : half + eighth + 1]
    for k, hit in enumerate(hits):
        gate_ref[k : k + 1, :] = jnp.sum(jnp.where(hit, term, 0.0), axis=0, keepdims=True)


def finish(e, ids_t, mine, got, width):
    top, toks = ids_t.shape
    return pl.pallas_call(
        finish_body,
        out_shape=(jax.ShapeDtypeStruct((toks, width), BF16), jax.ShapeDtypeStruct((top, toks), F32)),
        in_specs=[SMEM] + [VMEM] * 3,
        out_specs=[VMEM] * 2,
        compiler_params=pltpu.CompilerParams(vmem_limit_bytes=6 * MIB),
        name="finish_tokens",
    )(e, ids_t, mine, got)


def on_device(tokens, grad_out, expert_ids, gate_probs, w_gate, w_up, w_down):
    n_expert = lax.axis_size("expert")
    copies = n_expert // EXPERTS_ON
    place = lax.axis_index("expert")
    e = (place >= copies).astype(jnp.int32).reshape(1)
    t = lax.axis_index("tensor").astype(jnp.int32).reshape(1)
    width = tokens.shape[1]

    def partner(v):
        return lax.ppermute(v, "expert", [(i, (i + copies) % n_expert) for i in range(n_expert)])

    def across(v, d):
        return lax.ppermute(v, "expert", [(i, i ^ d) for i in range(n_expert)])

    def other_core(v):
        return lax.ppermute(v, "tensor", [(0, 1), (1, 0)])

    w_gate, w_up, w_down = (pltpu.with_memory_space_constraint(w, pltpu.HBM) for w in (w_gate, w_up, w_down))
    ids_t = expert_ids.T
    here = (pltpu.with_memory_space_constraint(v, pltpu.HBM) for v in (ids_t, gate_probs.T, tokens, grad_out))
    own, oth = pick(e, *here)
    far_first = sorted(range(1, copies), key=lambda d: (-d.bit_count(), d))
    got = partner(oth)
    first = {0: own} | {d: across(own, d) for d in far_first}
    second = {0: got} | {d: across(got, d) for d in far_first}
    mine = [piece for d in range(copies) for piece in (first[d], second[d])]
    theirs = [other_core(piece) for piece in mine]
    x, dh, du, give, keep, grad_w_down = expert_units(t, mine, theirs, w_gate, w_up, w_down, width)
    blocks = list(fold(copies, keep, other_core(give)))
    arrived = {d: across(blocks[d], d) for d in far_first}
    dh, local = lax.optimization_barrier((dh, blocks[0]))
    (grad_w_gate,) = weight_grads((dh,), x, "grad_gate")
    grad_w_gate, arrived = lax.optimization_barrier((grad_w_gate, arrived))
    kept, others = merge([local] + [arrived[d] for d in range(1, copies)])
    back = partner(others)
    du, kept = lax.optimization_barrier((du, kept))
    (grad_w_up,) = weight_grads((du,), x, "grad_up")
    grad_w_up, back = lax.optimization_barrier((grad_w_up, back))
    token_grad, gate_t = finish(e, ids_t, kept, back, width)
    return token_grad, gate_t.T, grad_w_gate, grad_w_up, grad_w_down


def solution(mesh):
    return jax.shard_map(
        on_device,
        mesh=mesh,
        in_specs=(
            P(("groups", "expert"), "tensor"),
            P(("groups", "expert"), "tensor"),
            P(("groups", "expert"), None),
            P(("groups", "expert"), None),
            P(("expert", "tensor"), None),
            P(("expert", "tensor"), None),
            P(("expert", "tensor"), None),
        ),
        out_specs=(
            P(("groups", "expert"), "tensor"),
            P(("groups", "expert"), None),
            P(("expert", "tensor"), "groups"),
            P(("expert", "tensor"), "groups"),
            P(("expert", "tensor"), "groups"),
        ),
        check_vma=False,
    )
```

```python
import functools

import jax
import jax.numpy as jnp
from jax import lax
from jax.experimental import pallas as pl
from jax.experimental.pallas import tpu as pltpu
from jax.sharding import PartitionSpec as P

EXPERTS_ON = 2
CAP = 5
LANES = 128
SUBS = 8
WHOLE = 4
F32 = jnp.float32
BF16 = jnp.bfloat16
MIB = 1 << 20
VMEM = pl.BlockSpec(memory_space=pltpu.VMEM)
SMEM = pl.BlockSpec(memory_space=pltpu.SMEM)
HBM = pl.BlockSpec(memory_space=pltpu.HBM)


def iota(shape, dim):
    return lax.broadcasted_iota(jnp.int32, shape, dim)


def chosen_rows(ids, expert, position):
    rows, toks = position.shape
    hits = [ids[k : k + 1, :] == expert for k in range(ids.shape[0])]
    member = functools.reduce(jnp.logical_or, hits).astype(F32)
    before = (iota((toks, toks), 0) < iota((toks, toks), 1)).astype(F32)
    earlier = jnp.dot(member, before, preferred_element_type=F32)
    return jnp.where(earlier == position.astype(F32), member, 0.0), hits


def sub_row(rows, toks):
    return iota((rows, toks), 0) % SUBS


def tile_of(hidden, most):
    sizes = [n for n in range(16, most + 1, 16) if hidden % n == 0]
    return max(sizes) if sizes else hidden


def pick_body(e_ref, ids_any, probs_any, tok_any, grad_any, own_ref, oth_ref, ids_ref, probs_ref, tok_ref, grad_ref, landed):
    copies = [
        pltpu.make_async_copy(src, dst, landed.at[n])
        for n, (src, dst) in enumerate(
            ((ids_any, ids_ref), (probs_any, probs_ref), (tok_any, tok_ref), (grad_any, grad_ref))
        )
    ]
    for copy in copies:
        copy.start()
    for copy in copies[:2]:
        copy.wait()
    ids = ids_ref[...]
    probs = probs_ref[...].astype(F32)
    toks, width = tok_ref.shape
    half, eighth = width // 2, width // SUBS
    size = half + eighth
    both = 2 * SUBS
    row = iota((both, toks), 0)
    sub = sub_row(both, toks)
    expert = jnp.where(row < SUBS, e_ref[0], 1 - e_ref[0])
    main, hits = chosen_rows(ids, expert, sub % WHOLE)
    tail, _ = chosen_rows(ids, expert, jnp.full((both, toks), WHOLE, jnp.int32))
    plain = jnp.where(sub < WHOLE, main, jnp.where(sub == WHOLE, tail, 0.0))
    halves = [jnp.where(sub // WHOLE == h, main, 0.0).astype(BF16) for h in range(2)]
    eighths = [jnp.where(sub == s, tail, 0.0).astype(BF16) for s in range(SUBS)]
    for at, src in enumerate((tok_ref, grad_ref)):
        copies[2 + at].wait()
        packed = sum(
            jnp.dot(one, src[:, h * half : (h + 1) * half], preferred_element_type=F32)
            for h, one in enumerate(halves)
        ).astype(BF16)
        last = sum(
            jnp.dot(one, src[:, s * eighth : (s + 1) * eighth], preferred_element_type=F32)
            for s, one in enumerate(eighths)
        ).astype(BF16)
        for n, dst in enumerate((own_ref, oth_ref)):
            dst[:, at * size : at * size + half] = packed[n * SUBS : (n + 1) * SUBS]
            dst[:, at * size + half : (at + 1) * size] = last[n * SUBS : (n + 1) * SUBS]
    weight = sum(jnp.where(hit, probs[k : k + 1, :], 0.0) for k, hit in enumerate(hits))
    gate = jnp.broadcast_to(jnp.sum(plain * weight, axis=1, keepdims=True), (both, LANES)).astype(BF16)
    for n, dst in enumerate((own_ref, oth_ref)):
        dst[:, 2 * size :] = gate[n * SUBS : (n + 1) * SUBS]


def pick(e, ids_t, probs_t, tokens, grad_out):
    width = tokens.shape[1]
    size = width // 2 + width // SUBS
    piece = jax.ShapeDtypeStruct((SUBS, 2 * size + LANES), BF16)
    return pl.pallas_call(
        pick_body,
        out_shape=(piece, piece),
        in_specs=[SMEM] + [HBM] * 4,
        out_specs=[VMEM] * 2,
        scratch_shapes=[pltpu.VMEM(v.shape, v.dtype) for v in (ids_t, probs_t, tokens, grad_out)]
        + [pltpu.SemaphoreType.DMA((4,))],
        compiler_params=pltpu.CompilerParams(vmem_limit_bytes=6 * MIB),
        name="pick_rows",
    )(e, ids_t, probs_t, tokens, grad_out)


NT = (((1,), (1,)), ((), ()))


def chunk_of(width, most):
    return max(n for n in range(LANES, most + 1, LANES) if width % n == 0)


def assemble(pieces, held, out, base, side):
    width = held.shape[1]
    half, eighth = width // 2, width // SUBS
    size = half + eighth
    for n, ref in enumerate(pieces):
        at = n * CAP
        piece = ref[:, side * size : (side + 1) * size].astype(F32)
        for h in range(2):
            held[at : at + WHOLE, h * half : (h + 1) * half] = piece[h * WHOLE : (h + 1) * WHOLE, :half]
        for s in range(SUBS):
            held[at + WHOLE : at + CAP, s * eighth : (s + 1) * eighth] = piece[s : s + 1, half:]
    out[:, pl.ds(base, width)] = held[...].astype(BF16)


def pack(part, gates, out, pieces):
    width = part.shape[1]
    half, eighth = width // 2, width // SUBS
    size = half + eighth
    for n in range(pieces):
        at, to = n * CAP, n * SUBS
        for h in range(2):
            out[to + h * WHOLE : to + (h + 1) * WHOLE, :half] = part[at : at + WHOLE, h * half : (h + 1) * half]
        for s in range(SUBS):
            out[to + s : to + s + 1, half:size] = part[at + WHOLE : at + CAP, s * eighth : (s + 1) * eighth]
        out[to : to + CAP, size:] = gates[at : at + CAP, :]
        out[to + CAP : to + SUBS, size:] = jnp.zeros((SUBS - CAP, LANES), F32)


def experts_body(pieces, chunk, ahead, t_ref, *refs):
    mine, theirs = refs[:pieces], refs[pieces : 2 * pieces]
    (wg_hbm, wu_hbm, wd_hbm, x_ref, dh_ref, du_ref, give_ref, keep_ref, down_ref,
     wg_ref, wu_ref, ring, g_ref, wt_ref, h_ref, u_ref, da_ref, dhr_ref, dur_ref, acc,
     held, factor, landed, ring_landed, sent) = refs[2 * pieces :]
    rows, depth = x_ref.shape
    hidden = wg_ref.shape[0]
    width = depth // 2
    slots = ring.shape[0]
    steps = depth // chunk
    t = t_ref[0]

    def columns(i):
        return pl.ds(pl.multiple_of(i * chunk, chunk), chunk)

    def load(i, n):
        src, dst = ((wg_hbm, wg_ref), (wu_hbm, wu_ref))[n]
        return pltpu.make_async_copy(src.at[:, columns(i)], dst.at[:, columns(i)], landed.at[i, n])

    def load_down(i):
        slot = lax.rem(i, slots)
        return pltpu.make_async_copy(wd_hbm.at[:, columns(i)], ring.at[slot], ring_landed.at[slot])

    def store_down(i):
        slot = lax.rem(i, slots)
        return pltpu.make_async_copy(ring.at[slot], down_ref.at[:, columns(i)], sent.at[slot])

    def start(i):
        load(i, 0).start()
        load(i, 1).start()
        load_down(i).start()

    start(0)
    held[...] = jnp.zeros_like(held)
    factor[...] = jnp.zeros_like(factor)
    for n, ref in enumerate(mine):
        factor[n * CAP : (n + 1) * CAP, :] = ref[:CAP, ref.shape[1] - LANES :].astype(F32)
    for side, out in enumerate((x_ref, g_ref)):
        for group, at in ((mine, t), (theirs, 1 - t)):
            assemble(group, held, out, pl.multiple_of(at * width, width), side)
    for i in range(1, min(ahead, steps)):
        start(i)

    def three(i):
        cols = columns(i)
        x = x_ref[:, cols]
        return (
            lambda: lax.dot_general(wg_ref[:, cols], x, NT, preferred_element_type=F32),
            lambda: lax.dot_general(wu_ref[:, cols], x, NT, preferred_element_type=F32),
            lambda: lax.dot_general(ring[lax.rem(i, slots)], g_ref[:, cols], NT, preferred_element_type=F32),
        )

    sums = (h_ref, u_ref, da_ref)
    waits = lambda i: (load(i, 0), load(i, 1), load_down(i))
    for wait, dot, out in zip(waits(0), three(0), sums):
        wait.wait()
        out[...] = dot()

    def up_step(i, carry):
        @pl.when(i + ahead - 1 < steps)
        def _():
            start(i + ahead - 1)

        for wait in waits(i):
            wait.wait()
        for dot, out in zip(three(i), sums):
            out[...] += dot()
        return carry

    lax.fori_loop(1, steps, up_step, 0)

    weight = factor[...].T[:1, :]

    def units(start, size, total):
        at = pl.ds(start, size)
        h = h_ref[at, :]
        u = u_ref[at, :]
        da = da_ref[at, :]
        sigma = 1.0 / (1.0 + jnp.exp(-h))
        silu = h * sigma
        act = silu * u
        scaled = weight * da
        wt_ref[at, :] = (weight * act).astype(BF16)
        dh = scaled * u * sigma * (1.0 + h * (1.0 - sigma))
        du = scaled * silu
        dh_ref[at, :] = dh.astype(BF16)
        du_ref[at, :] = du.astype(BF16)
        dhr_ref[:, at] = dh.T.astype(BF16)
        dur_ref[:, at] = du.T.astype(BF16)
        return total + jnp.sum(act * da, axis=0, keepdims=True)

    total = jnp.zeros((1, rows), F32)
    for begin in range(0, hidden, LANES):
        total = units(begin, min(LANES, hidden - begin), total)
    gates = jnp.broadcast_to(total, (LANES, rows)).T
    tile = tile_of(hidden, 448)

    def grad_step(i, carry):
        slot = lax.rem(i, slots)
        cols = columns(i)

        @pl.when(i >= slots)
        def _():
            store_down(i - slots).wait()

        g = g_ref[:, cols]
        for at in range(0, hidden, tile):
            ring[slot, at : at + tile, :] = jnp.dot(
                wt_ref[at : at + tile, :], g, preferred_element_type=F32
            ).astype(BF16)
        store_down(i).start()
        acc[:, cols] = jnp.dot(dhr_ref[...], wg_ref[:, cols], preferred_element_type=F32) + jnp.dot(
            dur_ref[...], wu_ref[:, cols], preferred_element_type=F32
        )
        return carry

    lax.fori_loop(0, steps, grad_step, 0)
    for at, out in ((1 - t, give_ref), (t, keep_ref)):
        held[...] = acc[:, pl.ds(pl.multiple_of(at * width, width), width)]
        pack(held, gates, out, pieces)
    for i in range(max(0, steps - slots), steps):
        store_down(i).wait()


def expert_units(t, mine, theirs, w_gate, w_up, w_down, width):
    hidden, depth = w_gate.shape
    pieces = len(mine)
    rows = -(-pieces * CAP // 16) * 16
    chunk = chunk_of(width, 768)
    steps = depth // chunk
    ahead = 3
    slots = 4
    unit = jax.ShapeDtypeStruct((hidden, rows), BF16)
    packed = jax.ShapeDtypeStruct((pieces * SUBS, width // 2 + width // SUBS + LANES), F32)
    return pl.pallas_call(
        functools.partial(experts_body, pieces, chunk, ahead),
        out_shape=(
            jax.ShapeDtypeStruct((rows, depth), BF16),
            unit,
            unit,
            packed,
            packed,
            jax.ShapeDtypeStruct((hidden, depth), BF16),
        ),
        in_specs=[SMEM] + [VMEM] * (2 * pieces) + [HBM] * 3,
        out_specs=[VMEM] * 5 + [HBM],
        scratch_shapes=[
            pltpu.VMEM((hidden, depth), BF16),
            pltpu.VMEM((hidden, depth), BF16),
            pltpu.VMEM((slots, hidden, chunk), BF16),
            pltpu.VMEM((rows, depth), BF16),
            pltpu.VMEM((hidden, rows), BF16),
            pltpu.VMEM((hidden, rows), F32),
            pltpu.VMEM((hidden, rows), F32),
            pltpu.VMEM((hidden, rows), F32),
            pltpu.VMEM((rows, hidden), BF16),
            pltpu.VMEM((rows, hidden), BF16),
            pltpu.VMEM((rows, depth), F32),
            pltpu.VMEM((rows, width), F32),
            pltpu.VMEM((rows, LANES), F32),
            pltpu.SemaphoreType.DMA((steps, 2)),
            pltpu.SemaphoreType.DMA((slots,)),
            pltpu.SemaphoreType.DMA((slots,)),
        ],
        compiler_params=pltpu.CompilerParams(vmem_limit_bytes=50 * MIB),
        cost_estimate=pl.CostEstimate(
            flops=12 * rows * hidden * depth, bytes_accessed=8 * hidden * depth, transcendentals=rows * hidden
        ),
        name="expert_units",
    )(t, *mine, *theirs, w_gate, w_up, w_down)


def weights_body(count, chunk, *refs):
    lefts, x_ref, outs, (ring, sent) = refs[:count], refs[count], refs[count + 1 : 2 * count + 1], refs[2 * count + 1 :]
    slots = ring.shape[1]
    hidden = lefts[0].shape[0]
    steps = x_ref.shape[1] // chunk
    tile = tile_of(hidden, 448)

    def store(i, n):
        cols = pl.ds(pl.multiple_of(i * chunk, chunk), chunk)
        slot = lax.rem(i, slots)
        return pltpu.make_async_copy(ring.at[n, slot], outs[n].at[:, cols], sent.at[n, slot])

    def step(i, carry):
        slot = lax.rem(i, slots)
        x = x_ref[:, pl.ds(pl.multiple_of(i * chunk, chunk), chunk)]
        for n in range(count):

            @pl.when(i >= slots)
            def _():
                store(i - slots, n).wait()

            for at in range(0, hidden, tile):
                ring[n, slot, at : at + tile, :] = jnp.dot(
                    lefts[n][at : at + tile, :], x, preferred_element_type=F32
                ).astype(BF16)
            store(i, n).start()
        return carry

    lax.fori_loop(0, steps, step, 0)
    for i in range(max(0, steps - slots), steps):
        for n in range(count):
            store(i, n).wait()


def weight_grads(lefts, right, name):
    count = len(lefts)
    hidden, rows = lefts[0].shape
    depth = right.shape[1]
    chunk = chunk_of(depth, 512)
    slots = min(4, depth // chunk)
    return pl.pallas_call(
        functools.partial(weights_body, count, chunk),
        out_shape=[jax.ShapeDtypeStruct((hidden, depth), BF16)] * count,
        in_specs=[VMEM] * (count + 1),
        out_specs=[HBM] * count,
        scratch_shapes=[pltpu.VMEM((count, slots, hidden, chunk), BF16), pltpu.SemaphoreType.DMA((count, slots))],
        compiler_params=pltpu.CompilerParams(vmem_limit_bytes=24 * MIB),
        cost_estimate=pl.CostEstimate(
            flops=2 * count * rows * hidden * depth, bytes_accessed=2 * count * hidden * depth, transcendentals=0
        ),
        name=name,
    )(*lefts, right)


def fold_body(copies, keep_ref, got_ref, *outs):
    for d, out in enumerate(outs):
        rows = slice(d * 2 * SUBS, (d + 1) * 2 * SUBS)
        out[...] = keep_ref[rows, :] + got_ref[rows, :]


def fold(copies, keep, got):
    return pl.pallas_call(
        functools.partial(fold_body, copies),
        out_shape=[jax.ShapeDtypeStruct((2 * SUBS, keep.shape[1]), F32)] * copies,
        in_specs=[VMEM] * 2,
        out_specs=[VMEM] * copies,
        compiler_params=pltpu.CompilerParams(vmem_limit_bytes=6 * MIB),
        name="fold_cores",
    )(keep, got)


def merge_body(*refs):
    blocks, (mine_ref, other_ref) = refs[:-2], refs[-2:]
    for at, out in ((0, mine_ref), (SUBS, other_ref)):
        total = blocks[0][at : at + SUBS, :]
        for block in blocks[1:]:
            total += block[at : at + SUBS, :]
        out[...] = total


def merge(blocks):
    part = jax.ShapeDtypeStruct((SUBS, blocks[0].shape[1]), F32)
    return pl.pallas_call(
        merge_body,
        out_shape=(part, part),
        in_specs=[VMEM] * len(blocks),
        out_specs=[VMEM] * 2,
        compiler_params=pltpu.CompilerParams(vmem_limit_bytes=6 * MIB),
        name="merge_chips",
    )(*blocks)


def finish_body(e_ref, ids_ref, mine_ref, got_ref, tok_ref, gate_ref):
    ids = ids_ref[...]
    toks, width = tok_ref.shape
    half, eighth = width // 2, width // SUBS
    both = 2 * SUBS
    row = iota((both, toks), 0)
    sub = sub_row(both, toks)
    expert = jnp.where(row < SUBS, e_ref[0], 1 - e_ref[0])
    main, hits = chosen_rows(ids, expert, sub % WHOLE)
    tail, _ = chosen_rows(ids, expert, jnp.full((both, toks), WHOLE, jnp.int32))
    plain = jnp.where(sub < WHOLE, main, jnp.where(sub == WHOLE, tail, 0.0))
    data = jnp.concatenate([mine_ref[...], got_ref[...]], axis=0)
    tn = (((0,), (0,)), ((), ()))
    exact = dict(precision=lax.Precision.HIGHEST, preferred_element_type=F32)
    halves = [
        lax.dot_general(jnp.where(sub // WHOLE == h, main, 0.0), data[:, :half], tn, **exact) for h in range(2)
    ]
    for s in range(SUBS):
        last = lax.dot_general(jnp.where(sub == s, tail, 0.0), data[:, half : half + eighth], tn, **exact)
        h, at = divmod(s * eighth, half)
        tok_ref[:, s * eighth : (s + 1) * eighth] = (halves[h][:, at : at + eighth] + last).astype(BF16)
    term = plain * data[:, half + eighth : half + eighth + 1]
    for k, hit in enumerate(hits):
        gate_ref[k : k + 1, :] = jnp.sum(jnp.where(hit, term, 0.0), axis=0, keepdims=True)


def finish(e, ids_t, mine, got, width):
    top, toks = ids_t.shape
    return pl.pallas_call(
        finish_body,
        out_shape=(jax.ShapeDtypeStruct((toks, width), BF16), jax.ShapeDtypeStruct((top, toks), F32)),
        in_specs=[SMEM] + [VMEM] * 3,
        out_specs=[VMEM] * 2,
        compiler_params=pltpu.CompilerParams(vmem_limit_bytes=6 * MIB),
        name="finish_tokens",
    )(e, ids_t, mine, got)


def on_device(tokens, grad_out, expert_ids, gate_probs, w_gate, w_up, w_down):
    n_expert = lax.axis_size("expert")
    copies = n_expert // EXPERTS_ON
    place = lax.axis_index("expert")
    e = (place >= copies).astype(jnp.int32).reshape(1)
    t = lax.axis_index("tensor").astype(jnp.int32).reshape(1)
    width = tokens.shape[1]

    def partner(v):
        return lax.ppermute(v, "expert", [(i, (i + copies) % n_expert) for i in range(n_expert)])

    def across(v, d):
        return lax.ppermute(v, "expert", [(i, i ^ d) for i in range(n_expert)])

    def other_core(v):
        return lax.ppermute(v, "tensor", [(0, 1), (1, 0)])

    w_gate, w_up, w_down = (pltpu.with_memory_space_constraint(w, pltpu.HBM) for w in (w_gate, w_up, w_down))
    ids_t = expert_ids.T
    here = (pltpu.with_memory_space_constraint(v, pltpu.HBM) for v in (ids_t, gate_probs.T, tokens, grad_out))
    own, oth = pick(e, *here)
    far_first = sorted(range(1, copies), key=lambda d: (-d.bit_count(), d))
    got = partner(oth)
    first = {0: own} | {d: across(own, d) for d in far_first}
    second = {0: got} | {d: across(got, d) for d in far_first}
    mine = [piece for d in range(copies) for piece in (first[d], second[d])]
    theirs = [other_core(piece) for piece in mine]
    x, dh, du, give, keep, grad_w_down = expert_units(t, mine, theirs, w_gate, w_up, w_down, width)
    blocks = list(fold(copies, keep, other_core(give)))
    arrived = {d: across(blocks[d], d) for d in far_first}
    dh, local = lax.optimization_barrier((dh, blocks[0]))
    (grad_w_gate,) = weight_grads((dh,), x, "grad_gate")
    grad_w_gate, arrived = lax.optimization_barrier((grad_w_gate, arrived))
    kept, others = merge([local] + [arrived[d] for d in range(1, copies)])
    back = partner(others)
    du, kept = lax.optimization_barrier((du, kept))
    (grad_w_up,) = weight_grads((du,), x, "grad_up")
    grad_w_up, back = lax.optimization_barrier((grad_w_up, back))
    token_grad, gate_t = finish(e, ids_t, kept, back, width)
    return token_grad, gate_t.T, grad_w_gate, grad_w_up, grad_w_down


def solution(mesh):
    return jax.shard_map(
        on_device,
        mesh=mesh,
        in_specs=(
            P(("groups", "expert"), "tensor"),
            P(("groups", "expert"), "tensor"),
            P(("groups", "expert"), None),
            P(("groups", "expert"), None),
            P(("expert", "tensor"), None),
            P(("expert", "tensor"), None),
            P(("expert", "tensor"), None),
        ),
        out_specs=(
            P(("groups", "expert"), "tensor"),
            P(("groups", "expert"), None),
            P(("expert", "tensor"), "groups"),
            P(("expert", "tensor"), "groups"),
            P(("expert", "tensor"), "groups"),
        ),
        check_vma=False,
    )
```

```python
import functools

import jax
import jax.numpy as jnp
from jax import lax
from jax.experimental import pallas as pl
from jax.experimental.pallas import tpu as pltpu
from jax.sharding import PartitionSpec as P

EXPERTS_ON = 2
CAP = 5
LANES = 128
SUBS = 8
WHOLE = 4
F32 = jnp.float32
BF16 = jnp.bfloat16
MIB = 1 << 20
VMEM = pl.BlockSpec(memory_space=pltpu.VMEM)
SMEM = pl.BlockSpec(memory_space=pltpu.SMEM)
HBM = pl.BlockSpec(memory_space=pltpu.HBM)


def iota(shape, dim):
    return lax.broadcasted_iota(jnp.int32, shape, dim)


def chosen_rows(ids, expert, position):
    rows, toks = position.shape
    hits = [ids[k : k + 1, :] == expert for k in range(ids.shape[0])]
    member = functools.reduce(jnp.logical_or, hits).astype(F32)
    before = (iota((toks, toks), 0) < iota((toks, toks), 1)).astype(F32)
    earlier = jnp.dot(member, before, preferred_element_type=F32)
    return jnp.where(earlier == position.astype(F32), member, 0.0), hits


def sub_row(rows, toks):
    return iota((rows, toks), 0) % SUBS


def tile_of(hidden, most):
    sizes = [n for n in range(16, most + 1, 16) if hidden % n == 0]
    return max(sizes) if sizes else hidden


def pick_body(e_ref, ids_any, probs_any, tok_any, grad_any, own_ref, oth_ref, ids_ref, probs_ref, tok_ref, grad_ref, landed):
    copies = [
        pltpu.make_async_copy(src, dst, landed.at[n])
        for n, (src, dst) in enumerate(
            ((ids_any, ids_ref), (probs_any, probs_ref), (tok_any, tok_ref), (grad_any, grad_ref))
        )
    ]
    for copy in copies:
        copy.start()
    for copy in copies[:2]:
        copy.wait()
    ids = ids_ref[...]
    probs = probs_ref[...].astype(F32)
    toks, width = tok_ref.shape
    half, eighth = width // 2, width // SUBS
    size = half + eighth
    both = 2 * SUBS
    row = iota((both, toks), 0)
    sub = sub_row(both, toks)
    expert = jnp.where(row < SUBS, e_ref[0], 1 - e_ref[0])
    main, hits = chosen_rows(ids, expert, sub % WHOLE)
    tail, _ = chosen_rows(ids, expert, jnp.full((both, toks), WHOLE, jnp.int32))
    plain = jnp.where(sub < WHOLE, main, jnp.where(sub == WHOLE, tail, 0.0))
    halves = [jnp.where(sub // WHOLE == h, main, 0.0).astype(BF16) for h in range(2)]
    eighths = [jnp.where(sub == s, tail, 0.0).astype(BF16) for s in range(SUBS)]
    for at, src in enumerate((tok_ref, grad_ref)):
        copies[2 + at].wait()
        packed = sum(
            jnp.dot(one, src[:, h * half : (h + 1) * half], preferred_element_type=F32)
            for h, one in enumerate(halves)
        ).astype(BF16)
        last = sum(
            jnp.dot(one, src[:, s * eighth : (s + 1) * eighth], preferred_element_type=F32)
            for s, one in enumerate(eighths)
        ).astype(BF16)
        for n, dst in enumerate((own_ref, oth_ref)):
            dst[:, at * size : at * size + half] = packed[n * SUBS : (n + 1) * SUBS]
            dst[:, at * size + half : (at + 1) * size] = last[n * SUBS : (n + 1) * SUBS]
    weight = sum(jnp.where(hit, probs[k : k + 1, :], 0.0) for k, hit in enumerate(hits))
    gate = jnp.broadcast_to(jnp.sum(plain * weight, axis=1, keepdims=True), (both, LANES)).astype(BF16)
    for n, dst in enumerate((own_ref, oth_ref)):
        dst[:, 2 * size :] = gate[n * SUBS : (n + 1) * SUBS]


def pick(e, ids_t, probs_t, tokens, grad_out):
    width = tokens.shape[1]
    size = width // 2 + width // SUBS
    piece = jax.ShapeDtypeStruct((SUBS, 2 * size + LANES), BF16)
    return pl.pallas_call(
        pick_body,
        out_shape=(piece, piece),
        in_specs=[SMEM] + [HBM] * 4,
        out_specs=[VMEM] * 2,
        scratch_shapes=[pltpu.VMEM(v.shape, v.dtype) for v in (ids_t, probs_t, tokens, grad_out)]
        + [pltpu.SemaphoreType.DMA((4,))],
        compiler_params=pltpu.CompilerParams(vmem_limit_bytes=6 * MIB),
        name="pick_rows",
    )(e, ids_t, probs_t, tokens, grad_out)


NT = (((1,), (1,)), ((), ()))


def chunk_of(width, most):
    return max(n for n in range(LANES, most + 1, LANES) if width % n == 0)


def assemble(pieces, held, out, base, side):
    width = held.shape[1]
    half, eighth = width // 2, width // SUBS
    size = half + eighth
    for n, ref in enumerate(pieces):
        at = n * CAP
        piece = ref[:, side * size : (side + 1) * size].astype(F32)
        for h in range(2):
            held[at : at + WHOLE, h * half : (h + 1) * half] = piece[h * WHOLE : (h + 1) * WHOLE, :half]
        for s in range(SUBS):
            held[at + WHOLE : at + CAP, s * eighth : (s + 1) * eighth] = piece[s : s + 1, half:]
    out[:, pl.ds(base, width)] = held[...].astype(BF16)


def slot_of(n, pieces):
    if n < 2:
        return n
    far = pieces // 2 - 1
    return 2 * (n - 1) if n < 2 + far else 2 * (n - 1 - far) + 1


def pack(part, gates, out, pieces):
    width = part.shape[1]
    half, eighth = width // 2, width // SUBS
    size = half + eighth
    for n in range(pieces):
        at, to = n * CAP, slot_of(n, pieces) * SUBS
        for h in range(2):
            out[to + h * WHOLE : to + (h + 1) * WHOLE, :half] = part[at : at + WHOLE, h * half : (h + 1) * half]
        for s in range(SUBS):
            out[to + s : to + s + 1, half:size] = part[at + WHOLE : at + CAP, s * eighth : (s + 1) * eighth]
        out[to : to + CAP, size:] = gates[at : at + CAP, :]
        out[to + CAP : to + SUBS, size:] = jnp.zeros((SUBS - CAP, LANES), F32)


def stack_body(*refs):
    for n, ref in enumerate(refs[:-1]):
        refs[-1][n] = ref[...]


def stack(pieces, name):
    return pl.pallas_call(
        stack_body,
        out_shape=jax.ShapeDtypeStruct((len(pieces),) + pieces[0].shape, BF16),
        in_specs=[VMEM] * len(pieces),
        out_specs=VMEM,
        compiler_params=pltpu.CompilerParams(vmem_limit_bytes=6 * MIB),
        name=name,
    )(*pieces)


def experts_body(pieces, chunk, ahead, t_ref, *refs):
    mine, (early, late) = refs[:pieces], refs[pieces : pieces + 2]
    theirs = [early.at[n] for n in range(early.shape[0])] + [late.at[n] for n in range(late.shape[0])]
    (wg_hbm, wu_hbm, wd_hbm, x_ref, dh_ref, du_ref, give_ref, keep_ref, down_ref,
     wg_ref, wu_ref, ring, g_ref, wt_ref, h_ref, u_ref, da_ref, dhr_ref, dur_ref, acc,
     held, factor, landed, ring_landed, sent) = refs[pieces + 2 :]
    rows, depth = x_ref.shape
    hidden = wg_ref.shape[0]
    width = depth // 2
    slots = ring.shape[0]
    steps = depth // chunk
    t = t_ref[0]

    def columns(i):
        return pl.ds(pl.multiple_of(i * chunk, chunk), chunk)

    def load(i, n):
        src, dst = ((wg_hbm, wg_ref), (wu_hbm, wu_ref))[n]
        return pltpu.make_async_copy(src.at[:, columns(i)], dst.at[:, columns(i)], landed.at[i, n])

    def load_down(i):
        slot = lax.rem(i, slots)
        return pltpu.make_async_copy(wd_hbm.at[:, columns(i)], ring.at[slot], ring_landed.at[slot])

    def start(i):
        load(i, 0).start()
        load(i, 1).start()
        load_down(i).start()

    start(0)
    held[...] = jnp.zeros_like(held)
    factor[...] = jnp.zeros_like(factor)
    for n, ref in enumerate(mine):
        factor[n * CAP : (n + 1) * CAP, :] = ref[:CAP, ref.shape[1] - LANES :].astype(F32)
    for side, out in enumerate((x_ref, g_ref)):
        for group, at in ((mine, t), (theirs, 1 - t)):
            assemble(group, held, out, pl.multiple_of(at * width, width), side)
    for i in range(1, min(ahead, steps)):
        start(i)

    def three(i):
        cols = columns(i)
        x = x_ref[:, cols]
        return (
            lambda: lax.dot_general(wg_ref[:, cols], x, NT, preferred_element_type=F32),
            lambda: lax.dot_general(wu_ref[:, cols], x, NT, preferred_element_type=F32),
            lambda: lax.dot_general(ring[lax.rem(i, slots)], g_ref[:, cols], NT, preferred_element_type=F32),
        )

    sums = (h_ref, u_ref, da_ref)
    waits = lambda i: (load(i, 0), load(i, 1), load_down(i))
    for wait, dot, out in zip(waits(0), three(0), sums):
        wait.wait()
        out[...] = dot()

    def up_step(i, carry):
        @pl.when(i + ahead - 1 < steps)
        def _():
            start(i + ahead - 1)

        for wait in waits(i):
            wait.wait()
        for dot, out in zip(three(i), sums):
            out[...] += dot()
        return carry

    lax.fori_loop(1, steps, up_step, 0)

    weight = factor[...].T[:1, :]

    def units(start, size, total):
        at = pl.ds(start, size)
        h = h_ref[at, :]
        u = u_ref[at, :]
        da = da_ref[at, :]
        sigma = 1.0 / (1.0 + jnp.exp(-h))
        silu = h * sigma
        act = silu * u
        scaled = weight * da
        wt_ref[at, :] = (weight * act).astype(BF16)
        dh = scaled * u * sigma * (1.0 + h * (1.0 - sigma))
        du = scaled * silu
        dh_ref[at, :] = dh.astype(BF16)
        du_ref[at, :] = du.astype(BF16)
        dhr_ref[:, at] = dh.T.astype(BF16)
        dur_ref[:, at] = du.T.astype(BF16)
        return total + jnp.sum(act * da, axis=0, keepdims=True)

    total = jnp.zeros((1, rows), F32)
    for begin in range(0, hidden, LANES):
        total = units(begin, min(LANES, hidden - begin), total)
    gates = jnp.broadcast_to(total, (LANES, rows)).T
    tile = tile_of(hidden, 448)
    leaving = []
    for i in range(steps):
        cols = pl.ds(i * chunk, chunk)
        acc[:, cols] = jnp.dot(dhr_ref[...], wg_ref[:, cols], preferred_element_type=F32) + jnp.dot(
            dur_ref[...], wu_ref[:, cols], preferred_element_type=F32
        )
        room = wg_ref.at[:, pl.ds((i - 1) * chunk, chunk)] if i else ring.at[0]
        for at in range(0, hidden, tile):
            room[at : at + tile, :] = jnp.dot(
                wt_ref[at : at + tile, :], g_ref[:, cols], preferred_element_type=F32
            ).astype(BF16)
        leaving.append(pltpu.make_async_copy(room, down_ref.at[:, cols], sent.at[i]))
        leaving[-1].start()
    for at, out in ((1 - t, give_ref), (t, keep_ref)):
        held[...] = acc[:, pl.ds(pl.multiple_of(at * width, width), width)]
        pack(held, gates, out, pieces)
    for copy in leaving:
        copy.wait()


def expert_units(t, mine, early, late, w_gate, w_up, w_down, width):
    hidden, depth = w_gate.shape
    pieces = len(mine)
    rows = -(-pieces * CAP // 16) * 16
    chunk = chunk_of(width, 768)
    steps = depth // chunk
    ahead = 3
    slots = 4
    unit = jax.ShapeDtypeStruct((hidden, rows), BF16)
    packed = jax.ShapeDtypeStruct((pieces * SUBS, width // 2 + width // SUBS + LANES), F32)
    return pl.pallas_call(
        functools.partial(experts_body, pieces, chunk, ahead),
        out_shape=(
            jax.ShapeDtypeStruct((rows, depth), BF16),
            unit,
            unit,
            packed,
            packed,
            jax.ShapeDtypeStruct((hidden, depth), BF16),
        ),
        in_specs=[SMEM] + [VMEM] * (pieces + 2) + [HBM] * 3,
        out_specs=[VMEM] * 5 + [HBM],
        scratch_shapes=[
            pltpu.VMEM((hidden, depth), BF16),
            pltpu.VMEM((hidden, depth), BF16),
            pltpu.VMEM((slots, hidden, chunk), BF16),
            pltpu.VMEM((rows, depth), BF16),
            pltpu.VMEM((hidden, rows), BF16),
            pltpu.VMEM((hidden, rows), F32),
            pltpu.VMEM((hidden, rows), F32),
            pltpu.VMEM((hidden, rows), F32),
            pltpu.VMEM((rows, hidden), BF16),
            pltpu.VMEM((rows, hidden), BF16),
            pltpu.VMEM((rows, depth), F32),
            pltpu.VMEM((rows, width), F32),
            pltpu.VMEM((rows, LANES), F32),
            pltpu.SemaphoreType.DMA((steps, 2)),
            pltpu.SemaphoreType.DMA((slots,)),
            pltpu.SemaphoreType.DMA((steps,)),
        ],
        compiler_params=pltpu.CompilerParams(vmem_limit_bytes=50 * MIB),
        cost_estimate=pl.CostEstimate(
            flops=12 * rows * hidden * depth, bytes_accessed=8 * hidden * depth, transcendentals=rows * hidden
        ),
        name="expert_units",
    )(t, *mine, early, late, w_gate, w_up, w_down)


def weights_body(chunk, left_ref, x_ref, out_ref, room, sent):
    hidden = left_ref.shape[0]
    steps = x_ref.shape[1] // chunk
    tile = tile_of(hidden, 448)
    leaving = []
    for i in range(steps):
        cols = pl.ds(i * chunk, chunk)
        for at in range(0, hidden, tile):
            room[i, at : at + tile, :] = jnp.dot(
                left_ref[at : at + tile, :], x_ref[:, cols], preferred_element_type=F32
            ).astype(BF16)
        leaving.append(pltpu.make_async_copy(room.at[i], out_ref.at[:, cols], sent.at[i]))
        leaving[-1].start()
    for copy in leaving:
        copy.wait()


def weight_grad(left, right, name):
    hidden, rows = left.shape
    depth = right.shape[1]
    chunk = chunk_of(depth, 768)
    steps = depth // chunk
    return pl.pallas_call(
        functools.partial(weights_body, chunk),
        out_shape=jax.ShapeDtypeStruct((hidden, depth), BF16),
        in_specs=[VMEM] * 2,
        out_specs=HBM,
        scratch_shapes=[pltpu.VMEM((steps, hidden, chunk), BF16), pltpu.SemaphoreType.DMA((steps,))],
        compiler_params=pltpu.CompilerParams(vmem_limit_bytes=28 * MIB),
        cost_estimate=pl.CostEstimate(
            flops=2 * rows * hidden * depth, bytes_accessed=2 * hidden * depth, transcendentals=0
        ),
        name=name,
    )(left, right)


def fold_body(copies, keep_ref, got_ref, *outs):
    for d, out in enumerate(outs):
        rows = slice(d * 2 * SUBS, (d + 1) * 2 * SUBS)
        out[...] = keep_ref[rows, :] + got_ref[rows, :]


def fold(copies, keep, got):
    return pl.pallas_call(
        functools.partial(fold_body, copies),
        out_shape=[jax.ShapeDtypeStruct((2 * SUBS, keep.shape[1]), F32)] * copies,
        in_specs=[VMEM] * 2,
        out_specs=[VMEM] * copies,
        compiler_params=pltpu.CompilerParams(vmem_limit_bytes=6 * MIB),
        name="fold_cores",
    )(keep, got)


def merge_body(*refs):
    blocks, (mine_ref, other_ref) = refs[:-2], refs[-2:]
    for at, out in ((0, mine_ref), (SUBS, other_ref)):
        total = blocks[0][at : at + SUBS, :]
        for block in blocks[1:]:
            total += block[at : at + SUBS, :]
        out[...] = total


def merge(blocks):
    part = jax.ShapeDtypeStruct((SUBS, blocks[0].shape[1]), F32)
    return pl.pallas_call(
        merge_body,
        out_shape=(part, part),
        in_specs=[VMEM] * len(blocks),
        out_specs=[VMEM] * 2,
        compiler_params=pltpu.CompilerParams(vmem_limit_bytes=6 * MIB),
        name="merge_chips",
    )(*blocks)


def finish_body(e_ref, ids_ref, mine_ref, got_ref, tok_ref, gate_ref):
    ids = ids_ref[...]
    toks, width = tok_ref.shape
    half, eighth = width // 2, width // SUBS
    both = 2 * SUBS
    row = iota((both, toks), 0)
    sub = sub_row(both, toks)
    expert = jnp.where(row < SUBS, e_ref[0], 1 - e_ref[0])
    main, hits = chosen_rows(ids, expert, sub % WHOLE)
    tail, _ = chosen_rows(ids, expert, jnp.full((both, toks), WHOLE, jnp.int32))
    plain = jnp.where(sub < WHOLE, main, jnp.where(sub == WHOLE, tail, 0.0))
    data = jnp.concatenate([mine_ref[...], got_ref[...]], axis=0)
    tn = (((0,), (0,)), ((), ()))
    exact = dict(precision=lax.Precision.HIGHEST, preferred_element_type=F32)
    halves = [
        lax.dot_general(jnp.where(sub // WHOLE == h, main, 0.0), data[:, :half], tn, **exact) for h in range(2)
    ]
    for s in range(SUBS):
        last = lax.dot_general(jnp.where(sub == s, tail, 0.0), data[:, half : half + eighth], tn, **exact)
        h, at = divmod(s * eighth, half)
        tok_ref[:, s * eighth : (s + 1) * eighth] = (halves[h][:, at : at + eighth] + last).astype(BF16)
    term = plain * data[:, half + eighth : half + eighth + 1]
    for k, hit in enumerate(hits):
        gate_ref[k : k + 1, :] = jnp.sum(jnp.where(hit, term, 0.0), axis=0, keepdims=True)


def finish(e, ids_t, mine, got, width):
    top, toks = ids_t.shape
    return pl.pallas_call(
        finish_body,
        out_shape=(jax.ShapeDtypeStruct((toks, width), BF16), jax.ShapeDtypeStruct((top, toks), F32)),
        in_specs=[SMEM] + [VMEM] * 3,
        out_specs=[VMEM] * 2,
        compiler_params=pltpu.CompilerParams(vmem_limit_bytes=6 * MIB),
        name="finish_tokens",
    )(e, ids_t, mine, got)


def on_device(tokens, grad_out, expert_ids, gate_probs, w_gate, w_up, w_down):
    n_expert = lax.axis_size("expert")
    copies = n_expert // EXPERTS_ON
    place = lax.axis_index("expert")
    e = (place >= copies).astype(jnp.int32).reshape(1)
    t = lax.axis_index("tensor").astype(jnp.int32).reshape(1)
    width = tokens.shape[1]

    def partner(v):
        return lax.ppermute(v, "expert", [(i, (i + copies) % n_expert) for i in range(n_expert)])

    def across(v, d):
        return lax.ppermute(v, "expert", [(i, i ^ d) for i in range(n_expert)])

    def other_core(v):
        return lax.ppermute(v, "tensor", [(0, 1), (1, 0)])

    w_gate, w_up, w_down = (pltpu.with_memory_space_constraint(w, pltpu.HBM) for w in (w_gate, w_up, w_down))
    ids_t = expert_ids.T
    here = (pltpu.with_memory_space_constraint(v, pltpu.HBM) for v in (ids_t, gate_probs.T, tokens, grad_out))
    own, oth = pick(e, *here)
    far_first = sorted(range(1, copies), key=lambda d: (-d.bit_count(), d))
    got = partner(oth)
    first = {0: own} | {d: across(own, d) for d in far_first}
    second = {0: got} | {d: across(got, d) for d in far_first}
    early = [own, got] + [first[d] for d in range(1, copies)]
    late = [second[d] for d in range(1, copies)]
    if late:
        early, late[far_first[0] - 1] = lax.optimization_barrier((early, late[far_first[0] - 1]))
    early_there = other_core(stack(early, "stack_early"))
    late_there = other_core(stack(late, "stack_late"))
    x, dh, du, give, keep, grad_w_down = expert_units(
        t, early + late, early_there, late_there, w_gate, w_up, w_down, width
    )
    blocks = list(fold(copies, keep, other_core(give)))
    arrived = {d: across(blocks[d], d) for d in far_first}
    dh, local = lax.optimization_barrier((dh, blocks[0]))
    grad_w_gate = weight_grad(dh, x, "grad_gate")
    grad_w_gate, arrived = lax.optimization_barrier((grad_w_gate, arrived))
    kept, others = merge([local] + [arrived[d] for d in range(1, copies)])
    back = partner(others)
    du, kept = lax.optimization_barrier((du, kept))
    grad_w_up = weight_grad(du, x, "grad_up")
    grad_w_up, back = lax.optimization_barrier((grad_w_up, back))
    token_grad, gate_t = finish(e, ids_t, kept, back, width)
    return token_grad, gate_t.T, grad_w_gate, grad_w_up, grad_w_down


def solution(mesh):
    return jax.shard_map(
        on_device,
        mesh=mesh,
        in_specs=(
            P(("groups", "expert"), "tensor"),
            P(("groups", "expert"), "tensor"),
            P(("groups", "expert"), None),
            P(("groups", "expert"), None),
            P(("expert", "tensor"), None),
            P(("expert", "tensor"), None),
            P(("expert", "tensor"), None),
        ),
        out_specs=(
            P(("groups", "expert"), "tensor"),
            P(("groups", "expert"), None),
            P(("expert", "tensor"), "groups"),
            P(("expert", "tensor"), "groups"),
            P(("expert", "tensor"), "groups"),
        ),
        check_vma=False,
    )
```

```python
import functools

import jax
import jax.numpy as jnp
from jax import lax
from jax.experimental import pallas as pl
from jax.experimental.pallas import tpu as pltpu
from jax.sharding import PartitionSpec as P

EXPERTS_ON = 2
CAP = 5
LANES = 128
SUBS = 8
WHOLE = 4
F32 = jnp.float32
BF16 = jnp.bfloat16
MIB = 1 << 20
BLOCK = 384
VMEM = pl.BlockSpec(memory_space=pltpu.VMEM)
SMEM = pl.BlockSpec(memory_space=pltpu.SMEM)
HBM = pl.BlockSpec(memory_space=pltpu.HBM)


def iota(shape, dim):
    return lax.broadcasted_iota(jnp.int32, shape, dim)


def chosen_rows(ids, expert, position):
    rows, toks = position.shape
    hits = [ids[k : k + 1, :] == expert for k in range(ids.shape[0])]
    member = functools.reduce(jnp.logical_or, hits).astype(F32)
    before = (iota((toks, toks), 0) < iota((toks, toks), 1)).astype(F32)
    earlier = jnp.dot(member, before, preferred_element_type=F32)
    return jnp.where(earlier == position.astype(F32), member, 0.0), hits


def sub_row(rows, toks):
    return iota((rows, toks), 0) % SUBS


def tile_of(hidden, most):
    sizes = [n for n in range(16, most + 1, 16) if hidden % n == 0]
    return max(sizes) if sizes else hidden


def pick_body(e_ref, ids_any, probs_any, tok_any, grad_any, own_ref, oth_ref, ids_ref, probs_ref, tok_ref, grad_ref, landed):
    copies = [
        pltpu.make_async_copy(src, dst, landed.at[n])
        for n, (src, dst) in enumerate(
            ((ids_any, ids_ref), (probs_any, probs_ref), (tok_any, tok_ref), (grad_any, grad_ref))
        )
    ]
    for copy in copies:
        copy.start()
    for copy in copies[:2]:
        copy.wait()
    ids = ids_ref[...]
    probs = probs_ref[...].astype(F32)
    toks, width = tok_ref.shape
    half, eighth = width // 2, width // SUBS
    size = half + eighth
    both = 2 * SUBS
    row = iota((both, toks), 0)
    sub = sub_row(both, toks)
    expert = jnp.where(row < SUBS, e_ref[0], 1 - e_ref[0])
    main, hits = chosen_rows(ids, expert, sub % WHOLE)
    tail, _ = chosen_rows(ids, expert, jnp.full((both, toks), WHOLE, jnp.int32))
    plain = jnp.where(sub < WHOLE, main, jnp.where(sub == WHOLE, tail, 0.0))
    halves = [jnp.where(sub // WHOLE == h, main, 0.0).astype(BF16) for h in range(2)]
    eighths = [jnp.where(sub == s, tail, 0.0).astype(BF16) for s in range(SUBS)]
    for at, src in enumerate((tok_ref, grad_ref)):
        copies[2 + at].wait()
        packed = sum(
            jnp.dot(one, src[:, h * half : (h + 1) * half], preferred_element_type=F32)
            for h, one in enumerate(halves)
        ).astype(BF16)
        last = sum(
            jnp.dot(one, src[:, s * eighth : (s + 1) * eighth], preferred_element_type=F32)
            for s, one in enumerate(eighths)
        ).astype(BF16)
        for n, dst in enumerate((own_ref, oth_ref)):
            dst[:, at * size : at * size + half] = packed[n * SUBS : (n + 1) * SUBS]
            dst[:, at * size + half : (at + 1) * size] = last[n * SUBS : (n + 1) * SUBS]
    weight = sum(jnp.where(hit, probs[k : k + 1, :], 0.0) for k, hit in enumerate(hits))
    gate = jnp.broadcast_to(jnp.sum(plain * weight, axis=1, keepdims=True), (both, LANES)).astype(BF16)
    for n, dst in enumerate((own_ref, oth_ref)):
        dst[:, 2 * size :] = gate[n * SUBS : (n + 1) * SUBS]


def pick(e, ids_t, probs_t, tokens, grad_out):
    width = tokens.shape[1]
    size = width // 2 + width // SUBS
    piece = jax.ShapeDtypeStruct((SUBS, 2 * size + LANES), BF16)
    return pl.pallas_call(
        pick_body,
        out_shape=(piece, piece),
        in_specs=[SMEM] + [HBM] * 4,
        out_specs=[VMEM] * 2,
        scratch_shapes=[pltpu.VMEM(v.shape, v.dtype) for v in (ids_t, probs_t, tokens, grad_out)]
        + [pltpu.SemaphoreType.DMA((4,))],
        compiler_params=pltpu.CompilerParams(vmem_limit_bytes=6 * MIB),
        name="pick_rows",
    )(e, ids_t, probs_t, tokens, grad_out)


NT = (((1,), (1,)), ((), ()))


def chunk_of(width, most):
    return max(n for n in range(LANES, most + 1, LANES) if width % n == 0)


def place_of(step, chunks, chunk, t):
    side = t if step < chunks else 1 - t
    return pl.multiple_of(side * (chunks * chunk) + step % chunks * chunk, chunk)


def assemble(pieces, held, out, base, side):
    width = held.shape[1]
    half, eighth = width // 2, width // SUBS
    size = half + eighth
    for n, ref in enumerate(pieces):
        at = n * CAP
        piece = ref[:, side * size : (side + 1) * size].astype(F32)
        for h in range(2):
            held[at : at + WHOLE, h * half : (h + 1) * half] = piece[h * WHOLE : (h + 1) * WHOLE, :half]
        for s in range(SUBS):
            held[at + WHOLE : at + CAP, s * eighth : (s + 1) * eighth] = piece[s : s + 1, half:]
    out[:, pl.ds(base, width)] = held[...].astype(BF16)


def pack(part, gates, out, pieces):
    width = part.shape[1]
    half, eighth = width // 2, width // SUBS
    size = half + eighth
    for n in range(pieces):
        at, to = n * CAP, n * SUBS
        for h in range(2):
            out[to + h * WHOLE : to + (h + 1) * WHOLE, :half] = part[at : at + WHOLE, h * half : (h + 1) * half]
        for s in range(SUBS):
            out[to + s : to + s + 1, half:size] = part[at + WHOLE : at + CAP, s * eighth : (s + 1) * eighth]
        out[to : to + CAP, size:] = gates[at : at + CAP, :]
        out[to + CAP : to + SUBS, size:] = jnp.zeros((SUBS - CAP, LANES), F32)


def stack_body(*refs):
    for n, ref in enumerate(refs[:-1]):
        refs[-1][n] = ref[...]


def stack(pieces, name):
    return pl.pallas_call(
        stack_body,
        out_shape=jax.ShapeDtypeStruct((len(pieces),) + pieces[0].shape, BF16),
        in_specs=[VMEM] * len(pieces),
        out_specs=VMEM,
        compiler_params=pltpu.CompilerParams(vmem_limit_bytes=6 * MIB),
        name=name,
    )(*pieces)


def experts_body(pieces, chunk, ahead, t_ref, *refs):
    mine = refs[:pieces]
    theirs = [refs[pieces].at[n] for n in range(pieces)]
    (wg_hbm, wu_hbm, wd_hbm, x_ref, dh_ref, du_ref, give_ref, keep_ref, down_ref,
     wg_ref, wu_ref, ring, g_ref, wt_ref, h_ref, u_ref, da_ref, dhr_ref, dur_ref, parts,
     held, factor, landed, ring_landed, sent) = refs[pieces + 1 :]
    rows, depth = x_ref.shape
    hidden = wg_ref.shape[0]
    width = depth // 2
    slots = ring.shape[0]
    steps = depth // chunk
    t = t_ref[0]

    def columns(i):
        return pl.ds(pl.multiple_of(i * chunk, chunk), chunk)

    def load(i, n):
        src, dst = ((wg_hbm, wg_ref), (wu_hbm, wu_ref))[n]
        return pltpu.make_async_copy(src.at[:, columns(i)], dst.at[:, columns(i)], landed.at[i, n])

    def load_down(i):
        slot = lax.rem(i, slots)
        return pltpu.make_async_copy(wd_hbm.at[:, columns(i)], ring.at[slot], ring_landed.at[slot])

    def start(i):
        load(i, 0).start()
        load(i, 1).start()
        load_down(i).start()

    start(0)
    held[...] = jnp.zeros_like(held)
    factor[...] = jnp.zeros_like(factor)
    for n, ref in enumerate(mine):
        factor[n * CAP : (n + 1) * CAP, :] = ref[:CAP, ref.shape[1] - LANES :].astype(F32)
    for side, out in enumerate((x_ref, g_ref)):
        for group, at in ((mine, t), (theirs, 1 - t)):
            assemble(group, held, out, pl.multiple_of(at * width, width), side)
    for i in range(1, min(ahead, steps)):
        start(i)

    def three(i):
        cols = columns(i)
        x = x_ref[:, cols]
        return (
            lambda: lax.dot_general(wg_ref[:, cols], x, NT, preferred_element_type=F32),
            lambda: lax.dot_general(wu_ref[:, cols], x, NT, preferred_element_type=F32),
            lambda: lax.dot_general(ring[lax.rem(i, slots)], g_ref[:, cols], NT, preferred_element_type=F32),
        )

    sums = (h_ref, u_ref, da_ref)
    waits = lambda i: (load(i, 0), load(i, 1), load_down(i))
    for wait, dot, out in zip(waits(0), three(0), sums):
        wait.wait()
        out[...] = dot()

    def up_step(i, carry):
        @pl.when(i + ahead - 1 < steps)
        def _():
            start(i + ahead - 1)

        for wait in waits(i):
            wait.wait()
        for dot, out in zip(three(i), sums):
            out[...] += dot()
        return carry

    lax.fori_loop(1, steps - 1, up_step, 0)

    weight = factor[...].T[:1, :]

    def units(begin, h, u, da):
        at = pl.ds(begin, h.shape[0])
        sigma = 1.0 / (1.0 + jnp.exp(-h))
        silu = h * sigma
        act = silu * u
        scaled = weight * da
        wt_ref[at, :] = (weight * act).astype(BF16)
        dh = scaled * u * sigma * (1.0 + h * (1.0 - sigma))
        du = scaled * silu
        dh_ref[at, :] = dh.astype(BF16)
        du_ref[at, :] = du.astype(BF16)
        dhr_ref[:, at] = dh.T.astype(BF16)
        dur_ref[:, at] = du.T.astype(BF16)
        return jnp.sum(act * da, axis=0, keepdims=True)

    last = steps - 1
    cols = pl.ds(last * chunk, chunk)
    for wait in waits(last):
        wait.wait()
    total = jnp.zeros((1, rows), F32)
    for begin in range(0, hidden, BLOCK):
        end = min(begin + BLOCK, hidden)
        h, u, da = (
            out[begin:end, :] + lax.dot_general(w, v[:, cols], NT, preferred_element_type=F32)
            for out, w, v in (
                (h_ref, wg_ref[begin:end, cols], x_ref),
                (u_ref, wu_ref[begin:end, cols], x_ref),
                (da_ref, ring[last % slots, begin:end, :], g_ref),
            )
        )
        for at in range(0, end - begin, LANES):
            part = slice(at, min(at + LANES, end - begin))
            total += units(begin + at, h[part], u[part], da[part])
    gates = jnp.broadcast_to(total, (LANES, rows)).T
    tile = tile_of(hidden, 448)
    half = steps // 2
    leaving = []
    for i in range(steps):
        side, c = divmod(i, half)
        cols = pl.ds(place_of(i, half, chunk, 1 - t), chunk)
        parts[side, :, c * chunk : (c + 1) * chunk] = jnp.dot(
            dhr_ref[...], wg_ref[:, cols], preferred_element_type=F32
        ) + jnp.dot(dur_ref[...], wu_ref[:, cols], preferred_element_type=F32)
        if i >= slots:
            leaving[i - slots].wait()
        room = ring.at[i % slots]
        for at in range(0, hidden, tile):
            room[at : at + tile, :] = jnp.dot(
                wt_ref[at : at + tile, :], g_ref[:, cols], preferred_element_type=F32
            ).astype(BF16)
        leaving.append(pltpu.make_async_copy(room, down_ref.at[:, cols], sent.at[i]))
        leaving[-1].start()
        if c == half - 1:
            pack(parts.at[side], gates, (give_ref, keep_ref)[side], pieces)
    for copy in leaving[-slots:]:
        copy.wait()


def expert_units(t, mine, theirs, w_gate, w_up, w_down, width):
    hidden, depth = w_gate.shape
    pieces = len(mine)
    rows = -(-pieces * CAP // 16) * 16
    chunk = chunk_of(width, 768)
    steps = depth // chunk
    ahead = 3
    slots = min(5, steps)
    unit = jax.ShapeDtypeStruct((hidden, rows), BF16)
    packed = jax.ShapeDtypeStruct((pieces * SUBS, width // 2 + width // SUBS + LANES), F32)
    return pl.pallas_call(
        functools.partial(experts_body, pieces, chunk, ahead),
        out_shape=(
            jax.ShapeDtypeStruct((rows, depth), BF16),
            unit,
            unit,
            packed,
            packed,
            jax.ShapeDtypeStruct((hidden, depth), BF16),
        ),
        in_specs=[SMEM] + [VMEM] * (pieces + 1) + [HBM] * 3,
        out_specs=[VMEM] * 5 + [HBM],
        scratch_shapes=[
            pltpu.VMEM((hidden, depth), BF16),
            pltpu.VMEM((hidden, depth), BF16),
            pltpu.VMEM((slots, hidden, chunk), BF16),
            pltpu.VMEM((rows, depth), BF16),
            pltpu.VMEM((hidden, rows), BF16),
            pltpu.VMEM((hidden, rows), F32),
            pltpu.VMEM((hidden, rows), F32),
            pltpu.VMEM((hidden, rows), F32),
            pltpu.VMEM((rows, hidden), BF16),
            pltpu.VMEM((rows, hidden), BF16),
            pltpu.VMEM((2, rows, width), F32),
            pltpu.VMEM((rows, width), F32),
            pltpu.VMEM((rows, LANES), F32),
            pltpu.SemaphoreType.DMA((steps, 2)),
            pltpu.SemaphoreType.DMA((slots,)),
            pltpu.SemaphoreType.DMA((steps,)),
        ],
        compiler_params=pltpu.CompilerParams(vmem_limit_bytes=50 * MIB),
        cost_estimate=pl.CostEstimate(
            flops=12 * rows * hidden * depth, bytes_accessed=8 * hidden * depth, transcendentals=rows * hidden
        ),
        name="expert_units",
    )(t, *mine, theirs, w_gate, w_up, w_down)


def weights_body(chunk, left_ref, x_ref, out_ref, room, sent):
    hidden = left_ref.shape[0]
    steps = x_ref.shape[1] // chunk
    tile = tile_of(hidden, 448)
    leaving = []
    for i in range(steps):
        cols = pl.ds(i * chunk, chunk)
        for at in range(0, hidden, tile):
            room[i, at : at + tile, :] = jnp.dot(
                left_ref[at : at + tile, :], x_ref[:, cols], preferred_element_type=F32
            ).astype(BF16)
        leaving.append(pltpu.make_async_copy(room.at[i], out_ref.at[:, cols], sent.at[i]))
        leaving[-1].start()
    for copy in leaving:
        copy.wait()


def weight_grad(left, right, name):
    hidden, rows = left.shape
    depth = right.shape[1]
    chunk = chunk_of(depth, 768)
    steps = depth // chunk
    return pl.pallas_call(
        functools.partial(weights_body, chunk),
        out_shape=jax.ShapeDtypeStruct((hidden, depth), BF16),
        in_specs=[VMEM] * 2,
        out_specs=HBM,
        scratch_shapes=[pltpu.VMEM((steps, hidden, chunk), BF16), pltpu.SemaphoreType.DMA((steps,))],
        compiler_params=pltpu.CompilerParams(vmem_limit_bytes=28 * MIB),
        cost_estimate=pl.CostEstimate(
            flops=2 * rows * hidden * depth, bytes_accessed=2 * hidden * depth, transcendentals=0
        ),
        name=name,
    )(left, right)


def fold_body(copies, keep_ref, got_ref, *outs):
    for d, out in enumerate(outs):
        rows = slice(d * 2 * SUBS, (d + 1) * 2 * SUBS)
        out[...] = keep_ref[rows, :] + got_ref[rows, :]


def fold(copies, keep, got):
    return pl.pallas_call(
        functools.partial(fold_body, copies),
        out_shape=[jax.ShapeDtypeStruct((2 * SUBS, keep.shape[1]), F32)] * copies,
        in_specs=[VMEM] * 2,
        out_specs=[VMEM] * copies,
        compiler_params=pltpu.CompilerParams(vmem_limit_bytes=6 * MIB),
        name="fold_cores",
    )(keep, got)


def merge_body(*refs):
    blocks, (mine_ref, other_ref) = refs[:-2], refs[-2:]
    for at, out in ((0, mine_ref), (SUBS, other_ref)):
        total = blocks[0][at : at + SUBS, :]
        for block in blocks[1:]:
            total += block[at : at + SUBS, :]
        out[...] = total


def merge(blocks):
    part = jax.ShapeDtypeStruct((SUBS, blocks[0].shape[1]), F32)
    return pl.pallas_call(
        merge_body,
        out_shape=(part, part),
        in_specs=[VMEM] * len(blocks),
        out_specs=[VMEM] * 2,
        compiler_params=pltpu.CompilerParams(vmem_limit_bytes=6 * MIB),
        name="merge_chips",
    )(*blocks)


def finish_body(e_ref, ids_ref, mine_ref, got_ref, tok_ref, gate_ref):
    ids = ids_ref[...]
    toks, width = tok_ref.shape
    half, eighth = width // 2, width // SUBS
    both = 2 * SUBS
    row = iota((both, toks), 0)
    sub = sub_row(both, toks)
    expert = jnp.where(row < SUBS, e_ref[0], 1 - e_ref[0])
    main, hits = chosen_rows(ids, expert, sub % WHOLE)
    tail, _ = chosen_rows(ids, expert, jnp.full((both, toks), WHOLE, jnp.int32))
    plain = jnp.where(sub < WHOLE, main, jnp.where(sub == WHOLE, tail, 0.0))
    data = jnp.concatenate([mine_ref[...], got_ref[...]], axis=0)
    tn = (((0,), (0,)), ((), ()))
    exact = dict(precision=lax.Precision.HIGHEST, preferred_element_type=F32)
    halves = [
        lax.dot_general(jnp.where(sub // WHOLE == h, main, 0.0), data[:, :half], tn, **exact) for h in range(2)
    ]
    for s in range(SUBS):
        last = lax.dot_general(jnp.where(sub == s, tail, 0.0), data[:, half : half + eighth], tn, **exact)
        h, at = divmod(s * eighth, half)
        tok_ref[:, s * eighth : (s + 1) * eighth] = (halves[h][:, at : at + eighth] + last).astype(BF16)
    term = plain * data[:, half + eighth : half + eighth + 1]
    for k, hit in enumerate(hits):
        gate_ref[k : k + 1, :] = jnp.sum(jnp.where(hit, term, 0.0), axis=0, keepdims=True)


def finish(e, ids_t, mine, got, width):
    top, toks = ids_t.shape
    return pl.pallas_call(
        finish_body,
        out_shape=(jax.ShapeDtypeStruct((toks, width), BF16), jax.ShapeDtypeStruct((top, toks), F32)),
        in_specs=[SMEM] + [VMEM] * 3,
        out_specs=[VMEM] * 2,
        compiler_params=pltpu.CompilerParams(vmem_limit_bytes=6 * MIB),
        name="finish_tokens",
    )(e, ids_t, mine, got)


def on_device(tokens, grad_out, expert_ids, gate_probs, w_gate, w_up, w_down):
    n_expert = lax.axis_size("expert")
    copies = n_expert // EXPERTS_ON
    place = lax.axis_index("expert")
    e = (place >= copies).astype(jnp.int32).reshape(1)
    t = lax.axis_index("tensor").astype(jnp.int32).reshape(1)
    width = tokens.shape[1]

    def partner(v):
        return lax.ppermute(v, "expert", [(i, (i + copies) % n_expert) for i in range(n_expert)])

    def across(v, d):
        return lax.ppermute(v, "expert", [(i, i ^ d) for i in range(n_expert)])

    def other_core(v):
        return lax.ppermute(v, "tensor", [(0, 1), (1, 0)])

    w_gate, w_up, w_down = (pltpu.with_memory_space_constraint(w, pltpu.HBM) for w in (w_gate, w_up, w_down))
    ids_t = expert_ids.T
    here = (pltpu.with_memory_space_constraint(v, pltpu.HBM) for v in (ids_t, gate_probs.T, tokens, grad_out))
    own, oth = pick(e, *here)
    far_first = sorted(range(1, copies), key=lambda d: (-d.bit_count(), d))
    got = partner(oth)
    first = {0: own} | {d: across(own, d) for d in far_first}
    second = {0: got} | {d: across(got, d) for d in far_first}
    pieces = [piece for d in range(copies) for piece in (first[d], second[d])]
    theirs = other_core(stack(pieces, "stack_pieces"))
    x, dh, du, give, keep, grad_w_down = expert_units(
        t, pieces, theirs, w_gate, w_up, w_down, width
    )
    blocks = list(fold(copies, keep, other_core(give)))
    arrived = {d: across(blocks[d], d) for d in far_first}
    dh, local = lax.optimization_barrier((dh, blocks[0]))
    grad_w_gate = weight_grad(dh, x, "grad_gate")
    grad_w_gate, arrived = lax.optimization_barrier((grad_w_gate, arrived))
    kept, others = merge([local] + [arrived[d] for d in range(1, copies)])
    back = partner(others)
    du, kept = lax.optimization_barrier((du, kept))
    grad_w_up = weight_grad(du, x, "grad_up")
    grad_w_up, back = lax.optimization_barrier((grad_w_up, back))
    token_grad, gate_t = finish(e, ids_t, kept, back, width)
    return token_grad, gate_t.T, grad_w_gate, grad_w_up, grad_w_down


def solution(mesh):
    return jax.shard_map(
        on_device,
        mesh=mesh,
        in_specs=(
            P(("groups", "expert"), "tensor"),
            P(("groups", "expert"), "tensor"),
            P(("groups", "expert"), None),
            P(("groups", "expert"), None),
            P(("expert", "tensor"), None),
            P(("expert", "tensor"), None),
            P(("expert", "tensor"), None),
        ),
        out_specs=(
            P(("groups", "expert"), "tensor"),
            P(("groups", "expert"), None),
            P(("expert", "tensor"), "groups"),
            P(("expert", "tensor"), "groups"),
            P(("expert", "tensor"), "groups"),
        ),
        check_vma=False,
    )
```

```python
import functools

import jax
import jax.numpy as jnp
from jax import lax
from jax.experimental import pallas as pl
from jax.experimental.pallas import tpu as pltpu
from jax.sharding import PartitionSpec as P

EXPERTS_ON = 2
CAP = 5
LANES = 128
SUBS = 8
WHOLE = 4
F32 = jnp.float32
BF16 = jnp.bfloat16
MIB = 1 << 20
GATE_CHUNKS = 2
UP_CHUNKS = 4
VMEM = pl.BlockSpec(memory_space=pltpu.VMEM)
SMEM = pl.BlockSpec(memory_space=pltpu.SMEM)
HBM = pl.BlockSpec(memory_space=pltpu.HBM)


def iota(shape, dim):
    return lax.broadcasted_iota(jnp.int32, shape, dim)


def chosen_rows(ids, expert, position):
    rows, toks = position.shape
    hits = [ids[k : k + 1, :] == expert for k in range(ids.shape[0])]
    member = functools.reduce(jnp.logical_or, hits).astype(F32)
    before = (iota((toks, toks), 0) < iota((toks, toks), 1)).astype(F32)
    earlier = jnp.dot(member, before, preferred_element_type=F32)
    return jnp.where(earlier == position.astype(F32), member, 0.0), hits


def sub_row(rows, toks):
    return iota((rows, toks), 0) % SUBS


def tile_of(hidden, most):
    sizes = [n for n in range(16, most + 1, 16) if hidden % n == 0]
    return max(sizes) if sizes else hidden


def pick_body(e_ref, ids_any, probs_any, tok_any, grad_any, own_ref, oth_ref, ids_ref, probs_ref, tok_ref, grad_ref, landed):
    copies = [
        pltpu.make_async_copy(src, dst, landed.at[n])
        for n, (src, dst) in enumerate(
            ((ids_any, ids_ref), (probs_any, probs_ref), (tok_any, tok_ref), (grad_any, grad_ref))
        )
    ]
    for copy in copies:
        copy.start()
    for copy in copies[:2]:
        copy.wait()
    ids = ids_ref[...]
    probs = probs_ref[...].astype(F32)
    toks, width = tok_ref.shape
    half, eighth = width // 2, width // SUBS
    size = half + eighth
    both = 2 * SUBS
    row = iota((both, toks), 0)
    sub = sub_row(both, toks)
    expert = jnp.where(row < SUBS, e_ref[0], 1 - e_ref[0])
    main, hits = chosen_rows(ids, expert, sub % WHOLE)
    tail, _ = chosen_rows(ids, expert, jnp.full((both, toks), WHOLE, jnp.int32))
    plain = jnp.where(sub < WHOLE, main, jnp.where(sub == WHOLE, tail, 0.0))
    halves = [jnp.where(sub // WHOLE == h, main, 0.0).astype(BF16) for h in range(2)]
    eighths = [jnp.where(sub == s, tail, 0.0).astype(BF16) for s in range(SUBS)]
    for at, src in enumerate((tok_ref, grad_ref)):
        copies[2 + at].wait()
        packed = sum(
            jnp.dot(one, src[:, h * half : (h + 1) * half], preferred_element_type=F32)
            for h, one in enumerate(halves)
        ).astype(BF16)
        last = sum(
            jnp.dot(one, src[:, s * eighth : (s + 1) * eighth], preferred_element_type=F32)
            for s, one in enumerate(eighths)
        ).astype(BF16)
        for n, dst in enumerate((own_ref, oth_ref)):
            dst[:, at * size : at * size + half] = packed[n * SUBS : (n + 1) * SUBS]
            dst[:, at * size + half : (at + 1) * size] = last[n * SUBS : (n + 1) * SUBS]
    weight = sum(jnp.where(hit, probs[k : k + 1, :], 0.0) for k, hit in enumerate(hits))
    gate = jnp.broadcast_to(jnp.sum(plain * weight, axis=1, keepdims=True), (both, LANES)).astype(BF16)
    for n, dst in enumerate((own_ref, oth_ref)):
        dst[:, 2 * size :] = gate[n * SUBS : (n + 1) * SUBS]


def pick(e, ids_t, probs_t, tokens, grad_out):
    width = tokens.shape[1]
    size = width // 2 + width // SUBS
    piece = jax.ShapeDtypeStruct((SUBS, 2 * size + LANES), BF16)
    return pl.pallas_call(
        pick_body,
        out_shape=(piece, piece),
        in_specs=[SMEM] + [HBM] * 4,
        out_specs=[VMEM] * 2,
        scratch_shapes=[pltpu.VMEM(v.shape, v.dtype) for v in (ids_t, probs_t, tokens, grad_out)]
        + [pltpu.SemaphoreType.DMA((4,))],
        compiler_params=pltpu.CompilerParams(vmem_limit_bytes=6 * MIB),
        name="pick_rows",
    )(e, ids_t, probs_t, tokens, grad_out)


NT = (((1,), (1,)), ((), ()))


def chunk_of(width, most):
    return max(n for n in range(LANES, most + 1, LANES) if width % n == 0)


def assemble(pieces, held, out, base, side):
    width = held.shape[1]
    half, eighth = width // 2, width // SUBS
    size = half + eighth
    for n, ref in enumerate(pieces):
        at = n * CAP
        piece = ref[:, side * size : (side + 1) * size].astype(F32)
        for h in range(2):
            held[at : at + WHOLE, h * half : (h + 1) * half] = piece[h * WHOLE : (h + 1) * WHOLE, :half]
        for s in range(SUBS):
            held[at + WHOLE : at + CAP, s * eighth : (s + 1) * eighth] = piece[s : s + 1, half:]
    out[:, pl.ds(base, width)] = held[...].astype(BF16)


def pack(part, gates, out, pieces):
    width = part.shape[1]
    half, eighth = width // 2, width // SUBS
    size = half + eighth
    for n in range(pieces):
        at, to = n * CAP, n * SUBS
        for h in range(2):
            out[to + h * WHOLE : to + (h + 1) * WHOLE, :half] = part[at : at + WHOLE, h * half : (h + 1) * half]
        for s in range(SUBS):
            out[to + s : to + s + 1, half:size] = part[at + WHOLE : at + CAP, s * eighth : (s + 1) * eighth]
        out[to : to + CAP, size:] = gates[at : at + CAP, :]
        out[to + CAP : to + SUBS, size:] = jnp.zeros((SUBS - CAP, LANES), F32)


def stack_body(*refs):
    for n, ref in enumerate(refs[:-1]):
        refs[-1][n] = ref[...]


def stack(pieces, name):
    return pl.pallas_call(
        stack_body,
        out_shape=jax.ShapeDtypeStruct((len(pieces),) + pieces[0].shape, BF16),
        in_specs=[VMEM] * len(pieces),
        out_specs=VMEM,
        compiler_params=pltpu.CompilerParams(vmem_limit_bytes=6 * MIB),
        name=name,
    )(*pieces)


def experts_body(pieces, chunk, ahead, t_ref, *refs):
    mine = refs[:pieces]
    theirs = [refs[pieces].at[n] for n in range(pieces)]
    (wg_hbm, wu_hbm, wd_hbm, x_ref, dh_ref, du_ref, give_ref, keep_ref, down_ref, gate_ref, up_ref,
     wg_ref, wu_ref, ring, g_ref, wt_ref, h_ref, u_ref, da_ref, dhr_ref, dur_ref, acc,
     held, factor, landed, ring_landed, sent) = refs[pieces + 1 :]
    rows, depth = x_ref.shape
    hidden = wg_ref.shape[0]
    width = depth // 2
    slots = ring.shape[0]
    steps = depth // chunk
    t = t_ref[0]

    def columns(i):
        return pl.ds(pl.multiple_of(i * chunk, chunk), chunk)

    def load(i, n):
        src, dst = ((wg_hbm, wg_ref), (wu_hbm, wu_ref))[n]
        return pltpu.make_async_copy(src.at[:, columns(i)], dst.at[:, columns(i)], landed.at[i, n])

    def load_down(i):
        slot = lax.rem(i, slots)
        return pltpu.make_async_copy(wd_hbm.at[:, columns(i)], ring.at[slot], ring_landed.at[slot])

    def start(i):
        load(i, 0).start()
        load(i, 1).start()
        load_down(i).start()

    start(0)
    held[...] = jnp.zeros_like(held)
    factor[...] = jnp.zeros_like(factor)
    for n, ref in enumerate(mine):
        factor[n * CAP : (n + 1) * CAP, :] = ref[:CAP, ref.shape[1] - LANES :].astype(F32)
    for side, out in enumerate((x_ref, g_ref)):
        for group, at in ((mine, t), (theirs, 1 - t)):
            assemble(group, held, out, pl.multiple_of(at * width, width), side)
    for i in range(1, min(ahead, steps)):
        start(i)

    def three(i):
        cols = columns(i)
        x = x_ref[:, cols]
        return (
            lambda: lax.dot_general(wg_ref[:, cols], x, NT, preferred_element_type=F32),
            lambda: lax.dot_general(wu_ref[:, cols], x, NT, preferred_element_type=F32),
            lambda: lax.dot_general(ring[lax.rem(i, slots)], g_ref[:, cols], NT, preferred_element_type=F32),
        )

    sums = (h_ref, u_ref, da_ref)
    waits = lambda i: (load(i, 0), load(i, 1), load_down(i))
    for wait, dot, out in zip(waits(0), three(0), sums):
        wait.wait()
        out[...] = dot()

    def up_step(i, carry):
        @pl.when(i + ahead - 1 < steps)
        def _():
            start(i + ahead - 1)

        for wait in waits(i):
            wait.wait()
        for dot, out in zip(three(i), sums):
            out[...] += dot()
        return carry

    lax.fori_loop(1, steps, up_step, 0)

    weight = factor[...].T[:1, :]

    def units(start, size, total):
        at = pl.ds(start, size)
        h = h_ref[at, :]
        u = u_ref[at, :]
        da = da_ref[at, :]
        sigma = 1.0 / (1.0 + jnp.exp(-h))
        silu = h * sigma
        act = silu * u
        scaled = weight * da
        wt_ref[at, :] = (weight * act).astype(BF16)
        dh = scaled * u * sigma * (1.0 + h * (1.0 - sigma))
        du = scaled * silu
        dh_ref[at, :] = dh.astype(BF16)
        du_ref[at, :] = du.astype(BF16)
        dhr_ref[:, at] = dh.T.astype(BF16)
        dur_ref[:, at] = du.T.astype(BF16)
        return total + jnp.sum(act * da, axis=0, keepdims=True)

    total = jnp.zeros((1, rows), F32)
    for begin in range(0, hidden, LANES):
        total = units(begin, min(LANES, hidden - begin), total)
    gates = jnp.broadcast_to(total, (LANES, rows)).T
    tile = tile_of(hidden, 448)
    leaving = []
    for i in range(steps):
        cols = pl.ds(i * chunk, chunk)
        acc[:, cols] = jnp.dot(dhr_ref[...], wg_ref[:, cols], preferred_element_type=F32) + jnp.dot(
            dur_ref[...], wu_ref[:, cols], preferred_element_type=F32
        )
        before = pl.ds((i - 1) * chunk, chunk)
        jobs = [(wt_ref, g_ref, wg_ref.at[:, before] if i else ring.at[0], down_ref)]
        if i < UP_CHUNKS:
            jobs.append((du_ref, x_ref, wu_ref.at[:, before] if i else ring.at[1], up_ref))
        if i < GATE_CHUNKS:
            jobs.append((dh_ref, x_ref, ring.at[2 + i], gate_ref))
        for left, right, room, out in jobs:
            for at in range(0, hidden, tile):
                room[at : at + tile, :] = jnp.dot(
                    left[at : at + tile, :], right[:, cols], preferred_element_type=F32
                ).astype(BF16)
            leaving.append(pltpu.make_async_copy(room, out.at[:, cols], sent.at[len(leaving)]))
            leaving[-1].start()
    for at, out in ((1 - t, give_ref), (t, keep_ref)):
        held[...] = acc[:, pl.ds(pl.multiple_of(at * width, width), width)]
        pack(held, gates, out, pieces)
    for copy in leaving:
        copy.wait()


def expert_units(t, mine, theirs, w_gate, w_up, w_down, width):
    hidden, depth = w_gate.shape
    pieces = len(mine)
    rows = -(-pieces * CAP // 16) * 16
    chunk = chunk_of(width, 768)
    steps = depth // chunk
    ahead = 3
    slots = 4
    unit = jax.ShapeDtypeStruct((hidden, rows), BF16)
    packed = jax.ShapeDtypeStruct((pieces * SUBS, width // 2 + width // SUBS + LANES), F32)
    return pl.pallas_call(
        functools.partial(experts_body, pieces, chunk, ahead),
        out_shape=(
            jax.ShapeDtypeStruct((rows, depth), BF16),
            unit,
            unit,
            packed,
            packed,
        )
        + (jax.ShapeDtypeStruct((hidden, depth), BF16),) * 3,
        in_specs=[SMEM] + [VMEM] * (pieces + 1) + [HBM] * 3,
        out_specs=[VMEM] * 5 + [HBM] * 3,
        scratch_shapes=[
            pltpu.VMEM((hidden, depth), BF16),
            pltpu.VMEM((hidden, depth), BF16),
            pltpu.VMEM((slots, hidden, chunk), BF16),
            pltpu.VMEM((rows, depth), BF16),
            pltpu.VMEM((hidden, rows), BF16),
            pltpu.VMEM((hidden, rows), F32),
            pltpu.VMEM((hidden, rows), F32),
            pltpu.VMEM((hidden, rows), F32),
            pltpu.VMEM((rows, hidden), BF16),
            pltpu.VMEM((rows, hidden), BF16),
            pltpu.VMEM((rows, depth), F32),
            pltpu.VMEM((rows, width), F32),
            pltpu.VMEM((rows, LANES), F32),
            pltpu.SemaphoreType.DMA((steps, 2)),
            pltpu.SemaphoreType.DMA((slots,)),
            pltpu.SemaphoreType.DMA((steps + UP_CHUNKS + GATE_CHUNKS,)),
        ],
        compiler_params=pltpu.CompilerParams(vmem_limit_bytes=50 * MIB),
        cost_estimate=pl.CostEstimate(
            flops=12 * rows * hidden * depth, bytes_accessed=8 * hidden * depth, transcendentals=rows * hidden
        ),
        name="expert_units",
    )(t, *mine, theirs, w_gate, w_up, w_down)


def weights_body(chunk, begun, left_ref, x_ref, _, out_ref, room, sent):
    hidden = left_ref.shape[0]
    tile = tile_of(hidden, 448)
    leaving = []
    for i in range(room.shape[0]):
        cols = pl.ds((begun + i) * chunk, chunk)
        for at in range(0, hidden, tile):
            room[i, at : at + tile, :] = jnp.dot(
                left_ref[at : at + tile, :], x_ref[:, cols], preferred_element_type=F32
            ).astype(BF16)
        leaving.append(pltpu.make_async_copy(room.at[i], out_ref.at[:, cols], sent.at[i]))
        leaving[-1].start()
    for copy in leaving:
        copy.wait()


def weight_grad(left, right, part, begun, name):
    hidden, rows = left.shape
    depth = right.shape[1]
    chunk = chunk_of(depth // 2, 768)
    steps = depth // chunk - begun
    return pl.pallas_call(
        functools.partial(weights_body, chunk, begun),
        out_shape=jax.ShapeDtypeStruct((hidden, depth), BF16),
        in_specs=[VMEM] * 2 + [HBM],
        out_specs=HBM,
        input_output_aliases={2: 0},
        scratch_shapes=[pltpu.VMEM((steps, hidden, chunk), BF16), pltpu.SemaphoreType.DMA((steps,))],
        compiler_params=pltpu.CompilerParams(vmem_limit_bytes=28 * MIB),
        cost_estimate=pl.CostEstimate(
            flops=2 * rows * hidden * steps * chunk, bytes_accessed=2 * hidden * steps * chunk, transcendentals=0
        ),
        name=name,
    )(left, right, part)


def fold_body(copies, keep_ref, got_ref, *outs):
    for d, out in enumerate(outs):
        rows = slice(d * 2 * SUBS, (d + 1) * 2 * SUBS)
        out[...] = keep_ref[rows, :] + got_ref[rows, :]


def fold(copies, keep, got):
    return pl.pallas_call(
        functools.partial(fold_body, copies),
        out_shape=[jax.ShapeDtypeStruct((2 * SUBS, keep.shape[1]), F32)] * copies,
        in_specs=[VMEM] * 2,
        out_specs=[VMEM] * copies,
        compiler_params=pltpu.CompilerParams(vmem_limit_bytes=6 * MIB),
        name="fold_cores",
    )(keep, got)


def merge_body(*refs):
    blocks, (mine_ref, other_ref) = refs[:-2], refs[-2:]
    for at, out in ((0, mine_ref), (SUBS, other_ref)):
        total = blocks[0][at : at + SUBS, :]
        for block in blocks[1:]:
            total += block[at : at + SUBS, :]
        out[...] = total


def merge(blocks):
    part = jax.ShapeDtypeStruct((SUBS, blocks[0].shape[1]), F32)
    return pl.pallas_call(
        merge_body,
        out_shape=(part, part),
        in_specs=[VMEM] * len(blocks),
        out_specs=[VMEM] * 2,
        compiler_params=pltpu.CompilerParams(vmem_limit_bytes=6 * MIB),
        name="merge_chips",
    )(*blocks)


def finish_body(e_ref, ids_ref, mine_ref, got_ref, tok_ref, gate_ref):
    ids = ids_ref[...]
    toks, width = tok_ref.shape
    half, eighth = width // 2, width // SUBS
    both = 2 * SUBS
    row = iota((both, toks), 0)
    sub = sub_row(both, toks)
    expert = jnp.where(row < SUBS, e_ref[0], 1 - e_ref[0])
    main, hits = chosen_rows(ids, expert, sub % WHOLE)
    tail, _ = chosen_rows(ids, expert, jnp.full((both, toks), WHOLE, jnp.int32))
    plain = jnp.where(sub < WHOLE, main, jnp.where(sub == WHOLE, tail, 0.0))
    data = jnp.concatenate([mine_ref[...], got_ref[...]], axis=0)
    tn = (((0,), (0,)), ((), ()))
    exact = dict(precision=lax.Precision.HIGHEST, preferred_element_type=F32)
    halves = [
        lax.dot_general(jnp.where(sub // WHOLE == h, main, 0.0), data[:, :half], tn, **exact) for h in range(2)
    ]
    for s in range(SUBS):
        last = lax.dot_general(jnp.where(sub == s, tail, 0.0), data[:, half : half + eighth], tn, **exact)
        h, at = divmod(s * eighth, half)
        tok_ref[:, s * eighth : (s + 1) * eighth] = (halves[h][:, at : at + eighth] + last).astype(BF16)
    term = plain * data[:, half + eighth : half + eighth + 1]
    for k, hit in enumerate(hits):
        gate_ref[k : k + 1, :] = jnp.sum(jnp.where(hit, term, 0.0), axis=0, keepdims=True)


def finish(e, ids_t, mine, got, width):
    top, toks = ids_t.shape
    return pl.pallas_call(
        finish_body,
        out_shape=(jax.ShapeDtypeStruct((toks, width), BF16), jax.ShapeDtypeStruct((top, toks), F32)),
        in_specs=[SMEM] + [VMEM] * 3,
        out_specs=[VMEM] * 2,
        compiler_params=pltpu.CompilerParams(vmem_limit_bytes=6 * MIB),
        name="finish_tokens",
    )(e, ids_t, mine, got)


def on_device(tokens, grad_out, expert_ids, gate_probs, w_gate, w_up, w_down):
    n_expert = lax.axis_size("expert")
    copies = n_expert // EXPERTS_ON
    place = lax.axis_index("expert")
    e = (place >= copies).astype(jnp.int32).reshape(1)
    t = lax.axis_index("tensor").astype(jnp.int32).reshape(1)
    width = tokens.shape[1]

    def partner(v):
        return lax.ppermute(v, "expert", [(i, (i + copies) % n_expert) for i in range(n_expert)])

    def across(v, d):
        return lax.ppermute(v, "expert", [(i, i ^ d) for i in range(n_expert)])

    def other_core(v):
        return lax.ppermute(v, "tensor", [(0, 1), (1, 0)])

    w_gate, w_up, w_down = (pltpu.with_memory_space_constraint(w, pltpu.HBM) for w in (w_gate, w_up, w_down))
    ids_t = expert_ids.T
    here = (pltpu.with_memory_space_constraint(v, pltpu.HBM) for v in (ids_t, gate_probs.T, tokens, grad_out))
    own, oth = pick(e, *here)
    far_first = sorted(range(1, copies), key=lambda d: (-d.bit_count(), d))
    got = partner(oth)
    first = {0: own} | {d: across(own, d) for d in far_first}
    second = {0: got} | {d: across(got, d) for d in far_first}
    pieces = [piece for d in range(copies) for piece in (first[d], second[d])]
    theirs = other_core(stack(pieces, "stack_pieces"))
    x, dh, du, give, keep, grad_w_down, gate_begun, up_begun = expert_units(
        t, pieces, theirs, w_gate, w_up, w_down, width
    )
    blocks = list(fold(copies, keep, other_core(give)))
    arrived = {d: across(blocks[d], d) for d in far_first}
    dh, local = lax.optimization_barrier((dh, blocks[0]))
    grad_w_gate = weight_grad(dh, x, gate_begun, GATE_CHUNKS, "grad_gate")
    grad_w_gate, arrived = lax.optimization_barrier((grad_w_gate, arrived))
    kept, others = merge([local] + [arrived[d] for d in range(1, copies)])
    back = partner(others)
    du, kept = lax.optimization_barrier((du, kept))
    grad_w_up = weight_grad(du, x, up_begun, UP_CHUNKS, "grad_up")
    grad_w_up, back = lax.optimization_barrier((grad_w_up, back))
    token_grad, gate_t = finish(e, ids_t, kept, back, width)
    return token_grad, gate_t.T, grad_w_gate, grad_w_up, grad_w_down


def solution(mesh):
    return jax.shard_map(
        on_device,
        mesh=mesh,
        in_specs=(
            P(("groups", "expert"), "tensor"),
            P(("groups", "expert"), "tensor"),
            P(("groups", "expert"), None),
            P(("groups", "expert"), None),
            P(("expert", "tensor"), None),
            P(("expert", "tensor"), None),
            P(("expert", "tensor"), None),
        ),
        out_specs=(
            P(("groups", "expert"), "tensor"),
            P(("groups", "expert"), None),
            P(("expert", "tensor"), "groups"),
            P(("expert", "tensor"), "groups"),
            P(("expert", "tensor"), "groups"),
        ),
        check_vma=False,
    )
```

```python
import functools

import jax
import jax.numpy as jnp
from jax import lax
from jax.experimental import pallas as pl
from jax.experimental.pallas import tpu as pltpu
from jax.sharding import PartitionSpec as P

EXPERTS_ON = 2
CAP = 5
LANES = 128
SUBS = 8
WHOLE = 4
F32 = jnp.float32
BF16 = jnp.bfloat16
MIB = 1 << 20
GATE_CHUNKS = 1
UP_CHUNKS = 4
VMEM = pl.BlockSpec(memory_space=pltpu.VMEM)
SMEM = pl.BlockSpec(memory_space=pltpu.SMEM)
HBM = pl.BlockSpec(memory_space=pltpu.HBM)


def iota(shape, dim):
    return lax.broadcasted_iota(jnp.int32, shape, dim)


def chosen_rows(ids, expert, position):
    rows, toks = position.shape
    hits = [ids[k : k + 1, :] == expert for k in range(ids.shape[0])]
    member = functools.reduce(jnp.logical_or, hits).astype(F32)
    before = (iota((toks, toks), 0) < iota((toks, toks), 1)).astype(F32)
    earlier = jnp.dot(member, before, preferred_element_type=F32)
    return jnp.where(earlier == position.astype(F32), member, 0.0), hits


def sub_row(rows, toks):
    return iota((rows, toks), 0) % SUBS


def tile_of(hidden, most):
    sizes = [n for n in range(16, most + 1, 16) if hidden % n == 0]
    return max(sizes) if sizes else hidden


def pick_body(e_ref, ids_any, probs_any, tok_any, grad_any, own_ref, oth_ref, ids_ref, probs_ref, tok_ref, grad_ref, landed):
    copies = [
        pltpu.make_async_copy(src, dst, landed.at[n])
        for n, (src, dst) in enumerate(
            ((ids_any, ids_ref), (probs_any, probs_ref), (tok_any, tok_ref), (grad_any, grad_ref))
        )
    ]
    for copy in copies:
        copy.start()
    for copy in copies[:2]:
        copy.wait()
    ids = ids_ref[...]
    probs = probs_ref[...].astype(F32)
    toks, width = tok_ref.shape
    half, eighth = width // 2, width // SUBS
    size = half + eighth
    both = 2 * SUBS
    row = iota((both, toks), 0)
    sub = sub_row(both, toks)
    expert = jnp.where(row < SUBS, e_ref[0], 1 - e_ref[0])
    main, hits = chosen_rows(ids, expert, sub % WHOLE)
    tail, _ = chosen_rows(ids, expert, jnp.full((both, toks), WHOLE, jnp.int32))
    plain = jnp.where(sub < WHOLE, main, jnp.where(sub == WHOLE, tail, 0.0))
    halves = [jnp.where(sub // WHOLE == h, main, 0.0).astype(BF16) for h in range(2)]
    eighths = [jnp.where(sub == s, tail, 0.0).astype(BF16) for s in range(SUBS)]
    for at, src in enumerate((tok_ref, grad_ref)):
        copies[2 + at].wait()
        packed = sum(
            jnp.dot(one, src[:, h * half : (h + 1) * half], preferred_element_type=F32)
            for h, one in enumerate(halves)
        ).astype(BF16)
        last = sum(
            jnp.dot(one, src[:, s * eighth : (s + 1) * eighth], preferred_element_type=F32)
            for s, one in enumerate(eighths)
        ).astype(BF16)
        for n, dst in enumerate((own_ref, oth_ref)):
            dst[:, at * size : at * size + half] = packed[n * SUBS : (n + 1) * SUBS]
            dst[:, at * size + half : (at + 1) * size] = last[n * SUBS : (n + 1) * SUBS]
    weight = sum(jnp.where(hit, probs[k : k + 1, :], 0.0) for k, hit in enumerate(hits))
    gate = jnp.broadcast_to(jnp.sum(plain * weight, axis=1, keepdims=True), (both, LANES)).astype(BF16)
    for n, dst in enumerate((own_ref, oth_ref)):
        dst[:, 2 * size :] = gate[n * SUBS : (n + 1) * SUBS]


def pick(e, ids_t, probs_t, tokens, grad_out):
    width = tokens.shape[1]
    size = width // 2 + width // SUBS
    piece = jax.ShapeDtypeStruct((SUBS, 2 * size + LANES), BF16)
    return pl.pallas_call(
        pick_body,
        out_shape=(piece, piece),
        in_specs=[SMEM] + [HBM] * 4,
        out_specs=[VMEM] * 2,
        scratch_shapes=[pltpu.VMEM(v.shape, v.dtype) for v in (ids_t, probs_t, tokens, grad_out)]
        + [pltpu.SemaphoreType.DMA((4,))],
        compiler_params=pltpu.CompilerParams(vmem_limit_bytes=6 * MIB),
        name="pick_rows",
    )(e, ids_t, probs_t, tokens, grad_out)


NT = (((1,), (1,)), ((), ()))


def chunk_of(width, most):
    return max(n for n in range(LANES, most + 1, LANES) if width % n == 0)


def assemble(pieces, held, out, base, side):
    width = held.shape[1]
    half, eighth = width // 2, width // SUBS
    size = half + eighth
    for n, ref in enumerate(pieces):
        at = n * CAP
        piece = ref[:, side * size : (side + 1) * size].astype(F32)
        for h in range(2):
            held[at : at + WHOLE, h * half : (h + 1) * half] = piece[h * WHOLE : (h + 1) * WHOLE, :half]
        for s in range(SUBS):
            held[at + WHOLE : at + CAP, s * eighth : (s + 1) * eighth] = piece[s : s + 1, half:]
    out[:, pl.ds(base, width)] = held[...].astype(BF16)


def pack(part, gates, out, pieces):
    width = part.shape[1]
    half, eighth = width // 2, width // SUBS
    size = half + eighth
    for n in range(pieces):
        at, to = n * CAP, n * SUBS
        for h in range(2):
            out[to + h * WHOLE : to + (h + 1) * WHOLE, :half] = part[at : at + WHOLE, h * half : (h + 1) * half]
        for s in range(SUBS):
            out[to + s : to + s + 1, half:size] = part[at + WHOLE : at + CAP, s * eighth : (s + 1) * eighth]
        out[to : to + CAP, size:] = gates[at : at + CAP, :]
        out[to + CAP : to + SUBS, size:] = jnp.zeros((SUBS - CAP, LANES), F32)


def stack_body(*refs):
    for n, ref in enumerate(refs[:-1]):
        refs[-1][n] = ref[...]


def stack(pieces, name):
    return pl.pallas_call(
        stack_body,
        out_shape=jax.ShapeDtypeStruct((len(pieces),) + pieces[0].shape, BF16),
        in_specs=[VMEM] * len(pieces),
        out_specs=VMEM,
        compiler_params=pltpu.CompilerParams(vmem_limit_bytes=6 * MIB),
        name=name,
    )(*pieces)


def experts_body(pieces, chunk, ahead, t_ref, *refs):
    mine = refs[:pieces]
    theirs = [refs[pieces].at[n] for n in range(pieces)]
    (wg_hbm, wu_hbm, wd_hbm, x_ref, dh_ref, du_ref, give_ref, keep_ref, down_ref, gate_ref, up_ref,
     wg_ref, wu_ref, ring, stage, g_ref, wt_ref, h_ref, u_ref, da_ref, dhr_ref, dur_ref, acc,
     held, factor, landed, ring_landed, sent) = refs[pieces + 1 :]
    rows, depth = x_ref.shape
    hidden = wg_ref.shape[0]
    width = depth // 2
    slots = ring.shape[0]
    steps = depth // chunk
    t = t_ref[0]

    def columns(i):
        return pl.ds(pl.multiple_of(i * chunk, chunk), chunk)

    def load(i, n):
        src, dst = ((wg_hbm, wg_ref), (wu_hbm, wu_ref))[n]
        return pltpu.make_async_copy(src.at[:, columns(i)], dst.at[:, columns(i)], landed.at[i, n])

    def load_down(i):
        slot = lax.rem(i, slots)
        return pltpu.make_async_copy(wd_hbm.at[:, columns(i)], ring.at[slot], ring_landed.at[slot])

    def start(i):
        load(i, 0).start()
        load(i, 1).start()

    start(0)
    held[...] = jnp.zeros_like(held)
    factor[...] = jnp.zeros_like(factor)
    for n, ref in enumerate(mine):
        factor[n * CAP : (n + 1) * CAP, :] = ref[:CAP, ref.shape[1] - LANES :].astype(F32)
    for side, out in enumerate((x_ref, g_ref)):
        for group, at in ((mine, t), (theirs, 1 - t)):
            assemble(group, held, out, pl.multiple_of(at * width, width), side)
    for i in range(1, min(ahead, steps)):
        start(i)

    def add_up(i):
        cols = columns(i)
        x = x_ref[:, cols]
        for n in range(2):
            load(i, n).wait()
        for w, out in ((wg_ref, h_ref), (wu_ref, u_ref)):
            more = lax.dot_general(w[:, cols], x, NT, preferred_element_type=F32)
            out[...] = jnp.where(i == 0, more, out[...] + more)

    def up_step(i, carry):
        @pl.when(i + ahead < steps)
        def _():
            start(i + ahead)

        @pl.when(jnp.logical_and(i + ahead >= steps, i + ahead - steps < slots))
        def _():
            load_down(i + ahead - steps).start()

        add_up(i)
        return carry

    lax.fori_loop(0, steps, up_step, 0)
    for i in range(min(ahead, steps, slots), min(slots, steps)):
        load_down(i).start()

    weight = factor[...].T[:1, :]

    spans = [(begin, min(begin + LANES, hidden)) for begin in range(0, hidden, LANES)]
    for begin, end in spans:
        h = h_ref[begin:end, :]
        silu = h * (1.0 / (1.0 + jnp.exp(-h)))
        wt_ref[begin:end, :] = (weight * (silu * u_ref[begin:end, :])).astype(BF16)

    tile = tile_of(hidden, 448)
    leaving = []

    def leave(left, right, room, out, cols):
        for at in range(0, hidden, tile):
            room[at : at + tile, :] = jnp.dot(
                left[at : at + tile, :], right[:, cols], preferred_element_type=F32
            ).astype(BF16)
        leaving.append(pltpu.make_async_copy(room, out.at[:, cols], sent.at[len(leaving)]))
        leaving[-1].start()

    staged = stage.shape[0]
    for i in range(steps):
        cols = pl.ds(i * chunk, chunk)
        load_down(i).wait()
        if i >= staged:
            leaving[i - staged].wait()
        more = lax.dot_general(ring[i % slots], g_ref[:, cols], NT, preferred_element_type=F32)
        da_ref[...] = da_ref[...] + more if i else more
        leave(wt_ref, g_ref, stage.at[i % staged], down_ref, cols)
        if i + slots < steps:
            load_down(i + slots).start()

    total = jnp.zeros((1, rows), F32)
    for begin, end in spans:
        h = h_ref[begin:end, :]
        u = u_ref[begin:end, :]
        da = da_ref[begin:end, :]
        sigma = 1.0 / (1.0 + jnp.exp(-h))
        silu = h * sigma
        act = silu * u
        scaled = weight * da
        dh = scaled * u * sigma * (1.0 + h * (1.0 - sigma))
        du = scaled * silu
        dh_ref[begin:end, :] = dh.astype(BF16)
        du_ref[begin:end, :] = du.astype(BF16)
        dhr_ref[:, begin:end] = dh.T.astype(BF16)
        dur_ref[:, begin:end] = du.T.astype(BF16)
        total += jnp.sum(act * da, axis=0, keepdims=True)
    gates = jnp.broadcast_to(total, (LANES, rows)).T
    for copy in leaving[steps - min(staged, steps) :]:
        copy.wait()
    gone = len(leaving)
    for i in range(steps):
        cols = pl.ds(i * chunk, chunk)
        acc[:, cols] = jnp.dot(dhr_ref[...], wg_ref[:, cols], preferred_element_type=F32) + jnp.dot(
            dur_ref[...], wu_ref[:, cols], preferred_element_type=F32
        )
        before = pl.ds((i - 1) * chunk, chunk)
        if i < UP_CHUNKS:
            leave(du_ref, x_ref, wu_ref.at[:, before] if i else stage.at[0], up_ref, cols)
        if i < GATE_CHUNKS:
            leave(dh_ref, x_ref, wg_ref.at[:, before] if i else stage.at[1], gate_ref, cols)
    for at, out in ((1 - t, give_ref), (t, keep_ref)):
        held[...] = acc[:, pl.ds(pl.multiple_of(at * width, width), width)]
        pack(held, gates, out, pieces)
    for copy in leaving[gone:]:
        copy.wait()


def expert_units(t, mine, theirs, w_gate, w_up, w_down, width):
    hidden, depth = w_gate.shape
    pieces = len(mine)
    rows = -(-pieces * CAP // 16) * 16
    chunk = chunk_of(width, 768)
    steps = depth // chunk
    ahead = 3
    slots = min(3, steps)
    unit = jax.ShapeDtypeStruct((hidden, rows), BF16)
    packed = jax.ShapeDtypeStruct((pieces * SUBS, width // 2 + width // SUBS + LANES), F32)
    return pl.pallas_call(
        functools.partial(experts_body, pieces, chunk, ahead),
        out_shape=(
            jax.ShapeDtypeStruct((rows, depth), BF16),
            unit,
            unit,
            packed,
            packed,
        )
        + (jax.ShapeDtypeStruct((hidden, depth), BF16),) * 3,
        in_specs=[SMEM] + [VMEM] * (pieces + 1) + [HBM] * 3,
        out_specs=[VMEM] * 5 + [HBM] * 3,
        scratch_shapes=[
            pltpu.VMEM((hidden, depth), BF16),
            pltpu.VMEM((hidden, depth), BF16),
            pltpu.VMEM((slots, hidden, chunk), BF16),
            pltpu.VMEM((2, hidden, chunk), BF16),
            pltpu.VMEM((rows, depth), BF16),
            pltpu.VMEM((hidden, rows), BF16),
            pltpu.VMEM((hidden, rows), F32),
            pltpu.VMEM((hidden, rows), F32),
            pltpu.VMEM((hidden, rows), F32),
            pltpu.VMEM((rows, hidden), BF16),
            pltpu.VMEM((rows, hidden), BF16),
            pltpu.VMEM((rows, depth), F32),
            pltpu.VMEM((rows, width), F32),
            pltpu.VMEM((rows, LANES), F32),
            pltpu.SemaphoreType.DMA((steps, 2)),
            pltpu.SemaphoreType.DMA((slots,)),
            pltpu.SemaphoreType.DMA((steps + UP_CHUNKS + GATE_CHUNKS,)),
        ],
        compiler_params=pltpu.CompilerParams(vmem_limit_bytes=50 * MIB),
        cost_estimate=pl.CostEstimate(
            flops=12 * rows * hidden * depth, bytes_accessed=8 * hidden * depth, transcendentals=rows * hidden
        ),
        name="expert_units",
    )(t, *mine, theirs, w_gate, w_up, w_down)


def weights_body(chunk, begun, left_ref, x_ref, _, out_ref, room, sent):
    hidden = left_ref.shape[0]
    tile = tile_of(hidden, 448)
    leaving = []
    for i in range(room.shape[0]):
        cols = pl.ds((begun + i) * chunk, chunk)
        for at in range(0, hidden, tile):
            room[i, at : at + tile, :] = jnp.dot(
                left_ref[at : at + tile, :], x_ref[:, cols], preferred_element_type=F32
            ).astype(BF16)
        leaving.append(pltpu.make_async_copy(room.at[i], out_ref.at[:, cols], sent.at[i]))
        leaving[-1].start()
    for copy in leaving:
        copy.wait()


def weight_grad(left, right, part, begun, name):
    hidden, rows = left.shape
    depth = right.shape[1]
    chunk = chunk_of(depth // 2, 768)
    steps = depth // chunk - begun
    return pl.pallas_call(
        functools.partial(weights_body, chunk, begun),
        out_shape=jax.ShapeDtypeStruct((hidden, depth), BF16),
        in_specs=[VMEM] * 2 + [HBM],
        out_specs=HBM,
        input_output_aliases={2: 0},
        scratch_shapes=[pltpu.VMEM((steps, hidden, chunk), BF16), pltpu.SemaphoreType.DMA((steps,))],
        compiler_params=pltpu.CompilerParams(vmem_limit_bytes=28 * MIB),
        cost_estimate=pl.CostEstimate(
            flops=2 * rows * hidden * steps * chunk, bytes_accessed=2 * hidden * steps * chunk, transcendentals=0
        ),
        name=name,
    )(left, right, part)


def fold_body(copies, keep_ref, got_ref, *outs):
    for d, out in enumerate(outs):
        rows = slice(d * 2 * SUBS, (d + 1) * 2 * SUBS)
        out[...] = keep_ref[rows, :] + got_ref[rows, :]


def fold(copies, keep, got):
    return pl.pallas_call(
        functools.partial(fold_body, copies),
        out_shape=[jax.ShapeDtypeStruct((2 * SUBS, keep.shape[1]), F32)] * copies,
        in_specs=[VMEM] * 2,
        out_specs=[VMEM] * copies,
        compiler_params=pltpu.CompilerParams(vmem_limit_bytes=6 * MIB),
        name="fold_cores",
    )(keep, got)


def merge_body(*refs):
    blocks, (mine_ref, other_ref) = refs[:-2], refs[-2:]
    for at, out in ((0, mine_ref), (SUBS, other_ref)):
        total = blocks[0][at : at + SUBS, :]
        for block in blocks[1:]:
            total += block[at : at + SUBS, :]
        out[...] = total


def merge(blocks):
    part = jax.ShapeDtypeStruct((SUBS, blocks[0].shape[1]), F32)
    return pl.pallas_call(
        merge_body,
        out_shape=(part, part),
        in_specs=[VMEM] * len(blocks),
        out_specs=[VMEM] * 2,
        compiler_params=pltpu.CompilerParams(vmem_limit_bytes=6 * MIB),
        name="merge_chips",
    )(*blocks)


def finish_body(e_ref, ids_ref, mine_ref, got_ref, tok_ref, gate_ref):
    ids = ids_ref[...]
    toks, width = tok_ref.shape
    half, eighth = width // 2, width // SUBS
    both = 2 * SUBS
    row = iota((both, toks), 0)
    sub = sub_row(both, toks)
    expert = jnp.where(row < SUBS, e_ref[0], 1 - e_ref[0])
    main, hits = chosen_rows(ids, expert, sub % WHOLE)
    tail, _ = chosen_rows(ids, expert, jnp.full((both, toks), WHOLE, jnp.int32))
    plain = jnp.where(sub < WHOLE, main, jnp.where(sub == WHOLE, tail, 0.0))
    data = jnp.concatenate([mine_ref[...], got_ref[...]], axis=0)
    tn = (((0,), (0,)), ((), ()))
    exact = dict(precision=lax.Precision.HIGHEST, preferred_element_type=F32)
    halves = [
        lax.dot_general(jnp.where(sub // WHOLE == h, main, 0.0), data[:, :half], tn, **exact) for h in range(2)
    ]
    for s in range(SUBS):
        last = lax.dot_general(jnp.where(sub == s, tail, 0.0), data[:, half : half + eighth], tn, **exact)
        h, at = divmod(s * eighth, half)
        tok_ref[:, s * eighth : (s + 1) * eighth] = (halves[h][:, at : at + eighth] + last).astype(BF16)
    term = plain * data[:, half + eighth : half + eighth + 1]
    for k, hit in enumerate(hits):
        gate_ref[k : k + 1, :] = jnp.sum(jnp.where(hit, term, 0.0), axis=0, keepdims=True)


def finish(e, ids_t, mine, got, width):
    top, toks = ids_t.shape
    return pl.pallas_call(
        finish_body,
        out_shape=(jax.ShapeDtypeStruct((toks, width), BF16), jax.ShapeDtypeStruct((top, toks), F32)),
        in_specs=[SMEM] + [VMEM] * 3,
        out_specs=[VMEM] * 2,
        compiler_params=pltpu.CompilerParams(vmem_limit_bytes=6 * MIB),
        name="finish_tokens",
    )(e, ids_t, mine, got)


def on_device(tokens, grad_out, expert_ids, gate_probs, w_gate, w_up, w_down):
    n_expert = lax.axis_size("expert")
    copies = n_expert // EXPERTS_ON
    place = lax.axis_index("expert")
    e = (place >= copies).astype(jnp.int32).reshape(1)
    t = lax.axis_index("tensor").astype(jnp.int32).reshape(1)
    width = tokens.shape[1]

    def partner(v):
        return lax.ppermute(v, "expert", [(i, (i + copies) % n_expert) for i in range(n_expert)])

    def across(v, d):
        return lax.ppermute(v, "expert", [(i, i ^ d) for i in range(n_expert)])

    def other_core(v):
        return lax.ppermute(v, "tensor", [(0, 1), (1, 0)])

    w_gate, w_up, w_down = (pltpu.with_memory_space_constraint(w, pltpu.HBM) for w in (w_gate, w_up, w_down))
    ids_t = expert_ids.T
    here = (pltpu.with_memory_space_constraint(v, pltpu.HBM) for v in (ids_t, gate_probs.T, tokens, grad_out))
    own, oth = pick(e, *here)
    far_first = sorted(range(1, copies), key=lambda d: (-d.bit_count(), d))
    got = partner(oth)
    first = {0: own} | {d: across(own, d) for d in far_first}
    second = {0: got} | {d: across(got, d) for d in far_first}
    pieces = [piece for d in range(copies) for piece in (first[d], second[d])]
    theirs = other_core(stack(pieces, "stack_pieces"))
    x, dh, du, give, keep, grad_w_down, gate_begun, up_begun = expert_units(
        t, pieces, theirs, w_gate, w_up, w_down, width
    )
    blocks = list(fold(copies, keep, other_core(give)))
    arrived = {d: across(blocks[d], d) for d in far_first}
    dh, local = lax.optimization_barrier((dh, blocks[0]))
    grad_w_gate = weight_grad(dh, x, gate_begun, GATE_CHUNKS, "grad_gate")
    grad_w_gate, arrived = lax.optimization_barrier((grad_w_gate, arrived))
    kept, others = merge([local] + [arrived[d] for d in range(1, copies)])
    back = partner(others)
    du, kept = lax.optimization_barrier((du, kept))
    grad_w_up = weight_grad(du, x, up_begun, UP_CHUNKS, "grad_up")
    grad_w_up, back = lax.optimization_barrier((grad_w_up, back))
    token_grad, gate_t = finish(e, ids_t, kept, back, width)
    return token_grad, gate_t.T, grad_w_gate, grad_w_up, grad_w_down


def solution(mesh):
    return jax.shard_map(
        on_device,
        mesh=mesh,
        in_specs=(
            P(("groups", "expert"), "tensor"),
            P(("groups", "expert"), "tensor"),
            P(("groups", "expert"), None),
            P(("groups", "expert"), None),
            P(("expert", "tensor"), None),
            P(("expert", "tensor"), None),
            P(("expert", "tensor"), None),
        ),
        out_specs=(
            P(("groups", "expert"), "tensor"),
            P(("groups", "expert"), None),
            P(("expert", "tensor"), "groups"),
            P(("expert", "tensor"), "groups"),
            P(("expert", "tensor"), "groups"),
        ),
        check_vma=False,
    )
```

```python
import functools

import jax
import jax.numpy as jnp
from jax import lax
from jax.experimental import pallas as pl
from jax.experimental.pallas import tpu as pltpu
from jax.sharding import PartitionSpec as P

EXPERTS_ON = 2
CAP = 5
LANES = 128
SUBS = 8
WHOLE = 4
F32 = jnp.float32
BF16 = jnp.bfloat16
MIB = 1 << 20
GATE_CHUNKS = 1
UP_CHUNKS = 4
VMEM = pl.BlockSpec(memory_space=pltpu.VMEM)
SMEM = pl.BlockSpec(memory_space=pltpu.SMEM)
HBM = pl.BlockSpec(memory_space=pltpu.HBM)


def iota(shape, dim):
    return lax.broadcasted_iota(jnp.int32, shape, dim)


def chosen_rows(ids, expert, position):
    rows, toks = position.shape
    hits = [ids[k : k + 1, :] == expert for k in range(ids.shape[0])]
    member = functools.reduce(jnp.logical_or, hits).astype(F32)
    before = (iota((toks, toks), 0) < iota((toks, toks), 1)).astype(F32)
    earlier = jnp.dot(member, before, preferred_element_type=F32)
    return jnp.where(earlier == position.astype(F32), member, 0.0), hits


def sub_row(rows, toks):
    return iota((rows, toks), 0) % SUBS


def tile_of(hidden, most):
    sizes = [n for n in range(16, most + 1, 16) if hidden % n == 0]
    return max(sizes) if sizes else hidden


def pick_body(e_ref, ids_any, probs_any, tok_any, grad_any, own_ref, oth_ref, ids_ref, probs_ref, tok_ref, grad_ref, landed):
    copies = [
        pltpu.make_async_copy(src, dst, landed.at[n])
        for n, (src, dst) in enumerate(
            ((ids_any, ids_ref), (probs_any, probs_ref), (tok_any, tok_ref), (grad_any, grad_ref))
        )
    ]
    for copy in copies:
        copy.start()
    for copy in copies[:2]:
        copy.wait()
    ids = ids_ref[...]
    probs = probs_ref[...].astype(F32)
    toks, width = tok_ref.shape
    half, eighth = width // 2, width // SUBS
    size = half + eighth
    both = 2 * SUBS
    row = iota((both, toks), 0)
    sub = sub_row(both, toks)
    expert = jnp.where(row < SUBS, e_ref[0], 1 - e_ref[0])
    main, hits = chosen_rows(ids, expert, sub % WHOLE)
    tail, _ = chosen_rows(ids, expert, jnp.full((both, toks), WHOLE, jnp.int32))
    plain = jnp.where(sub < WHOLE, main, jnp.where(sub == WHOLE, tail, 0.0))
    halves = [jnp.where(sub // WHOLE == h, main, 0.0).astype(BF16) for h in range(2)]
    eighths = [jnp.where(sub == s, tail, 0.0).astype(BF16) for s in range(SUBS)]
    for at, src in enumerate((tok_ref, grad_ref)):
        copies[2 + at].wait()
        packed = sum(
            jnp.dot(one, src[:, h * half : (h + 1) * half], preferred_element_type=F32)
            for h, one in enumerate(halves)
        ).astype(BF16)
        last = sum(
            jnp.dot(one, src[:, s * eighth : (s + 1) * eighth], preferred_element_type=F32)
            for s, one in enumerate(eighths)
        ).astype(BF16)
        for n, dst in enumerate((own_ref, oth_ref)):
            dst[:, at * size : at * size + half] = packed[n * SUBS : (n + 1) * SUBS]
            dst[:, at * size + half : (at + 1) * size] = last[n * SUBS : (n + 1) * SUBS]
    weight = sum(jnp.where(hit, probs[k : k + 1, :], 0.0) for k, hit in enumerate(hits))
    gate = jnp.broadcast_to(jnp.sum(plain * weight, axis=1, keepdims=True), (both, LANES)).astype(BF16)
    for n, dst in enumerate((own_ref, oth_ref)):
        dst[:, 2 * size :] = gate[n * SUBS : (n + 1) * SUBS]


def pick(e, ids_t, probs_t, tokens, grad_out):
    width = tokens.shape[1]
    size = width // 2 + width // SUBS
    piece = jax.ShapeDtypeStruct((SUBS, 2 * size + LANES), BF16)
    return pl.pallas_call(
        pick_body,
        out_shape=(piece, piece),
        in_specs=[SMEM] + [HBM] * 4,
        out_specs=[VMEM] * 2,
        scratch_shapes=[pltpu.VMEM(v.shape, v.dtype) for v in (ids_t, probs_t, tokens, grad_out)]
        + [pltpu.SemaphoreType.DMA((4,))],
        compiler_params=pltpu.CompilerParams(vmem_limit_bytes=6 * MIB),
        name="pick_rows",
    )(e, ids_t, probs_t, tokens, grad_out)


NT = (((1,), (1,)), ((), ()))


def chunk_of(width, most):
    return max(n for n in range(LANES, most + 1, LANES) if width % n == 0)


def assemble(pieces, held, out, base, side):
    width = held.shape[1]
    half, eighth = width // 2, width // SUBS
    size = half + eighth
    for n, ref in enumerate(pieces):
        at = n * CAP
        piece = ref[:, side * size : (side + 1) * size].astype(F32)
        for h in range(2):
            held[at : at + WHOLE, h * half : (h + 1) * half] = piece[h * WHOLE : (h + 1) * WHOLE, :half]
        for s in range(SUBS):
            held[at + WHOLE : at + CAP, s * eighth : (s + 1) * eighth] = piece[s : s + 1, half:]
    out[:, pl.ds(base, width)] = held[...].astype(BF16)


def pack(part, gates, out, pieces):
    width = part.shape[1]
    half, eighth = width // 2, width // SUBS
    size = half + eighth
    for n in range(pieces):
        at, to = n * CAP, n * SUBS
        for h in range(2):
            out[to + h * WHOLE : to + (h + 1) * WHOLE, :half] = part[at : at + WHOLE, h * half : (h + 1) * half]
        for s in range(SUBS):
            out[to + s : to + s + 1, half:size] = part[at + WHOLE : at + CAP, s * eighth : (s + 1) * eighth]
        out[to : to + CAP, size:] = gates[at : at + CAP, :]
        out[to + CAP : to + SUBS, size:] = jnp.zeros((SUBS - CAP, LANES), F32)


def stack_body(*refs):
    for n, ref in enumerate(refs[:-1]):
        refs[-1][n] = ref[...]


def stack(pieces, name):
    return pl.pallas_call(
        stack_body,
        out_shape=jax.ShapeDtypeStruct((len(pieces),) + pieces[0].shape, BF16),
        in_specs=[VMEM] * len(pieces),
        out_specs=VMEM,
        compiler_params=pltpu.CompilerParams(vmem_limit_bytes=6 * MIB),
        name=name,
    )(*pieces)


def experts_body(pieces, chunk, t_ref, *refs):
    mine = refs[:pieces]
    theirs = [refs[pieces].at[n] for n in range(pieces)]
    (wg_hbm, wu_hbm, wd_hbm, x_ref, dh_ref, du_ref, give_ref, keep_ref, down_ref, gate_ref, up_ref,
     wg_ref, wu_ref, ring, g_ref, wt_ref, h_ref, u_ref, da_ref, dhr_ref, dur_ref, acc,
     held, factor, landed, ring_landed, sent) = refs[pieces + 1 :]
    rows, depth = x_ref.shape
    hidden = wg_ref.shape[0]
    width = depth // 2
    slots = ring.shape[0]
    steps = depth // chunk
    t = t_ref[0]

    def columns(i):
        return pl.ds(pl.multiple_of(i * chunk, chunk), chunk)

    def load(i, n):
        src, dst = ((wg_hbm, wg_ref), (wu_hbm, wu_ref))[n]
        return pltpu.make_async_copy(src.at[:, columns(i)], dst.at[:, columns(i)], landed.at[i, n])

    def load_down(i):
        slot = lax.rem(i, slots)
        return pltpu.make_async_copy(wd_hbm.at[:, columns(i)], ring.at[slot], ring_landed.at[slot])

    def start(i):
        load(i, 0).start()
        load(i, 1).start()
        load_down(i).start()

    start(0)
    held[...] = jnp.zeros_like(held)
    factor[...] = jnp.zeros_like(factor)
    for n, ref in enumerate(mine):
        factor[n * CAP : (n + 1) * CAP, :] = ref[:CAP, ref.shape[1] - LANES :].astype(F32)
    for side, out in enumerate((x_ref, g_ref)):
        for group, at in ((mine, t), (theirs, 1 - t)):
            assemble(group, held, out, pl.multiple_of(at * width, width), side)
    for i in range(1, min(3, steps)):
        start(i)

    def three(i):
        cols = columns(i)
        x = x_ref[:, cols]
        return (
            lambda: lax.dot_general(wg_ref[:, cols], x, NT, preferred_element_type=F32),
            lambda: lax.dot_general(wu_ref[:, cols], x, NT, preferred_element_type=F32),
            lambda: lax.dot_general(ring[lax.rem(i, slots)], g_ref[:, cols], NT, preferred_element_type=F32),
        )

    sums = (h_ref, u_ref, da_ref)
    waits = lambda i: (load(i, 0), load(i, 1), load_down(i))
    for wait, dot, out in zip(waits(0), three(0), sums):
        wait.wait()
        out[...] = dot()

    def pair_step(j, carry):
        i = 1 + 2 * j
        for n in (i + 2, i + 3):

            @pl.when(n < steps)
            def _():
                start(n)

        for wait in waits(i) + waits(i + 1):
            wait.wait()
        for dot, other, out in zip(three(i), three(i + 1), sums):
            out[...] += dot() + other()
        return carry

    pairs = (steps - 1) // 2
    lax.fori_loop(0, pairs, pair_step, 0)
    for i in range(1 + 2 * pairs, steps):
        for wait in waits(i):
            wait.wait()
        for dot, out in zip(three(i), sums):
            out[...] += dot()

    weight = factor[...].T[:1, :]

    def units(start, size, total):
        at = pl.ds(start, size)
        h = h_ref[at, :]
        u = u_ref[at, :]
        da = da_ref[at, :]
        sigma = 1.0 / (1.0 + jnp.exp(-h))
        silu = h * sigma
        act = silu * u
        scaled = weight * da
        wt_ref[at, :] = (weight * act).astype(BF16)
        dh = scaled * u * sigma * (1.0 + h * (1.0 - sigma))
        du = scaled * silu
        dh_ref[at, :] = dh.astype(BF16)
        du_ref[at, :] = du.astype(BF16)
        dhr_ref[:, at] = dh.T.astype(BF16)
        dur_ref[:, at] = du.T.astype(BF16)
        return total + jnp.sum(act * da, axis=0, keepdims=True)

    total = jnp.zeros((1, rows), F32)
    for begin in range(0, hidden, LANES):
        total = units(begin, min(LANES, hidden - begin), total)
    gates = jnp.broadcast_to(total, (LANES, rows)).T
    tile = tile_of(hidden, 448)
    leaving = []
    for i in range(steps):
        cols = pl.ds(i * chunk, chunk)
        acc[:, cols] = jnp.dot(dhr_ref[...], wg_ref[:, cols], preferred_element_type=F32) + jnp.dot(
            dur_ref[...], wu_ref[:, cols], preferred_element_type=F32
        )
        before = pl.ds((i - 1) * chunk, chunk)
        jobs = [(wt_ref, g_ref, wg_ref.at[:, before] if i else ring.at[0], down_ref)]
        if i < UP_CHUNKS:
            jobs.append((du_ref, x_ref, wu_ref.at[:, before] if i else ring.at[1], up_ref))
        if i < GATE_CHUNKS:
            jobs.append((dh_ref, x_ref, ring.at[2 + i], gate_ref))
        for left, right, room, out in jobs:
            for at in range(0, hidden, tile):
                room[at : at + tile, :] = jnp.dot(
                    left[at : at + tile, :], right[:, cols], preferred_element_type=F32
                ).astype(BF16)
            leaving.append(pltpu.make_async_copy(room, out.at[:, cols], sent.at[len(leaving)]))
            leaving[-1].start()
    for at, out in ((1 - t, give_ref), (t, keep_ref)):
        held[...] = acc[:, pl.ds(pl.multiple_of(at * width, width), width)]
        pack(held, gates, out, pieces)
    for copy in leaving:
        copy.wait()


def expert_units(t, mine, theirs, w_gate, w_up, w_down, width):
    hidden, depth = w_gate.shape
    pieces = len(mine)
    rows = -(-pieces * CAP // 16) * 16
    chunk = chunk_of(width, 768)
    steps = depth // chunk
    slots = 4
    unit = jax.ShapeDtypeStruct((hidden, rows), BF16)
    packed = jax.ShapeDtypeStruct((pieces * SUBS, width // 2 + width // SUBS + LANES), F32)
    return pl.pallas_call(
        functools.partial(experts_body, pieces, chunk),
        out_shape=(
            jax.ShapeDtypeStruct((rows, depth), BF16),
            unit,
            unit,
            packed,
            packed,
        )
        + (jax.ShapeDtypeStruct((hidden, depth), BF16),) * 3,
        in_specs=[SMEM] + [VMEM] * (pieces + 1) + [HBM] * 3,
        out_specs=[VMEM] * 5 + [HBM] * 3,
        scratch_shapes=[
            pltpu.VMEM((hidden, depth), BF16),
            pltpu.VMEM((hidden, depth), BF16),
            pltpu.VMEM((slots, hidden, chunk), BF16),
            pltpu.VMEM((rows, depth), BF16),
            pltpu.VMEM((hidden, rows), BF16),
            pltpu.VMEM((hidden, rows), F32),
            pltpu.VMEM((hidden, rows), F32),
            pltpu.VMEM((hidden, rows), F32),
            pltpu.VMEM((rows, hidden), BF16),
            pltpu.VMEM((rows, hidden), BF16),
            pltpu.VMEM((rows, depth), F32),
            pltpu.VMEM((rows, width), F32),
            pltpu.VMEM((rows, LANES), F32),
            pltpu.SemaphoreType.DMA((steps, 2)),
            pltpu.SemaphoreType.DMA((slots,)),
            pltpu.SemaphoreType.DMA((steps + UP_CHUNKS + GATE_CHUNKS,)),
        ],
        compiler_params=pltpu.CompilerParams(vmem_limit_bytes=50 * MIB),
        cost_estimate=pl.CostEstimate(
            flops=12 * rows * hidden * depth, bytes_accessed=8 * hidden * depth, transcendentals=rows * hidden
        ),
        name="expert_units",
    )(t, *mine, theirs, w_gate, w_up, w_down)


def weights_body(chunk, begun, left_ref, x_ref, _, out_ref, room, sent):
    hidden = left_ref.shape[0]
    tile = tile_of(hidden, 448)
    leaving = []
    for i in range(room.shape[0]):
        cols = pl.ds((begun + i) * chunk, chunk)
        for at in range(0, hidden, tile):
            room[i, at : at + tile, :] = jnp.dot(
                left_ref[at : at + tile, :], x_ref[:, cols], preferred_element_type=F32
            ).astype(BF16)
        leaving.append(pltpu.make_async_copy(room.at[i], out_ref.at[:, cols], sent.at[i]))
        leaving[-1].start()
    for copy in leaving:
        copy.wait()


def weight_grad(left, right, part, begun, name):
    hidden, rows = left.shape
    depth = right.shape[1]
    chunk = chunk_of(depth // 2, 768)
    steps = depth // chunk - begun
    return pl.pallas_call(
        functools.partial(weights_body, chunk, begun),
        out_shape=jax.ShapeDtypeStruct((hidden, depth), BF16),
        in_specs=[VMEM] * 2 + [HBM],
        out_specs=HBM,
        input_output_aliases={2: 0},
        scratch_shapes=[pltpu.VMEM((steps, hidden, chunk), BF16), pltpu.SemaphoreType.DMA((steps,))],
        compiler_params=pltpu.CompilerParams(vmem_limit_bytes=28 * MIB),
        cost_estimate=pl.CostEstimate(
            flops=2 * rows * hidden * steps * chunk, bytes_accessed=2 * hidden * steps * chunk, transcendentals=0
        ),
        name=name,
    )(left, right, part)


def fold_body(copies, keep_ref, got_ref, *outs):
    for d, out in enumerate(outs):
        rows = slice(d * 2 * SUBS, (d + 1) * 2 * SUBS)
        out[...] = keep_ref[rows, :] + got_ref[rows, :]


def fold(copies, keep, got):
    return pl.pallas_call(
        functools.partial(fold_body, copies),
        out_shape=[jax.ShapeDtypeStruct((2 * SUBS, keep.shape[1]), F32)] * copies,
        in_specs=[VMEM] * 2,
        out_specs=[VMEM] * copies,
        compiler_params=pltpu.CompilerParams(vmem_limit_bytes=6 * MIB),
        name="fold_cores",
    )(keep, got)


def merge_body(*refs):
    blocks, (mine_ref, other_ref) = refs[:-2], refs[-2:]
    for at, out in ((0, mine_ref), (SUBS, other_ref)):
        total = blocks[0][at : at + SUBS, :]
        for block in blocks[1:]:
            total += block[at : at + SUBS, :]
        out[...] = total


def merge(blocks):
    part = jax.ShapeDtypeStruct((SUBS, blocks[0].shape[1]), F32)
    return pl.pallas_call(
        merge_body,
        out_shape=(part, part),
        in_specs=[VMEM] * len(blocks),
        out_specs=[VMEM] * 2,
        compiler_params=pltpu.CompilerParams(vmem_limit_bytes=6 * MIB),
        name="merge_chips",
    )(*blocks)


def finish_body(e_ref, ids_ref, mine_ref, got_ref, tok_ref, gate_ref):
    ids = ids_ref[...]
    toks, width = tok_ref.shape
    half, eighth = width // 2, width // SUBS
    both = 2 * SUBS
    row = iota((both, toks), 0)
    sub = sub_row(both, toks)
    expert = jnp.where(row < SUBS, e_ref[0], 1 - e_ref[0])
    main, hits = chosen_rows(ids, expert, sub % WHOLE)
    tail, _ = chosen_rows(ids, expert, jnp.full((both, toks), WHOLE, jnp.int32))
    plain = jnp.where(sub < WHOLE, main, jnp.where(sub == WHOLE, tail, 0.0))
    data = jnp.concatenate([mine_ref[...], got_ref[...]], axis=0)
    tn = (((0,), (0,)), ((), ()))
    exact = dict(precision=lax.Precision.HIGHEST, preferred_element_type=F32)
    halves = [
        lax.dot_general(jnp.where(sub // WHOLE == h, main, 0.0), data[:, :half], tn, **exact) for h in range(2)
    ]
    for s in range(SUBS):
        last = lax.dot_general(jnp.where(sub == s, tail, 0.0), data[:, half : half + eighth], tn, **exact)
        h, at = divmod(s * eighth, half)
        tok_ref[:, s * eighth : (s + 1) * eighth] = (halves[h][:, at : at + eighth] + last).astype(BF16)
    term = plain * data[:, half + eighth : half + eighth + 1]
    for k, hit in enumerate(hits):
        gate_ref[k : k + 1, :] = jnp.sum(jnp.where(hit, term, 0.0), axis=0, keepdims=True)


def finish(e, ids_t, mine, got, width):
    top, toks = ids_t.shape
    return pl.pallas_call(
        finish_body,
        out_shape=(jax.ShapeDtypeStruct((toks, width), BF16), jax.ShapeDtypeStruct((top, toks), F32)),
        in_specs=[SMEM] + [VMEM] * 3,
        out_specs=[VMEM] * 2,
        compiler_params=pltpu.CompilerParams(vmem_limit_bytes=6 * MIB),
        name="finish_tokens",
    )(e, ids_t, mine, got)


def on_device(tokens, grad_out, expert_ids, gate_probs, w_gate, w_up, w_down):
    n_expert = lax.axis_size("expert")
    copies = n_expert // EXPERTS_ON
    place = lax.axis_index("expert")
    e = (place >= copies).astype(jnp.int32).reshape(1)
    t = lax.axis_index("tensor").astype(jnp.int32).reshape(1)
    width = tokens.shape[1]

    def partner(v):
        return lax.ppermute(v, "expert", [(i, (i + copies) % n_expert) for i in range(n_expert)])

    def across(v, d):
        return lax.ppermute(v, "expert", [(i, i ^ d) for i in range(n_expert)])

    def other_core(v):
        return lax.ppermute(v, "tensor", [(0, 1), (1, 0)])

    w_gate, w_up, w_down = (pltpu.with_memory_space_constraint(w, pltpu.HBM) for w in (w_gate, w_up, w_down))
    ids_t = expert_ids.T
    here = (pltpu.with_memory_space_constraint(v, pltpu.HBM) for v in (ids_t, gate_probs.T, tokens, grad_out))
    own, oth = pick(e, *here)
    far_first = sorted(range(1, copies), key=lambda d: (-d.bit_count(), d))
    got = partner(oth)
    first = {0: own} | {d: across(own, d) for d in far_first}
    second = {0: got} | {d: across(got, d) for d in far_first}
    pieces = [piece for d in range(copies) for piece in (first[d], second[d])]
    theirs = other_core(stack(pieces, "stack_pieces"))
    x, dh, du, give, keep, grad_w_down, gate_begun, up_begun = expert_units(
        t, pieces, theirs, w_gate, w_up, w_down, width
    )
    blocks = list(fold(copies, keep, other_core(give)))
    arrived = {d: across(blocks[d], d) for d in far_first}
    dh, local = lax.optimization_barrier((dh, blocks[0]))
    grad_w_gate = weight_grad(dh, x, gate_begun, GATE_CHUNKS, "grad_gate")
    grad_w_gate, arrived = lax.optimization_barrier((grad_w_gate, arrived))
    kept, others = merge([local] + [arrived[d] for d in range(1, copies)])
    back = partner(others)
    du, kept = lax.optimization_barrier((du, kept))
    grad_w_up = weight_grad(du, x, up_begun, UP_CHUNKS, "grad_up")
    grad_w_up, back = lax.optimization_barrier((grad_w_up, back))
    token_grad, gate_t = finish(e, ids_t, kept, back, width)
    return token_grad, gate_t.T, grad_w_gate, grad_w_up, grad_w_down


def solution(mesh):
    return jax.shard_map(
        on_device,
        mesh=mesh,
        in_specs=(
            P(("groups", "expert"), "tensor"),
            P(("groups", "expert"), "tensor"),
            P(("groups", "expert"), None),
            P(("groups", "expert"), None),
            P(("expert", "tensor"), None),
            P(("expert", "tensor"), None),
            P(("expert", "tensor"), None),
        ),
        out_specs=(
            P(("groups", "expert"), "tensor"),
            P(("groups", "expert"), None),
            P(("expert", "tensor"), "groups"),
            P(("expert", "tensor"), "groups"),
            P(("expert", "tensor"), "groups"),
        ),
        check_vma=False,
    )
```

```python
import functools

import jax
import jax.numpy as jnp
from jax import lax
from jax.experimental import pallas as pl
from jax.experimental.pallas import tpu as pltpu
from jax.sharding import PartitionSpec as P

EXPERTS_ON = 2
CAP = 5
LANES = 128
SUBS = 8
WHOLE = 4
F32 = jnp.float32
BF16 = jnp.bfloat16
MIB = 1 << 20
GATE_CHUNKS = 1
UP_CHUNKS = 5
VMEM = pl.BlockSpec(memory_space=pltpu.VMEM)
SMEM = pl.BlockSpec(memory_space=pltpu.SMEM)
HBM = pl.BlockSpec(memory_space=pltpu.HBM)


def iota(shape, dim):
    return lax.broadcasted_iota(jnp.int32, shape, dim)


def chosen_rows(ids, expert, position):
    rows, toks = position.shape
    hits = [ids[k : k + 1, :] == expert for k in range(ids.shape[0])]
    member = functools.reduce(jnp.logical_or, hits).astype(F32)
    before = (iota((toks, toks), 0) < iota((toks, toks), 1)).astype(F32)
    earlier = jnp.dot(member, before, preferred_element_type=F32)
    return jnp.where(earlier == position.astype(F32), member, 0.0), hits


def sub_row(rows, toks):
    return iota((rows, toks), 0) % SUBS


def tile_of(hidden, most):
    sizes = [n for n in range(16, most + 1, 16) if hidden % n == 0]
    return max(sizes) if sizes else hidden


def pick_body(e_ref, ids_any, probs_any, tok_any, grad_any, own_ref, oth_ref, ids_ref, probs_ref, tok_ref, grad_ref, landed):
    copies = [
        pltpu.make_async_copy(src, dst, landed.at[n])
        for n, (src, dst) in enumerate(
            ((ids_any, ids_ref), (probs_any, probs_ref), (tok_any, tok_ref), (grad_any, grad_ref))
        )
    ]
    for copy in copies:
        copy.start()
    for copy in copies[:2]:
        copy.wait()
    ids = ids_ref[...]
    probs = probs_ref[...].astype(F32)
    toks, width = tok_ref.shape
    half, eighth = width // 2, width // SUBS
    size = half + eighth
    both = 2 * SUBS
    row = iota((both, toks), 0)
    sub = sub_row(both, toks)
    expert = jnp.where(row < SUBS, e_ref[0], 1 - e_ref[0])
    main, hits = chosen_rows(ids, expert, sub % WHOLE)
    tail, _ = chosen_rows(ids, expert, jnp.full((both, toks), WHOLE, jnp.int32))
    plain = jnp.where(sub < WHOLE, main, jnp.where(sub == WHOLE, tail, 0.0))
    halves = [jnp.where(sub // WHOLE == h, main, 0.0).astype(BF16) for h in range(2)]
    eighths = [jnp.where(sub == s, tail, 0.0).astype(BF16) for s in range(SUBS)]
    for at, src in enumerate((tok_ref, grad_ref)):
        copies[2 + at].wait()
        packed = sum(
            jnp.dot(one, src[:, h * half : (h + 1) * half], preferred_element_type=F32)
            for h, one in enumerate(halves)
        ).astype(BF16)
        last = sum(
            jnp.dot(one, src[:, s * eighth : (s + 1) * eighth], preferred_element_type=F32)
            for s, one in enumerate(eighths)
        ).astype(BF16)
        for n, dst in enumerate((own_ref, oth_ref)):
            dst[:, at * size : at * size + half] = packed[n * SUBS : (n + 1) * SUBS]
            dst[:, at * size + half : (at + 1) * size] = last[n * SUBS : (n + 1) * SUBS]
    weight = sum(jnp.where(hit, probs[k : k + 1, :], 0.0) for k, hit in enumerate(hits))
    gate = jnp.broadcast_to(jnp.sum(plain * weight, axis=1, keepdims=True), (both, LANES)).astype(BF16)
    for n, dst in enumerate((own_ref, oth_ref)):
        dst[:, 2 * size :] = gate[n * SUBS : (n + 1) * SUBS]


def pick(e, ids_t, probs_t, tokens, grad_out):
    width = tokens.shape[1]
    size = width // 2 + width // SUBS
    piece = jax.ShapeDtypeStruct((SUBS, 2 * size + LANES), BF16)
    return pl.pallas_call(
        pick_body,
        out_shape=(piece, piece),
        in_specs=[SMEM] + [HBM] * 4,
        out_specs=[VMEM] * 2,
        scratch_shapes=[pltpu.VMEM(v.shape, v.dtype) for v in (ids_t, probs_t, tokens, grad_out)]
        + [pltpu.SemaphoreType.DMA((4,))],
        compiler_params=pltpu.CompilerParams(vmem_limit_bytes=6 * MIB),
        name="pick_rows",
    )(e, ids_t, probs_t, tokens, grad_out)


NT = (((1,), (1,)), ((), ()))


def chunk_of(width, most):
    return max(n for n in range(LANES, most + 1, LANES) if width % n == 0)


def assemble(pieces, held, out, base, side):
    width = held.shape[1]
    half, eighth = width // 2, width // SUBS
    size = half + eighth
    for n, ref in enumerate(pieces):
        at = n * CAP
        piece = ref[:, side * size : (side + 1) * size].astype(F32)
        for h in range(2):
            held[at : at + WHOLE, h * half : (h + 1) * half] = piece[h * WHOLE : (h + 1) * WHOLE, :half]
        for s in range(SUBS):
            held[at + WHOLE : at + CAP, s * eighth : (s + 1) * eighth] = piece[s : s + 1, half:]
    out[:, pl.ds(base, width)] = held[...].astype(BF16)


def pack(part, gates, out, pieces):
    width = part.shape[1]
    half, eighth = width // 2, width // SUBS
    size = half + eighth
    for n in range(pieces):
        at, to = n * CAP, n * SUBS
        for h in range(2):
            out[to + h * WHOLE : to + (h + 1) * WHOLE, :half] = part[at : at + WHOLE, h * half : (h + 1) * half]
        for s in range(SUBS):
            out[to + s : to + s + 1, half:size] = part[at + WHOLE : at + CAP, s * eighth : (s + 1) * eighth]
        out[to : to + CAP, size:] = gates[at : at + CAP, :]
        out[to + CAP : to + SUBS, size:] = jnp.zeros((SUBS - CAP, LANES), F32)


def stack_body(*refs):
    for n, ref in enumerate(refs[:-1]):
        refs[-1][n] = ref[...]


def stack(pieces, name):
    return pl.pallas_call(
        stack_body,
        out_shape=jax.ShapeDtypeStruct((len(pieces),) + pieces[0].shape, BF16),
        in_specs=[VMEM] * len(pieces),
        out_specs=VMEM,
        compiler_params=pltpu.CompilerParams(vmem_limit_bytes=6 * MIB),
        name=name,
    )(*pieces)


def experts_body(pieces, chunk, ahead, t_ref, *refs):
    mine = refs[:pieces]
    theirs = [refs[pieces].at[n] for n in range(pieces)]
    (wg_hbm, wu_hbm, wd_hbm, x_ref, dh_ref, du_ref, give_ref, keep_ref, down_ref, gate_ref, up_ref,
     wg_ref, wu_ref, ring, g_ref, wt_ref, h_ref, u_ref, da_ref, dhr_ref, dur_ref, acc,
     held, factor, landed, ring_landed, sent) = refs[pieces + 1 :]
    rows, depth = x_ref.shape
    hidden = wg_ref.shape[0]
    width = depth // 2
    slots = ring.shape[0]
    steps = depth // chunk
    t = t_ref[0]

    def columns(i):
        return pl.ds(pl.multiple_of(i * chunk, chunk), chunk)

    def load(i, n):
        src, dst = ((wg_hbm, wg_ref), (wu_hbm, wu_ref))[n]
        return pltpu.make_async_copy(src.at[:, columns(i)], dst.at[:, columns(i)], landed.at[i, n])

    def load_down(i):
        slot = lax.rem(i, slots)
        return pltpu.make_async_copy(wd_hbm.at[:, columns(i)], ring.at[slot], ring_landed.at[slot])

    def start(i):
        load(i, 0).start()
        load(i, 1).start()
        load_down(i).start()

    start(0)
    held[...] = jnp.zeros_like(held)
    factor[...] = jnp.zeros_like(factor)
    for n, ref in enumerate(mine):
        factor[n * CAP : (n + 1) * CAP, :] = ref[:CAP, ref.shape[1] - LANES :].astype(F32)
    for side, out in enumerate((x_ref, g_ref)):
        for group, at in ((mine, t), (theirs, 1 - t)):
            assemble(group, held, out, pl.multiple_of(at * width, width), side)
    for i in range(1, min(ahead, steps)):
        start(i)

    def three(i):
        cols = columns(i)
        x = x_ref[:, cols]
        return (
            lambda: lax.dot_general(wg_ref[:, cols], x, NT, preferred_element_type=F32),
            lambda: lax.dot_general(wu_ref[:, cols], x, NT, preferred_element_type=F32),
            lambda: lax.dot_general(ring[lax.rem(i, slots)], g_ref[:, cols], NT, preferred_element_type=F32),
        )

    sums = (h_ref, u_ref, da_ref)
    waits = lambda i: (load(i, 0), load(i, 1), load_down(i))
    for wait, dot, out in zip(waits(0), three(0), sums):
        wait.wait()
        out[...] = dot()

    def up_step(i, carry):
        @pl.when(i + ahead - 1 < steps)
        def _():
            start(i + ahead - 1)

        for wait in waits(i):
            wait.wait()
        for dot, out in zip(three(i), sums):
            out[...] += dot()
        return carry

    lax.fori_loop(1, steps, up_step, 0)

    weight = factor[...].T[:1, :]

    def units(start, size, total):
        at = pl.ds(start, size)
        h = h_ref[at, :]
        u = u_ref[at, :]
        da = da_ref[at, :]
        sigma = 1.0 / (1.0 + jnp.exp(-h))
        silu = h * sigma
        act = silu * u
        scaled = weight * da
        wt_ref[at, :] = (weight * act).astype(BF16)
        dh = scaled * u * sigma * (1.0 + h * (1.0 - sigma))
        du = scaled * silu
        dh_ref[at, :] = dh.astype(BF16)
        du_ref[at, :] = du.astype(BF16)
        dhr_ref[:, at] = dh.T.astype(BF16)
        dur_ref[:, at] = du.T.astype(BF16)
        return total + jnp.sum(act * da, axis=0, keepdims=True)

    total = jnp.zeros((1, rows), F32)
    for begin in range(0, hidden, LANES):
        total = units(begin, min(LANES, hidden - begin), total)
    gates = jnp.broadcast_to(total, (LANES, rows)).T
    tile = tile_of(hidden, 448)
    leaving = []
    for i in range(steps):
        cols = pl.ds(i * chunk, chunk)
        acc[:, cols] = jnp.dot(dhr_ref[...], wg_ref[:, cols], preferred_element_type=F32) + jnp.dot(
            dur_ref[...], wu_ref[:, cols], preferred_element_type=F32
        )
        before = pl.ds((i - 1) * chunk, chunk)
        jobs = [(wt_ref, g_ref, wg_ref.at[:, before] if i else ring.at[0], down_ref)]
        if i < UP_CHUNKS:
            jobs.append((du_ref, x_ref, wu_ref.at[:, before] if i else ring.at[1], up_ref))
        if i < GATE_CHUNKS:
            jobs.append((dh_ref, x_ref, ring.at[2 + i], gate_ref))
        for left, right, room, out in jobs:
            for at in range(0, hidden, tile):
                room[at : at + tile, :] = jnp.dot(
                    left[at : at + tile, :], right[:, cols], preferred_element_type=F32
                ).astype(BF16)
            leaving.append(pltpu.make_async_copy(room, out.at[:, cols], sent.at[len(leaving)]))
            leaving[-1].start()
    for at, out in ((1 - t, give_ref), (t, keep_ref)):
        held[...] = acc[:, pl.ds(pl.multiple_of(at * width, width), width)]
        pack(held, gates, out, pieces)
    for copy in leaving:
        copy.wait()


def expert_units(t, mine, theirs, w_gate, w_up, w_down, width):
    hidden, depth = w_gate.shape
    pieces = len(mine)
    rows = -(-pieces * CAP // 16) * 16
    chunk = chunk_of(width, 768)
    steps = depth // chunk
    ahead = 3
    slots = 4
    unit = jax.ShapeDtypeStruct((hidden, rows), BF16)
    packed = jax.ShapeDtypeStruct((pieces * SUBS, width // 2 + width // SUBS + LANES), F32)
    return pl.pallas_call(
        functools.partial(experts_body, pieces, chunk, ahead),
        out_shape=(
            jax.ShapeDtypeStruct((rows, depth), BF16),
            unit,
            unit,
            packed,
            packed,
        )
        + (jax.ShapeDtypeStruct((hidden, depth), BF16),) * 3,
        in_specs=[SMEM] + [VMEM] * (pieces + 1) + [HBM] * 3,
        out_specs=[VMEM] * 5 + [HBM] * 3,
        scratch_shapes=[
            pltpu.VMEM((hidden, depth), BF16),
            pltpu.VMEM((hidden, depth), BF16),
            pltpu.VMEM((slots, hidden, chunk), BF16),
            pltpu.VMEM((rows, depth), BF16),
            pltpu.VMEM((hidden, rows), BF16),
            pltpu.VMEM((hidden, rows), F32),
            pltpu.VMEM((hidden, rows), F32),
            pltpu.VMEM((hidden, rows), F32),
            pltpu.VMEM((rows, hidden), BF16),
            pltpu.VMEM((rows, hidden), BF16),
            pltpu.VMEM((rows, depth), F32),
            pltpu.VMEM((rows, width), F32),
            pltpu.VMEM((rows, LANES), F32),
            pltpu.SemaphoreType.DMA((steps, 2)),
            pltpu.SemaphoreType.DMA((slots,)),
            pltpu.SemaphoreType.DMA((steps + UP_CHUNKS + GATE_CHUNKS,)),
        ],
        compiler_params=pltpu.CompilerParams(vmem_limit_bytes=50 * MIB),
        cost_estimate=pl.CostEstimate(
            flops=12 * rows * hidden * depth, bytes_accessed=8 * hidden * depth, transcendentals=rows * hidden
        ),
        name="expert_units",
    )(t, *mine, theirs, w_gate, w_up, w_down)


def weights_body(chunk, begun, left_ref, x_ref, _, out_ref, room, sent):
    hidden = left_ref.shape[0]
    tile = tile_of(hidden, 448)
    leaving = []
    for i in range(room.shape[0]):
        cols = pl.ds((begun + i) * chunk, chunk)
        for at in range(0, hidden, tile):
            room[i, at : at + tile, :] = jnp.dot(
                left_ref[at : at + tile, :], x_ref[:, cols], preferred_element_type=F32
            ).astype(BF16)
        leaving.append(pltpu.make_async_copy(room.at[i], out_ref.at[:, cols], sent.at[i]))
        leaving[-1].start()
    for copy in leaving:
        copy.wait()


def weight_grad(left, right, part, begun, name):
    hidden, rows = left.shape
    depth = right.shape[1]
    chunk = chunk_of(depth // 2, 768)
    steps = depth // chunk - begun
    return pl.pallas_call(
        functools.partial(weights_body, chunk, begun),
        out_shape=jax.ShapeDtypeStruct((hidden, depth), BF16),
        in_specs=[VMEM] * 2 + [HBM],
        out_specs=HBM,
        input_output_aliases={2: 0},
        scratch_shapes=[pltpu.VMEM((steps, hidden, chunk), BF16), pltpu.SemaphoreType.DMA((steps,))],
        compiler_params=pltpu.CompilerParams(vmem_limit_bytes=28 * MIB),
        cost_estimate=pl.CostEstimate(
            flops=2 * rows * hidden * steps * chunk, bytes_accessed=2 * hidden * steps * chunk, transcendentals=0
        ),
        name=name,
    )(left, right, part)


def fold_body(copies, keep_ref, got_ref, *outs):
    for d, out in enumerate(outs):
        rows = slice(d * 2 * SUBS, (d + 1) * 2 * SUBS)
        out[...] = keep_ref[rows, :] + got_ref[rows, :]


def fold(copies, keep, got):
    return pl.pallas_call(
        functools.partial(fold_body, copies),
        out_shape=[jax.ShapeDtypeStruct((2 * SUBS, keep.shape[1]), F32)] * copies,
        in_specs=[VMEM] * 2,
        out_specs=[VMEM] * copies,
        compiler_params=pltpu.CompilerParams(vmem_limit_bytes=6 * MIB),
        name="fold_cores",
    )(keep, got)


def merge_body(*refs):
    blocks, (mine_ref, other_ref) = refs[:-2], refs[-2:]
    for at, out in ((0, mine_ref), (SUBS, other_ref)):
        total = blocks[0][at : at + SUBS, :]
        for block in blocks[1:]:
            total += block[at : at + SUBS, :]
        out[...] = total


def merge(blocks):
    part = jax.ShapeDtypeStruct((SUBS, blocks[0].shape[1]), F32)
    return pl.pallas_call(
        merge_body,
        out_shape=(part, part),
        in_specs=[VMEM] * len(blocks),
        out_specs=[VMEM] * 2,
        compiler_params=pltpu.CompilerParams(vmem_limit_bytes=6 * MIB),
        name="merge_chips",
    )(*blocks)


def finish_body(e_ref, ids_ref, mine_ref, got_ref, tok_ref, gate_ref):
    ids = ids_ref[...]
    toks, width = tok_ref.shape
    half, eighth = width // 2, width // SUBS
    both = 2 * SUBS
    row = iota((both, toks), 0)
    sub = sub_row(both, toks)
    expert = jnp.where(row < SUBS, e_ref[0], 1 - e_ref[0])
    main, hits = chosen_rows(ids, expert, sub % WHOLE)
    tail, _ = chosen_rows(ids, expert, jnp.full((both, toks), WHOLE, jnp.int32))
    plain = jnp.where(sub < WHOLE, main, jnp.where(sub == WHOLE, tail, 0.0))
    data = jnp.concatenate([mine_ref[...], got_ref[...]], axis=0)
    tn = (((0,), (0,)), ((), ()))
    exact = dict(precision=lax.Precision.HIGHEST, preferred_element_type=F32)
    for s in range(SUBS):
        h, at = divmod(s * eighth, half)
        left = jnp.concatenate([jnp.where(sub // WHOLE == h, main, 0.0), jnp.where(sub == s, tail, 0.0)], axis=0)
        right = jnp.concatenate([data[:, at : at + eighth], data[:, half : half + eighth]], axis=0)
        tok_ref[:, s * eighth : (s + 1) * eighth] = lax.dot_general(left, right, tn, **exact).astype(BF16)
    term = plain * data[:, half + eighth : half + eighth + 1]
    for k, hit in enumerate(hits):
        gate_ref[k : k + 1, :] = jnp.sum(jnp.where(hit, term, 0.0), axis=0, keepdims=True)


def finish(e, ids_t, mine, got, width):
    top, toks = ids_t.shape
    return pl.pallas_call(
        finish_body,
        out_shape=(jax.ShapeDtypeStruct((toks, width), BF16), jax.ShapeDtypeStruct((top, toks), F32)),
        in_specs=[SMEM] + [VMEM] * 3,
        out_specs=[VMEM] * 2,
        compiler_params=pltpu.CompilerParams(vmem_limit_bytes=6 * MIB),
        name="finish_tokens",
    )(e, ids_t, mine, got)


def on_device(tokens, grad_out, expert_ids, gate_probs, w_gate, w_up, w_down):
    n_expert = lax.axis_size("expert")
    copies = n_expert // EXPERTS_ON
    place = lax.axis_index("expert")
    e = (place >= copies).astype(jnp.int32).reshape(1)
    t = lax.axis_index("tensor").astype(jnp.int32).reshape(1)
    width = tokens.shape[1]

    def partner(v):
        return lax.ppermute(v, "expert", [(i, (i + copies) % n_expert) for i in range(n_expert)])

    def across(v, d):
        return lax.ppermute(v, "expert", [(i, i ^ d) for i in range(n_expert)])

    def other_core(v):
        return lax.ppermute(v, "tensor", [(0, 1), (1, 0)])

    w_gate, w_up, w_down = (pltpu.with_memory_space_constraint(w, pltpu.HBM) for w in (w_gate, w_up, w_down))
    ids_t = expert_ids.T
    here = (pltpu.with_memory_space_constraint(v, pltpu.HBM) for v in (ids_t, gate_probs.T, tokens, grad_out))
    own, oth = pick(e, *here)
    far_first = sorted(range(1, copies), key=lambda d: (-d.bit_count(), d))
    got = partner(oth)
    first = {0: own} | {d: across(own, d) for d in far_first}
    second = {0: got} | {d: across(got, d) for d in far_first}
    pieces = [piece for d in range(copies) for piece in (first[d], second[d])]
    theirs = other_core(stack(pieces, "stack_pieces"))
    x, dh, du, give, keep, grad_w_down, gate_begun, up_begun = expert_units(
        t, pieces, theirs, w_gate, w_up, w_down, width
    )
    blocks = list(fold(copies, keep, other_core(give)))
    arrived = {d: across(blocks[d], d) for d in far_first}
    dh, local = lax.optimization_barrier((dh, blocks[0]))
    grad_w_gate = weight_grad(dh, x, gate_begun, GATE_CHUNKS, "grad_gate")
    grad_w_gate, arrived = lax.optimization_barrier((grad_w_gate, arrived))
    kept, others = merge([local] + [arrived[d] for d in range(1, copies)])
    back = partner(others)
    du, kept = lax.optimization_barrier((du, kept))
    grad_w_up = weight_grad(du, x, up_begun, UP_CHUNKS, "grad_up")
    grad_w_up, back = lax.optimization_barrier((grad_w_up, back))
    token_grad, gate_t = finish(e, ids_t, kept, back, width)
    return token_grad, gate_t.T, grad_w_gate, grad_w_up, grad_w_down


def solution(mesh):
    return jax.shard_map(
        on_device,
        mesh=mesh,
        in_specs=(
            P(("groups", "expert"), "tensor"),
            P(("groups", "expert"), "tensor"),
            P(("groups", "expert"), None),
            P(("groups", "expert"), None),
            P(("expert", "tensor"), None),
            P(("expert", "tensor"), None),
            P(("expert", "tensor"), None),
        ),
        out_specs=(
            P(("groups", "expert"), "tensor"),
            P(("groups", "expert"), None),
            P(("expert", "tensor"), "groups"),
            P(("expert", "tensor"), "groups"),
            P(("expert", "tensor"), "groups"),
        ),
        check_vma=False,
    )
```
